128 devices in a mesh: frame: 128 (over x, z, y, core).
Axes of the slice: x: 4, y: 4, z: 4, core: 2. Of those that a mesh axis runs over, the one named last changes fastest.
Arguments:
- video: bfloat16 [49152, 1280], P('frame'), may hold values from -6 to 6
- key_list: int32 [8], replicated, may hold values from 0 to 127, as said below
- pairs: int32 [128, 2], P('frame'), may hold values from 0 to 7, all different within a row
- norm_gain: float32 [1280], replicated, as said below
- qkv_weight: bfloat16 [1280, 3840], replicated, may hold values from -0.15625 to 0.15625
- out_weight: bfloat16 [1280, 1280], replicated, may hold values from -0.15625 to 0.15625
- time_gain: float32 [1280], replicated, as said below
- time_weight: bfloat16 [1280, 3840], replicated, may hold values from -0.15625 to 0.15625
Outputs:
- spatial: bfloat16 [49152, 1280], P('frame')
- temporal: bfloat16 [49152, 1280], P('frame')
The draws below stay inside these ranges and needn't reach their ends.
Inputs may be any that keep to these rules, and one draw needn't show every extreme that they name: `key_list`: distinct frame numbers in rising order, the first 0 and the last 127. `pairs`: each frame names two different keyframes; every keyframe is named by some frame. `norm_gain`: positive. `time_gain`: positive.
All inputs are finite; a program needn't handle non-finite values.
Results may differ from the reference program's by a relative error of at most 0.029.
Values may be sent and summed in bfloat16 or wider, within the bound.
No kernel may reach another device: no remote copies, remote signals or barrier semaphores. Data moves between devices by JAX's collectives and lax.ppermute only.
A program may use at most 192 MiB of HBM per device.

```python
import jax
import jax.numpy as jnp
from jax import lax

WIDTH = 1280
HEADS = 20
HEAD = 64
TOK = 384
KEYS = 8
FRAMES = 128


def draw_key_list(key, part):
    key = jax.random.fold_in(key, 3)
    stride = FRAMES // KEYS
    offsets = jax.random.randint(key, (KEYS,), 0, stride, dtype=jnp.int32)
    places = jnp.arange(KEYS, dtype=jnp.int32)
    frames_at = places * stride + offsets
    frames_at = jnp.where(places == 0, 0, frames_at)
    frames_at = jnp.where(places == KEYS - 1, FRAMES - 1, frames_at)
    return frames_at.astype(jnp.int32)


def spread_gain(key, lowest, highest):
    unit = jax.random.uniform(key, (WIDTH,), jnp.float32)
    return jnp.exp(jnp.log(lowest) + unit * (jnp.log(highest) - jnp.log(lowest)))


def draw_norm_gain(key, part):
    key = jax.random.fold_in(key, 11)
    return spread_gain(key, 0.8, 2.5)


def draw_time_gain(key, part):
    key = jax.random.fold_in(key, 17)
    return spread_gain(key, 0.8, 2.5)


def block_scale(key, dims, cuts, low, high):
    def one(position, blocks):
        steps = jax.random.uniform(jax.random.fold_in(jax.random.fold_in(key, 6), position), (blocks,), jnp.float32, low / len(cuts), high / len(cuts))
        return jnp.repeat(jnp.exp(steps), dims[position] // blocks).reshape((-1,) + (1,) * (len(dims) - position - 1))

    factor_of = one(*cuts[0])
    for cut in cuts[1:]:
        factor_of = factor_of * one(*cut)
    return factor_of


def different_ones(key, rows, count, top, lift):
    order = jax.random.permutation(jax.random.fold_in(key, 1), count)
    pull = order
    for power in range(3):
        pull = pull * pull // count
    pull = pull * lift // count
    tickets = jax.random.randint(jax.random.fold_in(key, 2), (rows, count), 0, 4096) + pull
    fixed_rows = jax.random.permutation(jax.random.fold_in(key, 3), rows)[jnp.arange(count) % rows]
    tickets = jnp.where(jnp.arange(rows)[:, None] == fixed_rows[None, :], 1 << 14, tickets)
    merit = tickets * count + jnp.arange(count)
    return lax.top_k(merit.astype(jnp.int32), top)[1].astype(jnp.int32)


def scatter_about(key, dims, scale, reach, split=(), kind=jnp.bfloat16):
    entries = jax.random.normal(key, dims, jnp.float32) * scale
    if len(split) > 0:
        entries = block_scale(key, dims, split, -0.22, 0.18) * entries
    return jnp.clip(entries, min=-reach, max=reach).astype(kind)


def setup_inputs(seed: int = 0) -> dict:
    key_of = jax.random.split(jax.random.key(seed), 9)
    video = scatter_about(key_of[0], (FRAMES * TOK, WIDTH), 1.0, 6.0, ((0, 128),))
    key_list = draw_key_list(jax.random.fold_in(key_of[8], 71), 0)
    pairs = different_ones(key_of[2], FRAMES, KEYS, 2, 4096)
    norm_gain = draw_norm_gain(jax.random.fold_in(key_of[8], 71), 0)
    qkv_weight = scatter_about(key_of[4], (WIDTH, 3 * WIDTH), WIDTH ** -0.5, 0.15625)
    out_weight = scatter_about(key_of[5], (WIDTH, WIDTH), WIDTH ** -0.5, 0.15625)
    time_gain = draw_time_gain(jax.random.fold_in(key_of[8], 71), 0)
    time_weight = scatter_about(key_of[7], (WIDTH, 3 * WIDTH), WIDTH ** -0.5, 0.15625)
    return dict(video=video, key_list=key_list, pairs=pairs, norm_gain=norm_gain, qkv_weight=qkv_weight, out_weight=out_weight, time_gain=time_gain, time_weight=time_weight)


def layer_norm(rows, gain):
    values = rows.astype(jnp.float32)
    centred = values - lax.optimization_barrier(jnp.mean(values, axis=-1, keepdims=True))
    spread = lax.optimization_barrier(jnp.mean(centred * centred, axis=-1, keepdims=True))
    return (centred * lax.rsqrt(spread + 1e-05) * gain).astype(jnp.bfloat16)

def attend_heads(queries, keys_all, values_all):
    count = queries.shape[0]
    span = keys_all.shape[0]
    query_f = queries.reshape(count, HEADS, HEAD).astype(jnp.float32)
    key_f = keys_all.reshape(span, HEADS, HEAD).astype(jnp.float32)
    value_f = values_all.reshape(span, HEADS, HEAD).astype(jnp.float32)
    scores = jnp.einsum('rhd,shd->hrs', query_f, key_f) * 0.125
    weights = jax.nn.softmax(scores, axis=-1).astype(jnp.bfloat16)
    weights = lax.optimization_barrier(weights).astype(jnp.float32)
    mixed = jnp.einsum('hrs,shd->rhd', weights, value_f)
    return mixed.astype(jnp.bfloat16).reshape(count, HEADS * HEAD)

def reference(video, key_list, pairs, norm_gain, qkv_weight, out_weight, time_gain, time_weight):
    normed = layer_norm(video, norm_gain)
    qkv = jnp.dot(normed, qkv_weight, preferred_element_type=jnp.float32).astype(jnp.bfloat16)
    qkv = qkv.reshape(FRAMES, TOK, 3 * WIDTH)
    owners = key_list[pairs].astype(jnp.int32)

    def one_frame(frame):
        mine = qkv[frame]
        first_rows = qkv[owners[frame, 0]]
        second_rows = qkv[owners[frame, 1]]
        keys_all = jnp.concatenate([mine[:, WIDTH:2 * WIDTH], first_rows[:, WIDTH:2 * WIDTH], second_rows[:, WIDTH:2 * WIDTH]], axis=0)
        values_all = jnp.concatenate([mine[:, 2 * WIDTH:], first_rows[:, 2 * WIDTH:], second_rows[:, 2 * WIDTH:]], axis=0)
        return attend_heads(mine[:, :WIDTH], keys_all, values_all)
    heads_out = lax.map(one_frame, jnp.arange(FRAMES, dtype=jnp.int32)).reshape(FRAMES * TOK, WIDTH)
    spatial = (video.astype(jnp.float32) + jnp.dot(heads_out, out_weight, preferred_element_type=jnp.float32)).astype(jnp.bfloat16)
    time_normed = layer_norm(spatial, time_gain)
    time_qkv = jnp.dot(time_normed, time_weight, preferred_element_type=jnp.float32).astype(jnp.bfloat16)
    pixel_block = 32
    time_qkv = time_qkv.reshape(FRAMES, TOK // pixel_block, pixel_block, 3 * WIDTH)
    blocks = jnp.moveaxis(time_qkv, 1, 0)

    def one_block(block):
        query_f = block[..., :WIDTH].reshape(FRAMES, pixel_block, HEADS, HEAD).astype(jnp.float32)
        key_f = block[..., WIDTH:2 * WIDTH].reshape(FRAMES, pixel_block, HEADS, HEAD).astype(jnp.float32)
        value_f = block[..., 2 * WIDTH:].reshape(FRAMES, pixel_block, HEADS, HEAD).astype(jnp.float32)
        scores = jnp.einsum('fphd,gphd->phfg', query_f, key_f) * 0.125
        weights = jax.nn.softmax(scores, axis=-1).astype(jnp.bfloat16)
        weights = lax.optimization_barrier(weights).astype(jnp.float32)
        mixed = jnp.einsum('phfg,gphd->fphd', weights, value_f)
        return mixed.astype(jnp.bfloat16).reshape(FRAMES, pixel_block, WIDTH)
    mixed_blocks = lax.map(one_block, blocks)
    temporal = jnp.moveaxis(mixed_blocks, 0, 1).reshape(FRAMES * TOK, WIDTH)
    return (spatial, temporal)
```

```python
import jax
import jax.numpy as jnp
from jax import lax
from jax.experimental import pallas as pl
from jax.experimental.pallas import tpu as pltpu
from jax.sharding import PartitionSpec as P

WIDTH = 1280
HEADS = 20
HEAD = 64
TOK = 384
FRAMES = 128
KEYS = 8
PARTS = TOK // FRAMES
LANES = 128
COLS = WIDTH // LANES
SLAB = 32
GROUP = 256
GROUPS = WIDTH // GROUP
SCALE = 0.125 * 1.4426950408889634

bf16 = jnp.bfloat16
f32 = jnp.float32


def params(mib, **more):
    return pltpu.CompilerParams(vmem_limit_bytes=mib << 20, **more)


def cost(flops, moved, exps=0):
    return pl.CostEstimate(flops=int(flops), bytes_accessed=int(moved), transcendentals=int(exps))


def norm_rows(values, gain):
    centred = values - jnp.mean(values, axis=-1, keepdims=True)
    spread = jnp.mean(centred * centred, axis=-1, keepdims=True)
    return (centred * lax.rsqrt(spread + 1e-05) * gain).astype(bf16)


def swap_matrix():
    row = lax.broadcasted_iota(jnp.int32, (256, 256), 0)
    col = lax.broadcasted_iota(jnp.int32, (256, 256), 1)
    return jnp.where(col == (row % 16) * 16 + row // 16, 1.0, 0.0).astype(bf16)


def rows_to_slab(rows_ref, slab_ref, swap, spare=None):
    for half in range(2):
        for pair in range(4):
            sides = []
            for block in (2 * pair, 2 * pair + 1):
                tiles = []
                for unit in range(16 * half, 16 * half + 16):
                    k, g = divmod(unit, COLS)
                    if k < PARTS:
                        at = k * FRAMES + 16 * block
                        tiles.append(rows_ref[at : at + 16, g * LANES : (g + 1) * LANES])
                    elif spare is None:
                        tiles.append(jnp.zeros((16, LANES), bf16))
                    else:
                        tiles.append(spare[unit - PARTS * COLS])
                sides.append(jnp.concatenate(tiles, axis=0))
            both = jnp.concatenate(sides, axis=1)
            moved = jnp.dot(swap, both, preferred_element_type=f32).astype(bf16)
            for side in range(2):
                block = 2 * pair + side
                slab_ref[16 * block : 16 * block + 16, 16 * half : 16 * half + 16, :] = moved[
                    :, side * LANES : (side + 1) * LANES
                ].reshape(16, 16, LANES)


def slab_to_rows(load, rows_ref, swap, first=0):
    for block in range(8):
        both = jnp.concatenate(
            [load(block, half).reshape(256, LANES) for half in range(2)], axis=1
        )
        moved = jnp.dot(swap, both, preferred_element_type=f32).astype(bf16)
        for unit in range(PARTS * COLS):
            half, row = divmod(unit, 16)
            k, g = divmod(unit, COLS)
            at = first + k * FRAMES + 16 * block
            rows_ref[at : at + 16, g * LANES : (g + 1) * LANES] = moved[
                16 * row : 16 * row + 16, half * LANES : (half + 1) * LANES
            ]


def prep_kernel(pairs_ref, video_ref, gain_ref, normed_ref, slab_ref):
    for k in range(PARTS):
        rows = pl.ds(k * FRAMES, FRAMES)
        normed_ref[rows, :] = norm_rows(video_ref[rows, :].astype(f32), gain_ref[...])
    spare = [
        jnp.full((16, LANES), pairs_ref[0, which], jnp.int32).astype(f32).astype(bf16)
        for which in range(2)
    ]
    rows_to_slab(normed_ref, slab_ref, swap_matrix(), spare)


def prep(pairs, video, gain):
    whole = pl.BlockSpec(memory_space=pltpu.VMEM)
    return pl.pallas_call(
        prep_kernel,
        out_shape=(
            jax.ShapeDtypeStruct((TOK, WIDTH), bf16),
            jax.ShapeDtypeStruct((FRAMES, SLAB, LANES), bf16),
        ),
        in_specs=[pl.BlockSpec(memory_space=pltpu.SMEM), whole, whole],
        out_specs=(whole, whole),
        compiler_params=params(16),
        cost_estimate=cost(6 * TOK * WIDTH, 6 * TOK * WIDTH),
        name="prep",
    )(pairs, video, gain)


def project_kernel(rows_ref, weight_ref, out_ref):
    product = jnp.dot(rows_ref[...], weight_ref[...], preferred_element_type=f32)
    product = product * jnp.where(pl.program_id(0) < GROUPS, SCALE, 1.0)
    out_ref[...] = product.astype(bf16)


def project(rows, weight):
    return pl.pallas_call(
        project_kernel,
        grid=(3 * GROUPS,),
        out_shape=jax.ShapeDtypeStruct((TOK, 3 * WIDTH), bf16),
        in_specs=[
            pl.BlockSpec((TOK, WIDTH), lambda i: (0, 0)),
            pl.BlockSpec((WIDTH, GROUP), lambda i: (0, i)),
        ],
        out_specs=pl.BlockSpec((TOK, GROUP), lambda i: (0, i)),
        compiler_params=params(16),
        cost_estimate=cost(6 * TOK * WIDTH * WIDTH, 6 * WIDTH * WIDTH + 8 * TOK * WIDTH),
        name="project",
    )(rows, weight)


def low_lanes(rows):
    return lax.broadcasted_iota(jnp.int32, (rows, LANES), 1) < HEAD


def attend_pair(queries, keys, values, top=None):
    count = queries.shape[0]
    low_q = low_lanes(count)
    low_v = low_lanes(values.shape[0])
    outs, tops = [], []
    for head in range(2):
        keep = low_q if head == 0 else ~low_q
        mine = jnp.where(keep, queries.astype(f32), 0.0).astype(bf16)
        keep_v = low_v if head == 0 else ~low_v
        padded = jnp.where(keep_v, values, 1.0).astype(bf16)
        scores = lax.dot_general(
            mine, keys, (((1,), (1,)), ((), ())), preferred_element_type=f32
        )
        most = jnp.max(scores, axis=-1, keepdims=True)
        if top is not None:
            most = jnp.maximum(most, top[:, head * HEAD : head * HEAD + 1])
        weights = jnp.exp2(scores - most).astype(bf16)
        outs.append(jnp.dot(weights, padded, preferred_element_type=f32))
        tops.append(most)
    mixed = jnp.where(low_q, outs[0], outs[1])
    total = pltpu.roll(jnp.where(low_q, outs[1], outs[0]), HEAD, 1)
    return mixed, total, jnp.where(low_q, tops[0], tops[1])


def own_kernel(q_ref, k_ref, v_ref, mixed_ref, total_ref, top_ref):
    values = v_ref[...].astype(f32)
    for k in range(PARTS):
        rows = pl.ds(k * FRAMES, FRAMES)
        mixed, total, top = attend_pair(q_ref[rows, :], k_ref[...], values)
        mixed_ref[rows, :] = mixed
        total_ref[rows, :] = total
        top_ref[rows, :] = top


def own_attend(qkv):
    out = jax.ShapeDtypeStruct((TOK, WIDTH), f32)
    out_spec = pl.BlockSpec((TOK, LANES), lambda i: (0, i))
    return pl.pallas_call(
        own_kernel,
        grid=(COLS,),
        out_shape=(out, out, out),
        in_specs=[
            pl.BlockSpec((TOK, LANES), lambda i: (0, i)),
            pl.BlockSpec((TOK, LANES), lambda i: (0, COLS + i)),
            pl.BlockSpec((TOK, LANES), lambda i: (0, 2 * COLS + i)),
        ],
        out_specs=(out_spec, out_spec, out_spec),
        compiler_params=params(16),
        cost_estimate=cost(8 * TOK * TOK * WIDTH, 18 * TOK * WIDTH, HEADS * TOK * TOK),
        name="own_attend",
    )(qkv, qkv, qkv)


def choose_kernel(key_list_ref, slab_ref, out_ref):
    keys = jnp.concatenate([slab_ref[key_list_ref[s]] for s in range(KEYS)], axis=0)
    row = lax.broadcasted_iota(jnp.int32, (SLAB, KEYS * SLAB), 0)
    col = lax.broadcasted_iota(jnp.int32, (SLAB, KEYS * SLAB), 1)
    same = (col % SLAB) == row
    slot = (lax.broadcasted_iota(jnp.int32, (1, KEYS * SLAB), 1) // SLAB).astype(f32)

    def some(step, carry):
        first = pl.multiple_of(step * 8, 8)
        picks = []
        for f in range(8):
            spare = slab_ref[first + f, 16:32, :].astype(f32)
            for which in range(2):
                wanted = spare[14 + which : 15 + which, :]
                wanted = jnp.concatenate([wanted, wanted], axis=1)
                pick = jnp.where(same & (slot == wanted), 1.0, 0.0)
                picks.append(pick.astype(bf16))
        chosen = jnp.dot(jnp.concatenate(picks, axis=0), keys, preferred_element_type=f32)
        out_ref[pl.ds(first, 8)] = chosen.astype(bf16).reshape(8, 2, SLAB, LANES)
        return carry

    lax.fori_loop(0, FRAMES // 8, some, 0)


def choose(key_list, slab):
    whole = pl.BlockSpec(memory_space=pltpu.VMEM)
    return pl.pallas_call(
        choose_kernel,
        out_shape=jax.ShapeDtypeStruct((FRAMES, 2, SLAB, LANES), bf16),
        in_specs=[pl.BlockSpec(memory_space=pltpu.SMEM), whole],
        out_specs=whole,
        compiler_params=params(16),
        cost_estimate=cost(4 * FRAMES * SLAB * LANES * 256, 6 * FRAMES * SLAB * LANES),
        name="choose",
    )(key_list, slab)


def attend_kernel(
    slab_ref, q_ref, mixed_ref, total_ref, top_ref, wk_ref, wv_ref, wo_ref, video_ref,
    spatial_ref, out_slab_ref, rows_ref, heads_ref,
):
    step = pl.program_id(0)

    @pl.when(step == 0)
    def _():
        swap = swap_matrix()
        for which in range(2):
            slab_to_rows(
                lambda block, half: slab_ref[
                    16 * block : 16 * block + 16, which, 16 * half : 16 * half + 16, :
                ],
                rows_ref, swap, which * TOK,
            )

    keys = jnp.dot(rows_ref[...], wk_ref[...], preferred_element_type=f32).astype(bf16)
    values = jnp.dot(rows_ref[...], wv_ref[...], preferred_element_type=f32)
    for pair in range(2):
        lanes = slice(pair * LANES, (pair + 1) * LANES)
        for k in range(PARTS):
            rows = pl.ds(k * FRAMES, FRAMES)
            top = top_ref[rows, lanes]
            mixed, total, most = attend_pair(
                q_ref[rows, lanes], keys[:, lanes], values[:, lanes], top
            )
            less = jnp.exp2(top - most)
            mixed = mixed + mixed_ref[rows, lanes] * less
            total = total + total_ref[rows, lanes] * less
            heads_ref[step, rows, lanes] = (mixed / total).astype(bf16)

    @pl.when(step == GROUPS - 1)
    def _():
        for k in range(PARTS):
            rows = pl.ds(k * FRAMES, FRAMES)
            heads = jnp.concatenate([heads_ref[g, rows, :] for g in range(GROUPS)], axis=1)
            added = jnp.dot(heads, wo_ref[...], preferred_element_type=f32)
            spatial_ref[rows, :] = (video_ref[rows, :].astype(f32) + added).astype(bf16)
        rows_to_slab(spatial_ref, out_slab_ref, swap_matrix())


def attend(slab, qkv, mixed, total, top, qkv_weight, out_weight, video):
    once = pl.Buffered(1)
    by_group = pl.BlockSpec((TOK, GROUP), lambda i: (0, i))
    return pl.pallas_call(
        attend_kernel,
        grid=(GROUPS,),
        out_shape=(
            jax.ShapeDtypeStruct((TOK, WIDTH), bf16),
            jax.ShapeDtypeStruct((FRAMES, SLAB, LANES), bf16),
        ),
        in_specs=[
            pl.BlockSpec((FRAMES, 2, SLAB, LANES), lambda i: (0, 0, 0, 0), pipeline_mode=once),
            by_group,
            by_group,
            by_group,
            by_group,
            pl.BlockSpec((WIDTH, GROUP), lambda i: (0, GROUPS + i)),
            pl.BlockSpec((WIDTH, GROUP), lambda i: (0, 2 * GROUPS + i)),
            pl.BlockSpec((WIDTH, WIDTH), lambda i: (0, 0), pipeline_mode=once),
            pl.BlockSpec((TOK, WIDTH), lambda i: (0, 0), pipeline_mode=once),
        ],
        out_specs=(
            pl.BlockSpec((TOK, WIDTH), lambda i: (0, 0)),
            pl.BlockSpec((FRAMES, SLAB, LANES), lambda i: (0, 0, 0)),
        ),
        scratch_shapes=[
            pltpu.VMEM((2 * TOK, WIDTH), bf16),
            pltpu.VMEM((GROUPS, TOK, GROUP), bf16),
        ],
        compiler_params=params(40),
        cost_estimate=cost(
            8 * TOK * WIDTH * WIDTH + 16 * TOK * TOK * WIDTH,
            6 * WIDTH * WIDTH + 20 * TOK * WIDTH,
            2 * HEADS * TOK * TOK,
        ),
        name="attend",
    )(slab, qkv, mixed, total, top, qkv_weight, qkv_weight, out_weight, video)


def time_kernel(
    slab_ref, gain_ref, wq_ref, wk_ref, wv_ref, out_slab_ref, rows_ref, heads_ref, swap_ref
):
    step = pl.program_id(0)

    @pl.when(step == 0)
    def _():
        swap_ref[...] = swap_matrix()
        slab_to_rows(
            lambda block, half: slab_ref[
                16 * block : 16 * block + 16, 16 * half : 16 * half + 16, :
            ],
            rows_ref, swap_ref[...],
        )
        for k in range(PARTS):
            rows = pl.ds(k * FRAMES, FRAMES)
            rows_ref[rows, :] = norm_rows(rows_ref[rows, :].astype(f32), gain_ref[...])

    rows = rows_ref[...]
    queries = (jnp.dot(rows, wq_ref[...], preferred_element_type=f32) * SCALE).astype(bf16)
    keys = jnp.dot(rows, wk_ref[...], preferred_element_type=f32).astype(bf16)
    values = jnp.dot(rows, wv_ref[...], preferred_element_type=f32)
    for pair in range(2):
        lanes = slice(pair * LANES, (pair + 1) * LANES)
        for k in range(PARTS):
            at = slice(k * FRAMES, (k + 1) * FRAMES)
            mixed, total, _ = attend_pair(queries[at, lanes], keys[at, lanes], values[at, lanes])
            heads_ref[2 * step + pair, at, :] = (mixed / total).astype(bf16)

    @pl.when(step == GROUPS - 1)
    def _():
        for k in range(PARTS):
            at = slice(k * FRAMES, (k + 1) * FRAMES)
            for g in range(COLS):
                rows_ref[at, g * LANES : (g + 1) * LANES] = heads_ref[g, at, :]
        rows_to_slab(rows_ref, out_slab_ref, swap_ref[...])


def time_attend(slab, gain, weight):
    once = pl.Buffered(1)
    return pl.pallas_call(
        time_kernel,
        grid=(GROUPS,),
        out_shape=jax.ShapeDtypeStruct((FRAMES, SLAB, LANES), bf16),
        in_specs=[
            pl.BlockSpec((FRAMES, SLAB, LANES), lambda i: (0, 0, 0), pipeline_mode=once),
            pl.BlockSpec((1, WIDTH), lambda i: (0, 0)),
            pl.BlockSpec((WIDTH, GROUP), lambda i: (0, i)),
            pl.BlockSpec((WIDTH, GROUP), lambda i: (0, GROUPS + i)),
            pl.BlockSpec((WIDTH, GROUP), lambda i: (0, 2 * GROUPS + i)),
        ],
        out_specs=pl.BlockSpec((FRAMES, SLAB, LANES), lambda i: (0, 0, 0)),
        scratch_shapes=[
            pltpu.VMEM((TOK, WIDTH), bf16),
            pltpu.VMEM((COLS, TOK, LANES), bf16),
            pltpu.VMEM((256, 256), bf16),
        ],
        compiler_params=params(24),
        cost_estimate=cost(
            6 * TOK * WIDTH * WIDTH + 8 * TOK * FRAMES * WIDTH,
            6 * WIDTH * WIDTH + 4 * TOK * WIDTH,
            HEADS * TOK * FRAMES,
        ),
        name="time_attend",
    )(slab, gain, weight, weight, weight)


def unpack_kernel(slab_ref, out_ref):
    slab_to_rows(
        lambda block, half: slab_ref[16 * block : 16 * block + 16, 16 * half : 16 * half + 16, :],
        out_ref, swap_matrix(),
    )


def unpack(slab):
    whole = pl.BlockSpec(memory_space=pltpu.VMEM)
    return pl.pallas_call(
        unpack_kernel,
        out_shape=jax.ShapeDtypeStruct((TOK, WIDTH), bf16),
        in_specs=[whole],
        out_specs=whole,
        compiler_params=params(16),
        cost_estimate=cost(2 * TOK * WIDTH * 256, 4 * TOK * WIDTH),
        name="unpack",
    )(slab)


def exchange(slab):
    return lax.all_to_all(slab, "frame", split_axis=0, concat_axis=0, tiled=True)


def body(video, key_list, pairs, norm_gain, qkv_weight, out_weight, time_gain, time_weight):
    normed, slab = prep(pairs, video, norm_gain.reshape(1, WIDTH))
    spread = exchange(slab)
    qkv = project(normed, qkv_weight)
    wanted = exchange(choose(key_list, spread))
    mixed, total, top = own_attend(qkv)
    spatial, slab = attend(wanted, qkv, mixed, total, top, qkv_weight, out_weight, video)
    slab = time_attend(exchange(slab), time_gain.reshape(1, WIDTH), time_weight)
    return spatial, unpack(exchange(slab))


def solution(mesh):
    return jax.shard_map(
        body,
        mesh=mesh,
        in_specs=(P("frame", None), P(), P("frame", None), P(), P(), P(), P(), P()),
        out_specs=(P("frame", None), P("frame", None)),
        check_vma=False,
    )
```

```python
import jax
import jax.numpy as jnp
from jax import lax
from jax.experimental import pallas as pl
from jax.experimental.pallas import tpu as pltpu
from jax.sharding import PartitionSpec as P

WIDTH = 1280
HEADS = 20
HEAD = 64
TOK = 384
FRAMES = 128
KEYS = 8
PARTS = TOK // FRAMES
LANES = 128
COLS = WIDTH // LANES
SLAB = 32
GROUP = 256
GROUPS = WIDTH // GROUP
CHOSEN = 32
VMEM = 60
SCALE = 0.125 * 1.4426950408889634

bf16 = jnp.bfloat16
f32 = jnp.float32


def params(mib, **more):
    return pltpu.CompilerParams(vmem_limit_bytes=mib << 20, **more)


def cost(flops, moved, exps=0):
    return pl.CostEstimate(flops=int(flops), bytes_accessed=int(moved), transcendentals=int(exps))


def norm_rows(values, gain):
    centred = values - jnp.mean(values, axis=-1, keepdims=True)
    spread = jnp.mean(centred * centred, axis=-1, keepdims=True)
    return (centred * lax.rsqrt(spread + 1e-05) * gain).astype(bf16)


def swap_matrix():
    row = lax.broadcasted_iota(jnp.int32, (256, 256), 0)
    col = lax.broadcasted_iota(jnp.int32, (256, 256), 1)
    return jnp.where(col == (row % 16) * 16 + row // 16, 1.0, 0.0).astype(bf16)


def rows_to_slab(rows_ref, slab_ref, swap, spare=None):
    for half in range(2):
        for pair in range(4):
            sides = []
            for block in (2 * pair, 2 * pair + 1):
                tiles = []
                for unit in range(16 * half, 16 * half + 16):
                    k, g = divmod(unit, COLS)
                    if k < PARTS:
                        at = k * FRAMES + 16 * block
                        tiles.append(rows_ref[at : at + 16, g * LANES : (g + 1) * LANES])
                    elif spare is None:
                        tiles.append(jnp.zeros((16, LANES), bf16))
                    else:
                        tiles.append(spare[unit - PARTS * COLS])
                sides.append(jnp.concatenate(tiles, axis=0))
            both = jnp.concatenate(sides, axis=1)
            moved = jnp.dot(swap, both, preferred_element_type=f32).astype(bf16)
            for side in range(2):
                block = 2 * pair + side
                slab_ref[16 * block : 16 * block + 16, 16 * half : 16 * half + 16, :] = moved[
                    :, side * LANES : (side + 1) * LANES
                ].reshape(16, 16, LANES)


def slab_to_rows(load, rows_ref, swap, first=0):
    for block in range(8):
        both = jnp.concatenate(
            [load(block, half).reshape(256, LANES) for half in range(2)], axis=1
        )
        moved = jnp.dot(swap, both, preferred_element_type=f32).astype(bf16)
        for unit in range(PARTS * COLS):
            half, row = divmod(unit, 16)
            k, g = divmod(unit, COLS)
            at = first + k * FRAMES + 16 * block
            rows_ref[at : at + 16, g * LANES : (g + 1) * LANES] = moved[
                16 * row : 16 * row + 16, half * LANES : (half + 1) * LANES
            ]


def prep_kernel(pairs_ref, video_ref, gain_ref, normed_ref, slab_ref):
    for k in range(PARTS):
        rows = pl.ds(k * FRAMES, FRAMES)
        normed_ref[rows, :] = norm_rows(video_ref[rows, :].astype(f32), gain_ref[...])
    spare = [
        jnp.full((16, LANES), pairs_ref[0, which], jnp.int32).astype(f32).astype(bf16)
        for which in range(2)
    ]
    rows_to_slab(normed_ref, slab_ref, swap_matrix(), spare)


def prep(pairs, video, gain):
    whole = pl.BlockSpec(memory_space=pltpu.VMEM)
    return pl.pallas_call(
        prep_kernel,
        out_shape=(
            jax.ShapeDtypeStruct((TOK, WIDTH), bf16),
            jax.ShapeDtypeStruct((FRAMES, SLAB, LANES), bf16),
        ),
        in_specs=[pl.BlockSpec(memory_space=pltpu.SMEM), whole, whole],
        out_specs=(whole, whole),
        compiler_params=params(VMEM),
        cost_estimate=cost(6 * TOK * WIDTH, 6 * TOK * WIDTH),
        name="prep",
    )(pairs, video, gain)


def project_kernel(rows_ref, wq_ref, wk_ref, wv_ref, q_ref, k_ref, v_ref):
    rows = rows_ref[...]
    queries = jnp.dot(rows, wq_ref[...], preferred_element_type=f32) * SCALE
    q_ref[...] = queries.astype(bf16)
    k_ref[...] = jnp.dot(rows, wk_ref[...], preferred_element_type=f32).astype(bf16)
    v_ref[...] = jnp.dot(rows, wv_ref[...], preferred_element_type=f32).astype(bf16)


def project(rows, weight):
    out = jax.ShapeDtypeStruct((TOK, WIDTH), bf16)
    out_spec = pl.BlockSpec((TOK, GROUP), lambda i: (0, i))
    return pl.pallas_call(
        project_kernel,
        grid=(GROUPS,),
        out_shape=(out, out, out),
        in_specs=[
            pl.BlockSpec((TOK, WIDTH), lambda i: (0, 0)),
            pl.BlockSpec((WIDTH, GROUP), lambda i: (0, i)),
            pl.BlockSpec((WIDTH, GROUP), lambda i: (0, GROUPS + i)),
            pl.BlockSpec((WIDTH, GROUP), lambda i: (0, 2 * GROUPS + i)),
        ],
        out_specs=(out_spec, out_spec, out_spec),
        compiler_params=params(VMEM),
        cost_estimate=cost(6 * TOK * WIDTH * WIDTH, 6 * WIDTH * WIDTH + 8 * TOK * WIDTH),
        name="project",
    )(rows, weight, weight, weight)


def low_lanes(rows):
    return lax.broadcasted_iota(jnp.int32, (rows, LANES), 1) < HEAD


def attend_pairs(units):
    scores, padded = [], []
    for queries, keys, values, _ in units:
        low_q, low_v = low_lanes(queries.shape[0]), low_lanes(values.shape[0])
        wide = queries.astype(f32)
        for head in range(2):
            mine = jnp.where(low_q, wide, 0.0) if head == 0 else jnp.where(low_q, 0.0, wide)
            rest = jnp.where(low_v, values, 1.0) if head == 0 else jnp.where(low_v, 1.0, values)
            padded.append(rest.astype(bf16))
            scores.append(
                lax.dot_general(
                    mine.astype(bf16), keys, (((1,), (1,)), ((), ())), preferred_element_type=f32
                )
            )
    tops = [jnp.max(s, axis=-1, keepdims=True) for s in scores]
    for i, (_, _, _, top) in enumerate(units):
        if top is not None:
            tops[2 * i] = jnp.maximum(tops[2 * i], top[:, 0:1])
            tops[2 * i + 1] = jnp.maximum(tops[2 * i + 1], top[:, HEAD : HEAD + 1])
    weights = [jnp.exp2(s - top).astype(bf16) for s, top in zip(scores, tops)]
    outs = [jnp.dot(w, v, preferred_element_type=f32) for w, v in zip(weights, padded)]
    given = []
    for i, (queries, _, _, _) in enumerate(units):
        low = low_lanes(queries.shape[0])
        one, two = outs[2 * i], outs[2 * i + 1]
        total = pltpu.roll(jnp.where(low, two, one), HEAD, 1)
        given.append((jnp.where(low, one, two), total, jnp.where(low, tops[2 * i], tops[2 * i + 1])))
    return given


def own_kernel(q_ref, k_ref, v_ref, mixed_ref, total_ref, top_ref):
    units = []
    for pair in range(2):
        lanes = slice(pair * LANES, (pair + 1) * LANES)
        units.append((q_ref[:, lanes], k_ref[:, lanes], v_ref[:, lanes].astype(f32), None))
    for pair, (mixed, total, top) in enumerate(attend_pairs(units)):
        lanes = slice(pair * LANES, (pair + 1) * LANES)
        mixed_ref[:, lanes] = mixed
        total_ref[:, lanes] = total
        top_ref[:, lanes] = top


def own_attend(queries, keys, values):
    out = jax.ShapeDtypeStruct((TOK, WIDTH), f32)
    out_spec = pl.BlockSpec((TOK, GROUP), lambda i: (0, i))
    return pl.pallas_call(
        own_kernel,
        grid=(GROUPS,),
        out_shape=(out, out, out),
        in_specs=[out_spec, out_spec, out_spec],
        out_specs=(out_spec, out_spec, out_spec),
        compiler_params=params(VMEM),
        cost_estimate=cost(8 * TOK * TOK * WIDTH, 18 * TOK * WIDTH, HEADS * TOK * TOK),
        name="own_attend",
    )(queries, keys, values)


def choose_kernel(key_list_ref, slab_ref, after_ref, out_ref):
    del after_ref
    halves = [
        jnp.concatenate([slab_ref[key_list_ref[s], at : at + 16, :] for s in range(KEYS)], axis=0)
        for at in (0, 16)
    ]
    keys = jnp.concatenate(halves, axis=1)
    row = lax.broadcasted_iota(jnp.int32, (16, LANES), 0)
    col = lax.broadcasted_iota(jnp.int32, (16, LANES), 1)
    slot = jnp.where(col % 16 == row, col // 16, -1).astype(f32)
    first = pl.program_id(0) * CHOSEN
    for f in range(0, CHOSEN, 8):
        picks = []
        for more in range(8):
            spare = slab_ref[first + f + more, 16:32, :].astype(f32)
            for which in range(2):
                wanted = spare[14 + which : 15 + which, :]
                picks.append(jnp.where(slot == wanted, 1.0, 0.0).astype(bf16))
        chosen = jnp.dot(jnp.concatenate(picks, axis=0), keys, preferred_element_type=f32)
        chosen = chosen.astype(bf16).reshape(8, 2, 16, 2 * LANES)
        out_ref[f : f + 8, :, 0:16, :] = chosen[..., :LANES]
        out_ref[f : f + 8, :, 16:32, :] = chosen[..., LANES:]


def choose(key_list, slab, after):
    return pl.pallas_call(
        choose_kernel,
        grid=(FRAMES // CHOSEN,),
        out_shape=jax.ShapeDtypeStruct((FRAMES, 2, SLAB, LANES), bf16),
        in_specs=[
            pl.BlockSpec(memory_space=pltpu.SMEM),
            pl.BlockSpec((FRAMES, SLAB, LANES), lambda i: (0, 0, 0)),
            pl.BlockSpec(memory_space=pl.ANY),
        ],
        out_specs=pl.BlockSpec((CHOSEN, 2, SLAB, LANES), lambda i: (i, 0, 0, 0)),
        compiler_params=params(VMEM),
        cost_estimate=cost(4 * FRAMES * SLAB * LANES * 256, 6 * FRAMES * SLAB * LANES),
        name="choose",
    )(key_list, slab, after)


def attend_kernel(
    slab_ref, q_ref, mixed_ref, total_ref, top_ref, wk_ref, wv_ref, wo_ref, video_ref,
    spatial_ref, out_slab_ref, rows_ref, heads_ref,
):
    step = pl.program_id(0)

    @pl.when(step == 0)
    def _():
        swap = swap_matrix()
        for which in range(2):
            slab_to_rows(
                lambda block, half: slab_ref[
                    16 * block : 16 * block + 16, which, 16 * half : 16 * half + 16, :
                ],
                rows_ref, swap, which * TOK,
            )

    keys = jnp.dot(rows_ref[...], wk_ref[...], preferred_element_type=f32).astype(bf16)
    values = jnp.dot(rows_ref[...], wv_ref[...], preferred_element_type=f32)
    units = []
    for pair in range(2):
        lanes = slice(pair * LANES, (pair + 1) * LANES)
        units.append((q_ref[:, lanes], keys[:, lanes], values[:, lanes], top_ref[:, lanes]))
    for pair, (mixed, total, most) in enumerate(attend_pairs(units)):
        lanes = slice(pair * LANES, (pair + 1) * LANES)
        less = jnp.exp2(top_ref[:, lanes] - most)
        mixed = mixed + mixed_ref[:, lanes] * less
        total = total + total_ref[:, lanes] * less
        heads_ref[step, :, lanes] = (mixed / total).astype(bf16)

    @pl.when(step == GROUPS - 1)
    def _():
        for k in range(PARTS):
            rows = pl.ds(k * FRAMES, FRAMES)
            heads = jnp.concatenate([heads_ref[g, rows, :] for g in range(GROUPS)], axis=1)
            added = jnp.dot(heads, wo_ref[...], preferred_element_type=f32)
            spatial_ref[rows, :] = (video_ref[rows, :].astype(f32) + added).astype(bf16)
        rows_to_slab(spatial_ref, out_slab_ref, swap_matrix())


def attend(slab, queries, mixed, total, top, qkv_weight, out_weight, video):
    once = pl.Buffered(1)
    by_group = pl.BlockSpec((TOK, GROUP), lambda i: (0, i))
    return pl.pallas_call(
        attend_kernel,
        grid=(GROUPS,),
        out_shape=(
            jax.ShapeDtypeStruct((TOK, WIDTH), bf16),
            jax.ShapeDtypeStruct((FRAMES, SLAB, LANES), bf16),
        ),
        in_specs=[
            pl.BlockSpec((FRAMES, 2, SLAB, LANES), lambda i: (0, 0, 0, 0), pipeline_mode=once),
            by_group,
            by_group,
            by_group,
            by_group,
            pl.BlockSpec((WIDTH, GROUP), lambda i: (0, GROUPS + i)),
            pl.BlockSpec((WIDTH, GROUP), lambda i: (0, 2 * GROUPS + i)),
            pl.BlockSpec((WIDTH, WIDTH), lambda i: (0, 0), pipeline_mode=once),
            pl.BlockSpec((TOK, WIDTH), lambda i: (0, 0), pipeline_mode=once),
        ],
        out_specs=(
            pl.BlockSpec((TOK, WIDTH), lambda i: (0, 0)),
            pl.BlockSpec((FRAMES, SLAB, LANES), lambda i: (0, 0, 0)),
        ),
        scratch_shapes=[
            pltpu.VMEM((2 * TOK, WIDTH), bf16),
            pltpu.VMEM((GROUPS, TOK, GROUP), bf16),
        ],
        compiler_params=params(VMEM),
        cost_estimate=cost(
            8 * TOK * WIDTH * WIDTH + 16 * TOK * TOK * WIDTH,
            6 * WIDTH * WIDTH + 20 * TOK * WIDTH,
            2 * HEADS * TOK * TOK,
        ),
        name="attend",
    )(slab, queries, mixed, total, top, qkv_weight, qkv_weight, out_weight, video)


def time_kernel(
    slab_ref, gain_ref, wq_ref, wk_ref, wv_ref, out_slab_ref, rows_ref, heads_ref, swap_ref
):
    step = pl.program_id(0)

    @pl.when(step == 0)
    def _():
        swap_ref[...] = swap_matrix()
        slab_to_rows(
            lambda block, half: slab_ref[
                16 * block : 16 * block + 16, 16 * half : 16 * half + 16, :
            ],
            rows_ref, swap_ref[...],
        )
        for k in range(PARTS):
            rows = pl.ds(k * FRAMES, FRAMES)
            rows_ref[rows, :] = norm_rows(rows_ref[rows, :].astype(f32), gain_ref[...])

    rows = rows_ref[...]
    queries = (jnp.dot(rows, wq_ref[...], preferred_element_type=f32) * SCALE).astype(bf16)
    keys = jnp.dot(rows, wk_ref[...], preferred_element_type=f32).astype(bf16)
    values = jnp.dot(rows, wv_ref[...], preferred_element_type=f32)
    units, places = [], []
    for pair in range(2):
        lanes = slice(pair * LANES, (pair + 1) * LANES)
        for k in range(PARTS):
            at = slice(k * FRAMES, (k + 1) * FRAMES)
            units.append((queries[at, lanes], keys[at, lanes], values[at, lanes], None))
            places.append((pair, at))
    for (pair, at), (mixed, total, _) in zip(places, attend_pairs(units)):
        heads_ref[2 * step + pair, at, :] = (mixed / total).astype(bf16)

    @pl.when(step == GROUPS - 1)
    def _():
        for k in range(PARTS):
            at = slice(k * FRAMES, (k + 1) * FRAMES)
            for g in range(COLS):
                rows_ref[at, g * LANES : (g + 1) * LANES] = heads_ref[g, at, :]
        rows_to_slab(rows_ref, out_slab_ref, swap_ref[...])


def time_attend(slab, gain, weight):
    once = pl.Buffered(1)
    return pl.pallas_call(
        time_kernel,
        grid=(GROUPS,),
        out_shape=jax.ShapeDtypeStruct((FRAMES, SLAB, LANES), bf16),
        in_specs=[
            pl.BlockSpec((FRAMES, SLAB, LANES), lambda i: (0, 0, 0), pipeline_mode=once),
            pl.BlockSpec((1, WIDTH), lambda i: (0, 0)),
            pl.BlockSpec((WIDTH, GROUP), lambda i: (0, i)),
            pl.BlockSpec((WIDTH, GROUP), lambda i: (0, GROUPS + i)),
            pl.BlockSpec((WIDTH, GROUP), lambda i: (0, 2 * GROUPS + i)),
        ],
        out_specs=pl.BlockSpec((FRAMES, SLAB, LANES), lambda i: (0, 0, 0)),
        scratch_shapes=[
            pltpu.VMEM((TOK, WIDTH), bf16),
            pltpu.VMEM((COLS, TOK, LANES), bf16),
            pltpu.VMEM((256, 256), bf16),
        ],
        compiler_params=params(VMEM),
        cost_estimate=cost(
            6 * TOK * WIDTH * WIDTH + 8 * TOK * FRAMES * WIDTH,
            6 * WIDTH * WIDTH + 4 * TOK * WIDTH,
            HEADS * TOK * FRAMES,
        ),
        name="time_attend",
    )(slab, gain, weight, weight, weight)


def unpack_kernel(slab_ref, out_ref):
    slab_to_rows(
        lambda block, half: slab_ref[16 * block : 16 * block + 16, 16 * half : 16 * half + 16, :],
        out_ref, swap_matrix(),
    )


def unpack(slab):
    whole = pl.BlockSpec(memory_space=pltpu.VMEM)
    return pl.pallas_call(
        unpack_kernel,
        out_shape=jax.ShapeDtypeStruct((TOK, WIDTH), bf16),
        in_specs=[whole],
        out_specs=whole,
        compiler_params=params(VMEM),
        cost_estimate=cost(2 * TOK * WIDTH * 256, 4 * TOK * WIDTH),
        name="unpack",
    )(slab)


def exchange(slab):
    return lax.all_to_all(slab, "frame", split_axis=0, concat_axis=0, tiled=True)


def body(video, key_list, pairs, norm_gain, qkv_weight, out_weight, time_gain, time_weight):
    normed, slab = prep(pairs, video, norm_gain.reshape(1, WIDTH))
    spread = exchange(slab)
    queries, keys, values = project(normed, qkv_weight)
    wanted = exchange(choose(key_list, spread, queries))
    mixed, total, top = own_attend(queries, keys, values)
    spatial, slab = attend(wanted, queries, mixed, total, top, qkv_weight, out_weight, video)
    slab = time_attend(exchange(slab), time_gain.reshape(1, WIDTH), time_weight)
    return spatial, unpack(exchange(slab))


def solution(mesh):
    return jax.shard_map(
        body,
        mesh=mesh,
        in_specs=(P("frame", None), P(), P("frame", None), P(), P(), P(), P(), P()),
        out_specs=(P("frame", None), P("frame", None)),
        check_vma=False,
    )
```

```python
import jax
import jax.numpy as jnp
from jax import lax
from jax.experimental import pallas as pl
from jax.experimental.pallas import tpu as pltpu
from jax.sharding import PartitionSpec as P

WIDTH = 1280
HEADS = 20
HEAD = 64
TOK = 384
FRAMES = 128
KEYS = 8
PARTS = TOK // FRAMES
LANES = 128
COLS = WIDTH // LANES
SLAB = 32
GROUP = 256
GROUPS = WIDTH // GROUP
VMEM = 52
SCALE = 0.125 * 1.4426950408889634

bf16 = jnp.bfloat16
f32 = jnp.float32


def params(mib, **more):
    return pltpu.CompilerParams(vmem_limit_bytes=mib << 20, **more)


def cost(flops, moved, exps=0):
    return pl.CostEstimate(flops=int(flops), bytes_accessed=int(moved), transcendentals=int(exps))


def in_vmem(x):
    return pltpu.with_memory_space_constraint(x, pltpu.VMEM)


def in_hbm(x):
    return pltpu.with_memory_space_constraint(x, pltpu.HBM)


WHOLE = pl.BlockSpec(memory_space=pltpu.VMEM)
THERE = pl.BlockSpec(memory_space=pl.ANY)
SMALL = pl.BlockSpec(memory_space=pltpu.SMEM)


def norm_rows(values, gain):
    centred = values - jnp.mean(values, axis=-1, keepdims=True)
    spread = jnp.mean(centred * centred, axis=-1, keepdims=True)
    return (centred * lax.rsqrt(spread + 1e-05) * gain).astype(bf16)


def swap_matrix():
    row = lax.broadcasted_iota(jnp.int32, (256, 256), 0)
    col = lax.broadcasted_iota(jnp.int32, (256, 256), 1)
    return jnp.where(col == (row % 16) * 16 + row // 16, 1.0, 0.0).astype(bf16)


def rows_to_slab(rows_ref, slab_ref, swap, spare=None):
    for half in range(2):
        for pair in range(4):
            sides = []
            for block in (2 * pair, 2 * pair + 1):
                tiles = []
                for unit in range(16 * half, 16 * half + 16):
                    k, g = divmod(unit, COLS)
                    if k < PARTS:
                        at = k * FRAMES + 16 * block
                        tiles.append(rows_ref[at : at + 16, g * LANES : (g + 1) * LANES])
                    elif spare is None:
                        tiles.append(jnp.zeros((16, LANES), bf16))
                    else:
                        tiles.append(spare[unit - PARTS * COLS])
                sides.append(jnp.concatenate(tiles, axis=0))
            both = jnp.concatenate(sides, axis=1)
            moved = jnp.dot(swap, both, preferred_element_type=f32).astype(bf16)
            for side in range(2):
                block = 2 * pair + side
                slab_ref[16 * block : 16 * block + 16, 16 * half : 16 * half + 16, :] = moved[
                    :, side * LANES : (side + 1) * LANES
                ].reshape(16, 16, LANES)


def slab_to_rows(load, rows_ref, swap, first=0):
    for block in range(8):
        both = jnp.concatenate(
            [load(block, half).reshape(256, LANES) for half in range(2)], axis=1
        )
        moved = jnp.dot(swap, both, preferred_element_type=f32).astype(bf16)
        for unit in range(PARTS * COLS):
            half, row = divmod(unit, 16)
            k, g = divmod(unit, COLS)
            at = first + k * FRAMES + 16 * block
            rows_ref[at : at + 16, g * LANES : (g + 1) * LANES] = moved[
                16 * row : 16 * row + 16, half * LANES : (half + 1) * LANES
            ]


def prep_kernel(pairs_ref, video_ref, gain_ref, normed_ref, slab_ref):
    for k in range(PARTS):
        rows = pl.ds(k * FRAMES, FRAMES)
        normed_ref[rows, :] = norm_rows(video_ref[rows, :].astype(f32), gain_ref[...].reshape(1, WIDTH))
    spare = [
        jnp.full((16, LANES), pairs_ref[0, which], jnp.int32).astype(f32).astype(bf16)
        for which in range(2)
    ]
    rows_to_slab(normed_ref, slab_ref, swap_matrix(), spare)


def prep(pairs, video, gain):
    return pl.pallas_call(
        prep_kernel,
        out_shape=(
            pltpu.HBM((TOK, WIDTH), bf16),
            pltpu.HBM((FRAMES, SLAB, LANES), bf16),
        ),
        in_specs=[SMALL, WHOLE, WHOLE],
        out_specs=(WHOLE, WHOLE),
        compiler_params=params(VMEM),
        cost_estimate=cost(6 * TOK * WIDTH, 6 * TOK * WIDTH),
        name="prep",
    )(in_hbm(pairs), in_hbm(video), in_hbm(gain))


def project_kernel(rows_ref, wq_ref, wk_ref, wv_ref, q_ref, k_ref, v_ref):
    rows = rows_ref[...]
    queries = jnp.dot(rows, wq_ref[...], preferred_element_type=f32) * SCALE
    q_ref[...] = queries.astype(bf16)
    k_ref[...] = jnp.dot(rows, wk_ref[...], preferred_element_type=f32).astype(bf16)
    v_ref[...] = jnp.dot(rows, wv_ref[...], preferred_element_type=f32).astype(bf16)


def project(rows, weight):
    out = pltpu.HBM((TOK, WIDTH), bf16)
    out_spec = pl.BlockSpec((TOK, GROUP), lambda i: (0, i))
    return pl.pallas_call(
        project_kernel,
        grid=(GROUPS,),
        out_shape=(out, out, out),
        in_specs=[
            WHOLE,
            pl.BlockSpec((WIDTH, GROUP), lambda i: (0, i)),
            pl.BlockSpec((WIDTH, GROUP), lambda i: (0, GROUPS + i)),
            pl.BlockSpec((WIDTH, GROUP), lambda i: (0, 2 * GROUPS + i)),
        ],
        out_specs=(out_spec, out_spec, out_spec),
        compiler_params=params(VMEM),
        cost_estimate=cost(6 * TOK * WIDTH * WIDTH, 6 * WIDTH * WIDTH + 8 * TOK * WIDTH),
        name="project",
    )(in_hbm(rows), in_hbm(weight), in_hbm(weight), in_hbm(weight))


def low_lanes(rows):
    return lax.broadcasted_iota(jnp.int32, (rows, LANES), 1) < HEAD


def attend_pairs(units):
    scores, padded = [], []
    for queries, keys, values, _ in units:
        low_q, low_v = low_lanes(queries.shape[0]), low_lanes(values.shape[0])
        wide = queries.astype(f32)
        for head in range(2):
            mine = jnp.where(low_q, wide, 0.0) if head == 0 else jnp.where(low_q, 0.0, wide)
            rest = jnp.where(low_v, values, 1.0) if head == 0 else jnp.where(low_v, 1.0, values)
            padded.append(rest.astype(bf16))
            scores.append(
                lax.dot_general(
                    mine.astype(bf16), keys, (((1,), (1,)), ((), ())), preferred_element_type=f32
                )
            )
    tops = [jnp.max(s, axis=-1, keepdims=True) for s in scores]
    for i, (_, _, _, top) in enumerate(units):
        if top is not None:
            for head in range(2):
                other = top[:, head * HEAD : head * HEAD + 1]
                tops[2 * i + head] = jnp.maximum(tops[2 * i + head], other)
    weights = [jnp.exp2(s - top).astype(bf16) for s, top in zip(scores, tops)]
    outs = [jnp.dot(w, v, preferred_element_type=f32) for w, v in zip(weights, padded)]
    given = []
    for i, (queries, _, _, _) in enumerate(units):
        low = low_lanes(queries.shape[0])
        one, two = outs[2 * i], outs[2 * i + 1]
        total = pltpu.roll(jnp.where(low, two, one), HEAD, 1)
        given.append((jnp.where(low, one, two), total, tops[2 * i : 2 * i + 2]))
    return given


def group_lanes(group, size, offset=0):
    return pl.ds(pl.multiple_of(offset + group * GROUP, LANES), size)


def own_kernel(q_ref, k_ref, v_ref, mixed_ref, total_ref, top_ref):
    @pl.loop(0, GROUPS)
    def _(group):
        places = [group_lanes(group, LANES, pair * LANES) for pair in range(2)]
        units = [(q_ref[:, at], k_ref[:, at], v_ref[:, at].astype(f32), None) for at in places]
        low = low_lanes(TOK)
        for at, (mixed, total, tops) in zip(places, attend_pairs(units)):
            mixed_ref[:, at] = mixed
            total_ref[:, at] = total
            top_ref[:, at] = jnp.where(low, tops[0], tops[1])


def own_attend(queries, keys, values):
    out = pltpu.HBM((TOK, WIDTH), f32)
    return pl.pallas_call(
        own_kernel,
        out_shape=(out, out, out),
        in_specs=[WHOLE, WHOLE, WHOLE],
        out_specs=(WHOLE, WHOLE, WHOLE),
        compiler_params=params(VMEM),
        cost_estimate=cost(8 * TOK * TOK * WIDTH, 30 * TOK * WIDTH, HEADS * TOK * TOK),
        name="own_attend",
    )(in_hbm(queries), in_hbm(keys), in_hbm(values))


def choose_kernel(key_list_ref, slab_ref, after_ref, out_ref):
    del after_ref
    halves = [
        jnp.concatenate([slab_ref[key_list_ref[s], at : at + 16, :] for s in range(KEYS)], axis=0)
        for at in (0, 16)
    ]
    keys = jnp.concatenate(halves, axis=1)
    row = lax.broadcasted_iota(jnp.int32, (16, LANES), 0)
    col = lax.broadcasted_iota(jnp.int32, (16, LANES), 1)
    slot = jnp.where(col % 16 == row, col // 16, -1).astype(f32)
    for f in range(0, FRAMES, 8):
        picks = []
        for more in range(8):
            spare = slab_ref[f + more, 16:32, :].astype(f32)
            for which in range(2):
                wanted = spare[14 + which : 15 + which, :]
                picks.append(jnp.where(slot == wanted, 1.0, 0.0).astype(bf16))
        chosen = jnp.dot(jnp.concatenate(picks, axis=0), keys, preferred_element_type=f32)
        chosen = chosen.astype(bf16).reshape(8, 2, 16, 2 * LANES)
        out_ref[f : f + 8, :, 0:16, :] = chosen[..., :LANES]
        out_ref[f : f + 8, :, 16:32, :] = chosen[..., LANES:]


def choose(key_list, slab, after):
    return pl.pallas_call(
        choose_kernel,
        out_shape=jax.ShapeDtypeStruct((FRAMES, 2, SLAB, LANES), bf16),
        in_specs=[SMALL, WHOLE, THERE],
        out_specs=WHOLE,
        compiler_params=params(VMEM),
        cost_estimate=cost(4 * FRAMES * SLAB * LANES * 256, 6 * FRAMES * SLAB * LANES),
        name="choose",
    )(in_hbm(key_list), in_vmem(slab), in_hbm(after))


LARGE = 1e30


def attend_kernel(
    slab_ref, q_hbm, mixed_hbm, total_hbm, top_hbm, weight_hbm, wo_hbm, video_hbm,
    spatial_ref, out_slab_ref,
    rows_ref, heads_ref, most_ref, q_ref, mixed_ref, total_ref, top_ref, wk_ref, wv_ref,
    wo_ref, video_ref, sems, last_sems,
):
    def copies(group):
        pairs = (
            (weight_hbm.at[:, group_lanes(group, GROUP, WIDTH)], wk_ref),
            (weight_hbm.at[:, group_lanes(group, GROUP, 2 * WIDTH)], wv_ref),
            (q_hbm.at[:, group_lanes(group, GROUP)], q_ref),
            (top_hbm.at[:, group_lanes(group, GROUP)], top_ref),
            (mixed_hbm.at[:, group_lanes(group, GROUP)], mixed_ref),
            (total_hbm.at[:, group_lanes(group, GROUP)], total_ref),
        )
        return [
            pltpu.make_async_copy(source, target.at[group], sems.at[i, group])
            for i, (source, target) in enumerate(pairs)
        ]

    last = (
        pltpu.make_async_copy(wo_hbm, wo_ref, last_sems.at[0]),
        pltpu.make_async_copy(video_hbm, video_ref, last_sems.at[1]),
    )
    for group in range(GROUPS):
        for copy in copies(group):
            copy.start()
    for copy in last:
        copy.start()

    swap = swap_matrix()
    for which in range(2):
        slab_to_rows(
            lambda block, half: slab_ref[
                16 * block : 16 * block + 16, which, 16 * half : 16 * half + 16, :
            ],
            rows_ref, swap, which * TOK,
        )
    most_ref[...] = jnp.zeros_like(most_ref)

    def project_group(group):
        rows = rows_ref[...]
        keys = jnp.dot(rows, wk_ref[group], preferred_element_type=f32).astype(bf16)
        return keys, jnp.dot(rows, wv_ref[group], preferred_element_type=f32)

    @pl.loop(0, GROUPS)
    def _(group):
        for copy in copies(group):
            copy.wait()
        keys, values = project_group(group)
        low_q, low_v = low_lanes(TOK), low_lanes(2 * TOK)
        outs = []
        for pair in range(2):
            lanes = slice(pair * LANES, (pair + 1) * LANES)
            queries = q_ref[group, :, lanes].astype(f32)
            some = values[:, lanes]
            top = top_ref[group, :, lanes]
            other = pltpu.roll(top, HEAD, 1)
            for head in range(2):
                if head == 0:
                    mine, padded = jnp.where(low_q, queries, 0.0), jnp.where(low_v, some, 1.0)
                    wide = jnp.where(low_q, top, other)
                else:
                    mine, padded = jnp.where(low_q, 0.0, queries), jnp.where(low_v, 1.0, some)
                    wide = jnp.where(low_q, other, top)
                scores = lax.dot_general(
                    mine.astype(bf16), keys[:, lanes], (((1,), (1,)), ((), ())),
                    preferred_element_type=f32,
                )
                tops = jnp.concatenate([wide] * (2 * TOK // LANES), axis=1)
                weights = jnp.exp2(scores - tops).astype(bf16)
                outs.append(jnp.dot(weights, padded.astype(bf16), preferred_element_type=f32))
        for pair in range(2):
            lanes = slice(pair * LANES, (pair + 1) * LANES)
            one, two = outs[2 * pair], outs[2 * pair + 1]
            mixed = jnp.where(low_q, one, two) + mixed_ref[group, :, lanes]
            total = jnp.where(low_q, two, one)
            total = pltpu.roll(total, HEAD, 1) + total_ref[group, :, lanes]
            heads_ref[2 * group + pair] = (mixed / total).astype(bf16)
            most = jnp.max(total.reshape(TOK // 8, 8, LANES), axis=0)
            most_ref[...] = jnp.maximum(most_ref[...], most)

    @pl.when(jnp.logical_not(jnp.max(most_ref[...]) < LARGE))
    def _():
        @pl.loop(0, GROUPS)
        def _(group):
            keys, values = project_group(group)
            for pair in range(2):
                lanes = slice(pair * LANES, (pair + 1) * LANES)
                top = top_ref[group, :, lanes]
                ((mixed, total, tops),) = attend_pairs(
                    [(q_ref[group, :, lanes], keys[:, lanes], values[:, lanes], top)]
                )
                less = jnp.exp2(top - jnp.where(low_lanes(TOK), tops[0], tops[1]))
                mixed = mixed + mixed_ref[group, :, lanes] * less
                total = total + total_ref[group, :, lanes] * less
                heads_ref[2 * group + pair] = (mixed / total).astype(bf16)

    for copy in last:
        copy.wait()
    for k in range(PARTS):
        rows = pl.ds(k * FRAMES, FRAMES)
        heads = jnp.concatenate([heads_ref[c, rows, :] for c in range(COLS)], axis=1)
        added = jnp.dot(heads, wo_ref[...], preferred_element_type=f32)
        spatial_ref[rows, :] = (video_ref[rows, :].astype(f32) + added).astype(bf16)
    rows_to_slab(spatial_ref, out_slab_ref, swap)


def attend(slab, queries, mixed, total, top, weight, out_weight, video):
    return pl.pallas_call(
        attend_kernel,
        out_shape=(
            jax.ShapeDtypeStruct((TOK, WIDTH), bf16),
            jax.ShapeDtypeStruct((FRAMES, SLAB, LANES), bf16),
        ),
        in_specs=[WHOLE] + [THERE] * 7,
        out_specs=(WHOLE, WHOLE),
        scratch_shapes=[
            pltpu.VMEM((2 * TOK, WIDTH), bf16),
            pltpu.VMEM((COLS, TOK, LANES), bf16),
            pltpu.VMEM((8, LANES), f32),
            pltpu.VMEM((GROUPS, TOK, GROUP), bf16),
            pltpu.VMEM((GROUPS, TOK, GROUP), f32),
            pltpu.VMEM((GROUPS, TOK, GROUP), f32),
            pltpu.VMEM((GROUPS, TOK, GROUP), f32),
            pltpu.VMEM((GROUPS, WIDTH, GROUP), bf16),
            pltpu.VMEM((GROUPS, WIDTH, GROUP), bf16),
            pltpu.VMEM((WIDTH, WIDTH), bf16),
            pltpu.VMEM((TOK, WIDTH), bf16),
            pltpu.SemaphoreType.DMA((6, GROUPS)),
            pltpu.SemaphoreType.DMA((2,)),
        ],
        compiler_params=params(VMEM),
        cost_estimate=cost(
            8 * TOK * WIDTH * WIDTH + 16 * TOK * TOK * WIDTH,
            6 * WIDTH * WIDTH + 20 * TOK * WIDTH,
            2 * HEADS * TOK * TOK,
        ),
        name="attend",
    )(
        in_vmem(slab), in_hbm(queries), in_hbm(mixed), in_hbm(total), in_hbm(top),
        in_hbm(weight), in_hbm(out_weight), in_hbm(video),
    )


def time_kernel(
    slab_ref, gain_ref, weight_hbm, out_slab_ref, rows_ref, heads_ref, weight_ref, sems
):
    def copies(group):
        return [
            pltpu.make_async_copy(
                weight_hbm.at[:, group_lanes(group, GROUP, which * WIDTH)],
                weight_ref.at[which, group],
                sems.at[which, group],
            )
            for which in range(3)
        ]

    for group in range(GROUPS):
        for copy in copies(group):
            copy.start()
    swap = swap_matrix()
    slab_to_rows(
        lambda block, half: slab_ref[16 * block : 16 * block + 16, 16 * half : 16 * half + 16, :],
        rows_ref, swap,
    )
    for k in range(PARTS):
        rows = pl.ds(k * FRAMES, FRAMES)
        rows_ref[rows, :] = norm_rows(rows_ref[rows, :].astype(f32), gain_ref[...].reshape(1, WIDTH))

    @pl.loop(0, GROUPS)
    def _(group):
        for copy in copies(group):
            copy.wait()
        rows = rows_ref[...]
        made = [
            jnp.dot(rows, weight_ref[which, group], preferred_element_type=f32)
            for which in range(3)
        ]
        queries, keys, values = (made[0] * SCALE).astype(bf16), made[1].astype(bf16), made[2]
        units, places = [], []
        for pair in range(2):
            lanes = slice(pair * LANES, (pair + 1) * LANES)
            for k in range(PARTS):
                at = slice(k * FRAMES, (k + 1) * FRAMES)
                units.append((queries[at, lanes], keys[at, lanes], values[at, lanes], None))
                places.append((pair, at))
        for (pair, at), (mixed, total, _) in zip(places, attend_pairs(units)):
            heads_ref[2 * group + pair, at, :] = (mixed / total).astype(bf16)

    for k in range(PARTS):
        at = slice(k * FRAMES, (k + 1) * FRAMES)
        for g in range(COLS):
            rows_ref[at, g * LANES : (g + 1) * LANES] = heads_ref[g, at, :]
    rows_to_slab(rows_ref, out_slab_ref, swap)


def time_attend(slab, gain, weight):
    return pl.pallas_call(
        time_kernel,
        out_shape=jax.ShapeDtypeStruct((FRAMES, SLAB, LANES), bf16),
        in_specs=[WHOLE, WHOLE, THERE],
        out_specs=WHOLE,
        scratch_shapes=[
            pltpu.VMEM((TOK, WIDTH), bf16),
            pltpu.VMEM((COLS, TOK, LANES), bf16),
            pltpu.VMEM((3, GROUPS, WIDTH, GROUP), bf16),
            pltpu.SemaphoreType.DMA((3, GROUPS)),
        ],
        compiler_params=params(VMEM),
        cost_estimate=cost(
            6 * TOK * WIDTH * WIDTH + 8 * TOK * FRAMES * WIDTH,
            6 * WIDTH * WIDTH + 4 * TOK * WIDTH,
            HEADS * TOK * FRAMES,
        ),
        name="time_attend",
    )(in_vmem(slab), in_hbm(gain), in_hbm(weight))


def unpack_kernel(slab_ref, out_ref):
    slab_to_rows(
        lambda block, half: slab_ref[16 * block : 16 * block + 16, 16 * half : 16 * half + 16, :],
        out_ref, swap_matrix(),
    )


def unpack(slab):
    return pl.pallas_call(
        unpack_kernel,
        out_shape=jax.ShapeDtypeStruct((TOK, WIDTH), bf16),
        in_specs=[WHOLE],
        out_specs=WHOLE,
        compiler_params=params(VMEM),
        cost_estimate=cost(2 * TOK * WIDTH * 256, 4 * TOK * WIDTH),
        name="unpack",
    )(in_vmem(slab))


def exchange(slab):
    return lax.all_to_all(slab, "frame", split_axis=0, concat_axis=0, tiled=True)


def body(video, key_list, pairs, norm_gain, qkv_weight, out_weight, time_gain, time_weight):
    normed, slab = prep(pairs, video, norm_gain)
    spread = exchange(slab)
    queries, keys, values = project(normed, qkv_weight)
    wanted = exchange(choose(key_list, spread, queries))
    mixed, total, top = own_attend(queries, keys, values)
    spatial, slab = attend(wanted, queries, mixed, total, top, qkv_weight, out_weight, video)
    slab = time_attend(exchange(slab), time_gain, time_weight)
    return spatial, unpack(exchange(slab))


def solution(mesh):
    return jax.shard_map(
        body,
        mesh=mesh,
        in_specs=(P("frame", None), P(), P("frame", None), P(), P(), P(), P(), P()),
        out_specs=(P("frame", None), P("frame", None)),
        check_vma=False,
    )
```

```python
import jax
import jax.numpy as jnp
from jax import lax
from jax.experimental import pallas as pl
from jax.experimental.pallas import tpu as pltpu
from jax.sharding import PartitionSpec as P

WIDTH = 1280
HEADS = 20
HEAD = 64
TOK = 384
FRAMES = 128
KEYS = 8
PARTS = TOK // FRAMES
LANES = 128
COLS = WIDTH // LANES
SLAB = 32
GROUP = 256
GROUPS = WIDTH // GROUP
VMEM = 52
SCALE = 0.125 * 1.4426950408889634

bf16 = jnp.bfloat16
f32 = jnp.float32


def params(mib, **more):
    return pltpu.CompilerParams(vmem_limit_bytes=mib << 20, **more)


def cost(flops, moved, exps=0):
    return pl.CostEstimate(flops=int(flops), bytes_accessed=int(moved), transcendentals=int(exps))


def in_vmem(x):
    return pltpu.with_memory_space_constraint(x, pltpu.VMEM)


def in_hbm(x):
    return pltpu.with_memory_space_constraint(x, pltpu.HBM)


WHOLE = pl.BlockSpec(memory_space=pltpu.VMEM)
THERE = pl.BlockSpec(memory_space=pl.ANY)
SMALL = pl.BlockSpec(memory_space=pltpu.SMEM)


def norm_rows(values, gain):
    centred = values - jnp.mean(values, axis=-1, keepdims=True)
    spread = jnp.mean(centred * centred, axis=-1, keepdims=True)
    return (centred * lax.rsqrt(spread + 1e-05) * gain).astype(bf16)


def swap_matrix():
    row = lax.broadcasted_iota(jnp.int32, (256, 256), 0)
    col = lax.broadcasted_iota(jnp.int32, (256, 256), 1)
    return jnp.where(col == (row % 16) * 16 + row // 16, 1.0, 0.0).astype(bf16)


def rows_to_slab(tile, slab_ref, swap, spare=None, halves=(0, 1)):
    for half in halves:
        for pair in range(4):
            sides = []
            for block in (2 * pair, 2 * pair + 1):
                tiles = []
                for unit in range(16 * half, 16 * half + 16):
                    k, g = divmod(unit, COLS)
                    if k < PARTS:
                        tiles.append(tile(k * FRAMES + 16 * block, g))
                    elif spare is None:
                        tiles.append(jnp.zeros((16, LANES), bf16))
                    else:
                        tiles.append(spare[unit - PARTS * COLS])
                sides.append(jnp.concatenate(tiles, axis=0))
            both = jnp.concatenate(sides, axis=1)
            moved = jnp.dot(swap, both, preferred_element_type=f32).astype(bf16)
            for side in range(2):
                block = 2 * pair + side
                slab_ref[16 * block : 16 * block + 16, 16 * half : 16 * half + 16, :] = moved[
                    :, side * LANES : (side + 1) * LANES
                ].reshape(16, 16, LANES)


def tiles_of(rows_ref):
    return lambda at, g: rows_ref[at : at + 16, g * LANES : (g + 1) * LANES]


def slab_to_rows(load, rows_ref, swap, first=0, blocks=range(8)):
    for block in blocks:
        both = jnp.concatenate(
            [load(block, half).reshape(256, LANES) for half in range(2)], axis=1
        )
        moved = jnp.dot(swap, both, preferred_element_type=f32).astype(bf16)
        for unit in range(PARTS * COLS):
            half, row = divmod(unit, 16)
            k, g = divmod(unit, COLS)
            at = first + k * FRAMES + 16 * block
            rows_ref[at : at + 16, g * LANES : (g + 1) * LANES] = moved[
                16 * row : 16 * row + 16, half * LANES : (half + 1) * LANES
            ]


def prep_kernel(
    pairs_ref, video_hbm, gain_ref, slab_hbm, video_ref, normed_ref, slab_ref, sems, out_sems
):
    arriving = []
    for part in range(2 * PARTS):
        rows = pl.ds(part * 64, 64)
        arriving.append(
            pltpu.make_async_copy(video_hbm.at[rows], video_ref.at[rows], sems.at[part])
        )
        arriving[-1].start()
    spare = [
        jnp.full((16, LANES), pairs_ref[0, which], jnp.int32).astype(f32).astype(bf16)
        for which in range(2)
    ]
    swap = swap_matrix()
    gain = gain_ref[...].reshape(1, WIDTH)
    leaving = []

    def give(half):
        rows_to_slab(tiles_of(normed_ref), slab_ref, swap, spare, halves=(half,))
        some = pl.ds(16 * half, 16)
        leaving.append(
            pltpu.make_async_copy(slab_ref.at[:, some], slab_hbm.at[:, some], out_sems.at[half])
        )
        leaving[-1].start()

    for part, copy in enumerate(arriving):
        copy.wait()
        rows = pl.ds(part * 64, 64)
        normed_ref[rows, :] = norm_rows(video_ref[rows, :].astype(f32), gain)
        if part == 3:
            give(0)
    give(1)
    for copy in leaving:
        copy.wait()


def prep(pairs, video, gain):
    return pl.pallas_call(
        prep_kernel,
        out_shape=pltpu.HBM((FRAMES, SLAB, LANES), bf16),
        in_specs=[SMALL, THERE, WHOLE],
        out_specs=THERE,
        scratch_shapes=[
            pltpu.VMEM((TOK, WIDTH), bf16),
            pltpu.VMEM((TOK, WIDTH), bf16),
            pltpu.VMEM((FRAMES, SLAB, LANES), bf16),
            pltpu.SemaphoreType.DMA((2 * PARTS,)),
            pltpu.SemaphoreType.DMA((2,)),
        ],
        compiler_params=params(VMEM),
        cost_estimate=cost(6 * TOK * WIDTH, 4 * TOK * WIDTH),
        name="prep",
    )(in_hbm(pairs), in_hbm(video), in_hbm(gain))


def project_kernel(video_ref, gain_ref, wq_ref, wk_ref, wv_ref, q_ref, k_ref, v_ref, normed_ref):
    @pl.when(pl.program_id(0) == 0)
    def _():
        gain = gain_ref[...].reshape(1, WIDTH)
        normed_ref[...] = norm_rows(video_ref[...].astype(f32), gain)

    rows = normed_ref[...]
    queries = jnp.dot(rows, wq_ref[...], preferred_element_type=f32) * SCALE
    q_ref[...] = queries.astype(bf16)
    k_ref[...] = jnp.dot(rows, wk_ref[...], preferred_element_type=f32).astype(bf16)
    v_ref[...] = jnp.dot(rows, wv_ref[...], preferred_element_type=f32).astype(bf16)


def project(video, gain, weight):
    out = pltpu.HBM((TOK, WIDTH), bf16)
    out_spec = pl.BlockSpec((TOK, GROUP), lambda i: (0, i))
    return pl.pallas_call(
        project_kernel,
        grid=(GROUPS,),
        out_shape=(out, out, out),
        in_specs=[
            WHOLE,
            WHOLE,
            pl.BlockSpec((WIDTH, GROUP), lambda i: (0, i)),
            pl.BlockSpec((WIDTH, GROUP), lambda i: (0, GROUPS + i)),
            pl.BlockSpec((WIDTH, GROUP), lambda i: (0, 2 * GROUPS + i)),
        ],
        out_specs=(out_spec, out_spec, out_spec),
        scratch_shapes=[pltpu.VMEM((TOK, WIDTH), bf16)],
        compiler_params=params(VMEM),
        cost_estimate=cost(6 * TOK * WIDTH * WIDTH, 6 * WIDTH * WIDTH + 8 * TOK * WIDTH),
        name="project",
    )(in_hbm(video), in_hbm(gain), in_hbm(weight), in_hbm(weight), in_hbm(weight))


def low_lanes(rows):
    return lax.broadcasted_iota(jnp.int32, (rows, LANES), 1) < HEAD


def attend_pairs(units):
    scores, padded = [], []
    for queries, keys, values, _ in units:
        low_q, low_v = low_lanes(queries.shape[0]), low_lanes(values.shape[0])
        wide = queries.astype(f32)
        for head in range(2):
            mine = jnp.where(low_q, wide, 0.0) if head == 0 else jnp.where(low_q, 0.0, wide)
            rest = jnp.where(low_v, values, 1.0) if head == 0 else jnp.where(low_v, 1.0, values)
            padded.append(rest.astype(bf16))
            scores.append(
                lax.dot_general(
                    mine.astype(bf16), keys, (((1,), (1,)), ((), ())), preferred_element_type=f32
                )
            )
    tops = [jnp.max(s, axis=-1, keepdims=True) for s in scores]
    for i, (_, _, _, top) in enumerate(units):
        if top is not None:
            for head in range(2):
                other = top[:, head * HEAD : head * HEAD + 1]
                tops[2 * i + head] = jnp.maximum(tops[2 * i + head], other)
    weights = [jnp.exp2(s - top).astype(bf16) for s, top in zip(scores, tops)]
    outs = [jnp.dot(w, v, preferred_element_type=f32) for w, v in zip(weights, padded)]
    given = []
    for i, (queries, _, _, _) in enumerate(units):
        low = low_lanes(queries.shape[0])
        one, two = outs[2 * i], outs[2 * i + 1]
        total = pltpu.roll(jnp.where(low, two, one), HEAD, 1)
        given.append((jnp.where(low, one, two), total, tops[2 * i : 2 * i + 2]))
    return given


def group_lanes(group, size, offset=0):
    return pl.ds(pl.multiple_of(offset + group * GROUP, LANES), size)


def own_kernel(q_ref, k_ref, v_ref, mixed_ref, total_ref, top_ref):
    @pl.loop(0, GROUPS)
    def _(group):
        places = [group_lanes(group, LANES, pair * LANES) for pair in range(2)]
        units = [(q_ref[:, at], k_ref[:, at], v_ref[:, at].astype(f32), None) for at in places]
        low = low_lanes(TOK)
        for at, (mixed, total, tops) in zip(places, attend_pairs(units)):
            mixed_ref[:, at] = mixed
            total_ref[:, at] = total
            top_ref[:, at] = jnp.where(low, tops[0], tops[1])


def own_attend(queries, keys, values):
    out = pltpu.HBM((TOK, WIDTH), f32)
    return pl.pallas_call(
        own_kernel,
        out_shape=(out, out, out),
        in_specs=[WHOLE, WHOLE, WHOLE],
        out_specs=(WHOLE, WHOLE, WHOLE),
        compiler_params=params(VMEM),
        cost_estimate=cost(8 * TOK * TOK * WIDTH, 30 * TOK * WIDTH, HEADS * TOK * TOK),
        name="own_attend",
    )(in_hbm(queries), in_hbm(keys), in_hbm(values))


def choose_kernel(key_list_ref, slab_ref, after_ref, out_hbm, out_ref, sems):
    del after_ref
    copies = []
    halves = [
        jnp.concatenate([slab_ref[key_list_ref[s], at : at + 16, :] for s in range(KEYS)], axis=0)
        for at in (0, 16)
    ]
    keys = jnp.concatenate(halves, axis=1)
    row = lax.broadcasted_iota(jnp.int32, (16, LANES), 0)
    col = lax.broadcasted_iota(jnp.int32, (16, LANES), 1)
    slot = jnp.where(col % 16 == row, col // 16, -1).astype(f32)
    for f in range(0, FRAMES, 8):
        picks = []
        for more in range(8):
            spare = slab_ref[f + more, 16:32, :].astype(f32)
            for which in range(2):
                wanted = spare[14 + which : 15 + which, :]
                picks.append(jnp.where(slot == wanted, 1.0, 0.0).astype(bf16))
        chosen = jnp.dot(jnp.concatenate(picks, axis=0), keys, preferred_element_type=f32)
        chosen = chosen.astype(bf16).reshape(8, 2, 16, 2 * LANES)
        out_ref[f : f + 8, :, 0:16, :] = chosen[..., :LANES]
        out_ref[f : f + 8, :, 16:32, :] = chosen[..., LANES:]
        if (f + 8) % 32 == 0:
            some = pl.ds(f - 24, 32)
            copies.append(
                pltpu.make_async_copy(out_ref.at[some], out_hbm.at[some], sems.at[len(copies)])
            )
            copies[-1].start()
    for copy in copies:
        copy.wait()


def choose(key_list, slab, after):
    return pl.pallas_call(
        choose_kernel,
        out_shape=pltpu.HBM((FRAMES, 2, SLAB, LANES), bf16),
        in_specs=[SMALL, WHOLE, THERE],
        out_specs=THERE,
        scratch_shapes=[
            pltpu.VMEM((FRAMES, 2, SLAB, LANES), bf16),
            pltpu.SemaphoreType.DMA((4,)),
        ],
        compiler_params=params(VMEM),
        cost_estimate=cost(4 * FRAMES * SLAB * LANES * 256, 6 * FRAMES * SLAB * LANES),
        name="choose",
    )(key_list, in_vmem(slab), in_hbm(after))


LARGE = 1e30


def attend_kernel(
    slab_ref, q_hbm, mixed_hbm, total_hbm, top_hbm, weight_hbm, wo_hbm, video_hbm,
    spatial_hbm, out_slab_hbm,
    spatial_ref, out_slab_ref, rows_ref, heads_ref, most_ref, q_ref, mixed_ref, total_ref, top_ref, wk_ref, wv_ref,
    wo_ref, video_ref, sems, last_sems, out_sems,
):
    def copies(group):
        pairs = (
            (weight_hbm.at[:, group_lanes(group, GROUP, WIDTH)], wk_ref),
            (weight_hbm.at[:, group_lanes(group, GROUP, 2 * WIDTH)], wv_ref),
            (q_hbm.at[:, group_lanes(group, GROUP)], q_ref),
            (top_hbm.at[:, group_lanes(group, GROUP)], top_ref),
            (mixed_hbm.at[:, group_lanes(group, GROUP)], mixed_ref),
            (total_hbm.at[:, group_lanes(group, GROUP)], total_ref),
        )
        return [
            pltpu.make_async_copy(source, target.at[group], sems.at[i, group])
            for i, (source, target) in enumerate(pairs)
        ]

    last = (
        pltpu.make_async_copy(wo_hbm, wo_ref, last_sems.at[0]),
        pltpu.make_async_copy(video_hbm, video_ref, last_sems.at[1]),
    )
    for group in range(GROUPS):
        for copy in copies(group):
            copy.start()
    for copy in last:
        copy.start()

    swap = swap_matrix()
    for which in range(2):
        slab_to_rows(
            lambda block, half: slab_ref[
                16 * block : 16 * block + 16, which, 16 * half : 16 * half + 16, :
            ],
            rows_ref, swap, which * TOK,
        )
    most_ref[...] = jnp.zeros_like(most_ref)

    def project_group(group):
        rows = rows_ref[...]
        keys = jnp.dot(rows, wk_ref[group], preferred_element_type=f32).astype(bf16)
        return keys, jnp.dot(rows, wv_ref[group], preferred_element_type=f32)

    @pl.loop(0, GROUPS)
    def _(group):
        arriving = copies(group)
        for copy in arriving[:2]:
            copy.wait()
        keys, values = project_group(group)
        for copy in arriving[2:]:
            copy.wait()
        low_q, low_v = low_lanes(TOK), low_lanes(2 * TOK)
        pending = []
        for pair in range(2):
            lanes = slice(pair * LANES, (pair + 1) * LANES)
            queries = q_ref[group, :, lanes].astype(f32)
            some = values[:, lanes]
            top = top_ref[group, :, lanes]
            other = pltpu.roll(top, HEAD, 1)
            for head in range(2):
                if head == 0:
                    mine, padded = jnp.where(low_q, queries, 0.0), jnp.where(low_v, some, 1.0)
                    wide = jnp.where(low_q, top, other)
                else:
                    mine, padded = jnp.where(low_q, 0.0, queries), jnp.where(low_v, 1.0, some)
                    wide = jnp.where(low_q, other, top)
                scores = lax.dot_general(
                    mine.astype(bf16), keys[:, lanes], (((1,), (1,)), ((), ())),
                    preferred_element_type=f32,
                )
                tops = jnp.concatenate([wide] * (2 * TOK // LANES), axis=1)
                pending.append((scores, tops, padded.astype(bf16)))
        pending = [(jnp.exp2(s - tops).astype(bf16), padded) for s, tops, padded in pending]
        outs = [jnp.dot(w, padded, preferred_element_type=f32) for w, padded in pending]
        for pair in range(2):
            lanes = slice(pair * LANES, (pair + 1) * LANES)
            one, two = outs[2 * pair], outs[2 * pair + 1]
            mixed = jnp.where(low_q, one, two) + mixed_ref[group, :, lanes]
            total = jnp.where(low_q, two, one)
            total = pltpu.roll(total, HEAD, 1) + total_ref[group, :, lanes]
            heads_ref[2 * group + pair] = (mixed / total).astype(bf16)
            most = jnp.max(total.reshape(TOK // 8, 8, LANES), axis=0)
            most_ref[...] = jnp.maximum(most_ref[...], most)

    @pl.when(jnp.logical_not(jnp.max(most_ref[...]) < LARGE))
    def _():
        @pl.loop(0, GROUPS)
        def _(group):
            keys, values = project_group(group)
            for pair in range(2):
                lanes = slice(pair * LANES, (pair + 1) * LANES)
                top = top_ref[group, :, lanes]
                ((mixed, total, tops),) = attend_pairs(
                    [(q_ref[group, :, lanes], keys[:, lanes], values[:, lanes], top)]
                )
                less = jnp.exp2(top - jnp.where(low_lanes(TOK), tops[0], tops[1]))
                mixed = mixed + mixed_ref[group, :, lanes] * less
                total = total + total_ref[group, :, lanes] * less
                heads_ref[2 * group + pair] = (mixed / total).astype(bf16)

    given = []

    def give(source, target):
        given.append(pltpu.make_async_copy(source, target, out_sems.at[len(given)]))
        given[-1].start()

    for copy in last:
        copy.wait()
    for k in range(PARTS):
        rows = pl.ds(k * FRAMES, FRAMES)
        heads = jnp.concatenate([heads_ref[c, rows, :] for c in range(COLS)], axis=1)
        added = jnp.dot(heads, wo_ref[...], preferred_element_type=f32)
        spatial_ref[rows, :] = (video_ref[rows, :].astype(f32) + added).astype(bf16)
        give(spatial_ref.at[rows], spatial_hbm.at[rows])
        if k == 1:
            rows_to_slab(tiles_of(spatial_ref), out_slab_ref, swap, halves=(0,))
            give(out_slab_ref.at[:, pl.ds(0, 16)], out_slab_hbm.at[:, pl.ds(0, 16)])
    rows_to_slab(tiles_of(spatial_ref), out_slab_ref, swap, halves=(1,))
    give(out_slab_ref.at[:, pl.ds(16, 16)], out_slab_hbm.at[:, pl.ds(16, 16)])
    for copy in given:
        copy.wait()


def attend(slab, queries, mixed, total, top, weight, out_weight, video):
    return pl.pallas_call(
        attend_kernel,
        out_shape=(
            jax.ShapeDtypeStruct((TOK, WIDTH), bf16),
            pltpu.HBM((FRAMES, SLAB, LANES), bf16),
        ),
        in_specs=[WHOLE] + [THERE] * 7,
        out_specs=(THERE, THERE),
        scratch_shapes=[
            pltpu.VMEM((TOK, WIDTH), bf16),
            pltpu.VMEM((FRAMES, SLAB, LANES), bf16),
            pltpu.VMEM((2 * TOK, WIDTH), bf16),
            pltpu.VMEM((COLS, TOK, LANES), bf16),
            pltpu.VMEM((8, LANES), f32),
            pltpu.VMEM((GROUPS, TOK, GROUP), bf16),
            pltpu.VMEM((GROUPS, TOK, GROUP), f32),
            pltpu.VMEM((GROUPS, TOK, GROUP), f32),
            pltpu.VMEM((GROUPS, TOK, GROUP), f32),
            pltpu.VMEM((GROUPS, WIDTH, GROUP), bf16),
            pltpu.VMEM((GROUPS, WIDTH, GROUP), bf16),
            pltpu.VMEM((WIDTH, WIDTH), bf16),
            pltpu.VMEM((TOK, WIDTH), bf16),
            pltpu.SemaphoreType.DMA((6, GROUPS)),
            pltpu.SemaphoreType.DMA((2,)),
            pltpu.SemaphoreType.DMA((PARTS + 2,)),
        ],
        compiler_params=params(VMEM),
        cost_estimate=cost(
            8 * TOK * WIDTH * WIDTH + 16 * TOK * TOK * WIDTH,
            6 * WIDTH * WIDTH + 20 * TOK * WIDTH,
            2 * HEADS * TOK * TOK,
        ),
        name="attend",
    )(
        in_vmem(slab), in_hbm(queries), in_hbm(mixed), in_hbm(total), in_hbm(top),
        in_hbm(weight), in_hbm(out_weight), in_hbm(video),
    )


def time_kernel(
    slab_ref, gain_ref, weight_hbm, out_slab_ref, rows_ref, heads_ref, weight_ref, sems
):
    def copies(group):
        return [
            pltpu.make_async_copy(
                weight_hbm.at[:, group_lanes(group, GROUP, which * WIDTH)],
                weight_ref.at[which, group],
                sems.at[which, group],
            )
            for which in range(3)
        ]

    for group in range(GROUPS):
        for copy in copies(group):
            copy.start()
    swap = swap_matrix()
    slab_to_rows(
        lambda block, half: slab_ref[16 * block : 16 * block + 16, 16 * half : 16 * half + 16, :],
        rows_ref, swap,
    )
    for k in range(PARTS):
        rows = pl.ds(k * FRAMES, FRAMES)
        rows_ref[rows, :] = norm_rows(rows_ref[rows, :].astype(f32), gain_ref[...].reshape(1, WIDTH))

    @pl.loop(0, GROUPS)
    def _(group):
        for copy in copies(group):
            copy.wait()
        rows = rows_ref[...]
        made = [
            jnp.dot(rows, weight_ref[which, group], preferred_element_type=f32)
            for which in range(3)
        ]
        queries, keys, values = (made[0] * SCALE).astype(bf16), made[1].astype(bf16), made[2]
        units, places = [], []
        for pair in range(2):
            lanes = slice(pair * LANES, (pair + 1) * LANES)
            for k in range(PARTS):
                at = slice(k * FRAMES, (k + 1) * FRAMES)
                units.append((queries[at, lanes], keys[at, lanes], values[at, lanes], None))
                places.append((pair, at))
        for (pair, at), (mixed, total, _) in zip(places, attend_pairs(units)):
            heads_ref[2 * group + pair, at, :] = (mixed / total).astype(bf16)

    rows_to_slab(lambda at, g: heads_ref[g, at : at + 16, :], out_slab_ref, swap)


def time_attend(slab, gain, weight):
    return pl.pallas_call(
        time_kernel,
        out_shape=jax.ShapeDtypeStruct((FRAMES, SLAB, LANES), bf16),
        in_specs=[WHOLE, WHOLE, THERE],
        out_specs=WHOLE,
        scratch_shapes=[
            pltpu.VMEM((TOK, WIDTH), bf16),
            pltpu.VMEM((COLS, TOK, LANES), bf16),
            pltpu.VMEM((3, GROUPS, WIDTH, GROUP), bf16),
            pltpu.SemaphoreType.DMA((3, GROUPS)),
        ],
        compiler_params=params(VMEM),
        cost_estimate=cost(
            6 * TOK * WIDTH * WIDTH + 8 * TOK * FRAMES * WIDTH,
            6 * WIDTH * WIDTH + 4 * TOK * WIDTH,
            HEADS * TOK * FRAMES,
        ),
        name="time_attend",
    )(in_vmem(slab), gain, in_hbm(weight))


def unpack_kernel(slab_ref, out_hbm, out_ref, sems):
    swap = swap_matrix()
    copies = []
    for part in range(4):
        slab_to_rows(
            lambda block, half: slab_ref[
                16 * block : 16 * block + 16, 16 * half : 16 * half + 16, :
            ],
            out_ref, swap, blocks=(2 * part, 2 * part + 1),
        )
        for k in range(PARTS):
            some = pl.ds(k * FRAMES + 32 * part, 32)
            copies.append(
                pltpu.make_async_copy(out_ref.at[some], out_hbm.at[some], sems.at[len(copies)])
            )
            copies[-1].start()
    for copy in copies:
        copy.wait()


def unpack(slab):
    return pl.pallas_call(
        unpack_kernel,
        out_shape=jax.ShapeDtypeStruct((TOK, WIDTH), bf16),
        in_specs=[WHOLE],
        out_specs=THERE,
        scratch_shapes=[pltpu.VMEM((TOK, WIDTH), bf16), pltpu.SemaphoreType.DMA((4 * PARTS,))],
        compiler_params=params(VMEM),
        cost_estimate=cost(2 * TOK * WIDTH * 256, 4 * TOK * WIDTH),
        name="unpack",
    )(in_vmem(slab))


def exchange(slab):
    return lax.all_to_all(slab, "frame", split_axis=0, concat_axis=0, tiled=True)


def body(video, key_list, pairs, norm_gain, qkv_weight, out_weight, time_gain, time_weight):
    spread = exchange(prep(pairs, video, norm_gain))
    queries, keys, values = project(video, norm_gain, qkv_weight)
    wanted = exchange(choose(key_list, spread, queries))
    mixed, total, top = own_attend(queries, keys, values)
    spatial, slab = attend(wanted, queries, mixed, total, top, qkv_weight, out_weight, video)
    slab = time_attend(exchange(slab), time_gain, time_weight)
    return spatial, unpack(exchange(slab))


def solution(mesh):
    return jax.shard_map(
        body,
        mesh=mesh,
        in_specs=(P("frame", None), P(), P("frame", None), P(), P(), P(), P(), P()),
        out_specs=(P("frame", None), P("frame", None)),
        check_vma=False,
    )
```

```python
import jax
import jax.numpy as jnp
from jax import lax
from jax.experimental import pallas as pl
from jax.experimental.pallas import tpu as pltpu
from jax.sharding import PartitionSpec as P

WIDTH = 1280
HEADS = 20
HEAD = 64
TOK = 384
FRAMES = 128
KEYS = 8
PARTS = TOK // FRAMES
LANES = 128
COLS = WIDTH // LANES
SLAB = 32
GROUP = 256
GROUPS = WIDTH // GROUP
VMEM = 52
SCALE = 0.125 * 1.4426950408889634

bf16 = jnp.bfloat16
f32 = jnp.float32


def params(mib, **more):
    return pltpu.CompilerParams(vmem_limit_bytes=mib << 20, **more)


def cost(flops, moved, exps=0):
    return pl.CostEstimate(flops=int(flops), bytes_accessed=int(moved), transcendentals=int(exps))


def in_vmem(x):
    return pltpu.with_memory_space_constraint(x, pltpu.VMEM)


def in_hbm(x):
    return pltpu.with_memory_space_constraint(x, pltpu.HBM)


WHOLE = pl.BlockSpec(memory_space=pltpu.VMEM)
THERE = pl.BlockSpec(memory_space=pl.ANY)
SMALL = pl.BlockSpec(memory_space=pltpu.SMEM)


def norm_rows(values, gain):
    centred = values - jnp.mean(values, axis=-1, keepdims=True)
    spread = jnp.mean(centred * centred, axis=-1, keepdims=True)
    return (centred * lax.rsqrt(spread + 1e-05) * gain).astype(bf16)


def swap_matrix():
    row = lax.broadcasted_iota(jnp.int32, (256, 256), 0)
    col = lax.broadcasted_iota(jnp.int32, (256, 256), 1)
    return jnp.where(col == (row % 16) * 16 + row // 16, 1.0, 0.0).astype(bf16)


def rows_to_slab(tile, slab_ref, swap, spare=None, halves=(0, 1)):
    for half in halves:
        for pair in range(4):
            sides = []
            for block in (2 * pair, 2 * pair + 1):
                tiles = []
                for unit in range(16 * half, 16 * half + 16):
                    k, g = divmod(unit, COLS)
                    if k < PARTS:
                        tiles.append(tile(k * FRAMES + 16 * block, g))
                    elif spare is None:
                        tiles.append(jnp.zeros((16, LANES), bf16))
                    else:
                        tiles.append(spare[unit - PARTS * COLS])
                sides.append(jnp.concatenate(tiles, axis=0))
            both = jnp.concatenate(sides, axis=1)
            moved = jnp.dot(swap, both, preferred_element_type=f32).astype(bf16)
            for side in range(2):
                block = 2 * pair + side
                slab_ref[16 * block : 16 * block + 16, 16 * half : 16 * half + 16, :] = moved[
                    :, side * LANES : (side + 1) * LANES
                ].reshape(16, 16, LANES)


def tiles_of(rows_ref):
    return lambda at, g: rows_ref[at : at + 16, g * LANES : (g + 1) * LANES]


def slab_to_rows(load, rows_ref, swap, first=0, blocks=range(8)):
    for block in blocks:
        both = jnp.concatenate(
            [load(block, half).reshape(256, LANES) for half in range(2)], axis=1
        )
        moved = jnp.dot(swap, both, preferred_element_type=f32).astype(bf16)
        for unit in range(PARTS * COLS):
            half, row = divmod(unit, 16)
            k, g = divmod(unit, COLS)
            at = first + k * FRAMES + 16 * block
            rows_ref[at : at + 16, g * LANES : (g + 1) * LANES] = moved[
                16 * row : 16 * row + 16, half * LANES : (half + 1) * LANES
            ]


def prep_kernel(
    pairs_hbm, video_hbm, gain_hbm, slab_hbm,
    pairs_ref, video_ref, gain_ref, normed_ref, slab_ref, sems, out_sems,
):
    small = (
        pltpu.make_async_copy(gain_hbm, gain_ref, sems.at[PARTS]),
        pltpu.make_async_copy(pairs_hbm, pairs_ref, sems.at[PARTS + 1]),
    )
    arriving = []
    for part in range(PARTS):
        rows = pl.ds(part * FRAMES, FRAMES)
        arriving.append(
            pltpu.make_async_copy(video_hbm.at[rows], video_ref.at[rows], sems.at[part])
        )
    for copy in (small[0], arriving[0], small[1], *arriving[1:]):
        copy.start()
    swap = swap_matrix()
    leaving = []

    def give(half, spare=None):
        rows_to_slab(tiles_of(normed_ref), slab_ref, swap, spare, halves=(half,))
        some = pl.ds(16 * half, 16)
        leaving.append(
            pltpu.make_async_copy(slab_ref.at[:, some], slab_hbm.at[:, some], out_sems.at[half])
        )
        leaving[-1].start()

    small[0].wait()
    gain = gain_ref[...].reshape(1, WIDTH)
    for part, copy in enumerate(arriving):
        copy.wait()
        rows = pl.ds(part * FRAMES, FRAMES)
        normed_ref[rows, :] = norm_rows(video_ref[rows, :].astype(f32), gain)
        if part == 1:
            give(0)
    small[1].wait()
    spare = [
        jnp.full((16, LANES), pairs_ref[0, which], jnp.int32).astype(f32).astype(bf16)
        for which in range(2)
    ]
    give(1, spare)
    for copy in leaving:
        copy.wait()


def prep(pairs, video, gain):
    return pl.pallas_call(
        prep_kernel,
        out_shape=pltpu.HBM((FRAMES, SLAB, LANES), bf16),
        in_specs=[THERE, THERE, THERE],
        out_specs=THERE,
        scratch_shapes=[
            pltpu.SMEM((1, 2), jnp.int32),
            pltpu.VMEM((TOK, WIDTH), bf16),
            pltpu.VMEM((WIDTH,), f32),
            pltpu.VMEM((TOK, WIDTH), bf16),
            pltpu.VMEM((FRAMES, SLAB, LANES), bf16),
            pltpu.SemaphoreType.DMA((PARTS + 2,)),
            pltpu.SemaphoreType.DMA((2,)),
        ],
        compiler_params=params(VMEM),
        cost_estimate=cost(6 * TOK * WIDTH, 4 * TOK * WIDTH),
        name="prep",
    )(in_hbm(pairs), in_hbm(video), in_hbm(gain))


def project_kernel(video_ref, gain_ref, wq_ref, wk_ref, wv_ref, q_ref, k_ref, v_ref, normed_ref):
    @pl.when(pl.program_id(0) == 0)
    def _():
        gain = gain_ref[...].reshape(1, WIDTH)
        normed_ref[...] = norm_rows(video_ref[...].astype(f32), gain)

    rows = normed_ref[...]
    queries = jnp.dot(rows, wq_ref[...], preferred_element_type=f32) * SCALE
    q_ref[...] = queries.astype(bf16)
    k_ref[...] = jnp.dot(rows, wk_ref[...], preferred_element_type=f32).astype(bf16)
    v_ref[...] = jnp.dot(rows, wv_ref[...], preferred_element_type=f32).astype(bf16)


def project(video, gain, weight):
    out = pltpu.HBM((TOK, WIDTH), bf16)
    out_spec = pl.BlockSpec((TOK, GROUP), lambda i: (0, i))
    return pl.pallas_call(
        project_kernel,
        grid=(GROUPS,),
        out_shape=(out, out, out),
        in_specs=[
            WHOLE,
            WHOLE,
            pl.BlockSpec((WIDTH, GROUP), lambda i: (0, i)),
            pl.BlockSpec((WIDTH, GROUP), lambda i: (0, GROUPS + i)),
            pl.BlockSpec((WIDTH, GROUP), lambda i: (0, 2 * GROUPS + i)),
        ],
        out_specs=(out_spec, out_spec, out_spec),
        scratch_shapes=[pltpu.VMEM((TOK, WIDTH), bf16)],
        compiler_params=params(VMEM),
        cost_estimate=cost(6 * TOK * WIDTH * WIDTH, 6 * WIDTH * WIDTH + 8 * TOK * WIDTH),
        name="project",
    )(in_hbm(video), in_hbm(gain), in_hbm(weight), in_hbm(weight), in_hbm(weight))


def low_lanes(rows):
    return lax.broadcasted_iota(jnp.int32, (rows, LANES), 1) < HEAD


def attend_pairs(units):
    scores, padded = [], []
    for queries, keys, values, _ in units:
        low_q, low_v = low_lanes(queries.shape[0]), low_lanes(values.shape[0])
        wide = queries.astype(f32)
        for head in range(2):
            mine = jnp.where(low_q, wide, 0.0) if head == 0 else jnp.where(low_q, 0.0, wide)
            rest = jnp.where(low_v, values, 1.0) if head == 0 else jnp.where(low_v, 1.0, values)
            padded.append(rest.astype(bf16))
            scores.append(
                lax.dot_general(
                    mine.astype(bf16), keys, (((1,), (1,)), ((), ())), preferred_element_type=f32
                )
            )
    tops = [jnp.max(s, axis=-1, keepdims=True) for s in scores]
    for i, (_, _, _, top) in enumerate(units):
        if top is not None:
            for head in range(2):
                other = top[:, head * HEAD : head * HEAD + 1]
                tops[2 * i + head] = jnp.maximum(tops[2 * i + head], other)
    weights = [jnp.exp2(s - top).astype(bf16) for s, top in zip(scores, tops)]
    outs = [jnp.dot(w, v, preferred_element_type=f32) for w, v in zip(weights, padded)]
    given = []
    for i, (queries, _, _, _) in enumerate(units):
        low = low_lanes(queries.shape[0])
        one, two = outs[2 * i], outs[2 * i + 1]
        total = pltpu.roll(jnp.where(low, two, one), HEAD, 1)
        given.append((jnp.where(low, one, two), total, tops[2 * i : 2 * i + 2]))
    return given


def group_lanes(group, size, offset=0):
    return pl.ds(pl.multiple_of(offset + group * GROUP, LANES), size)


def flipped_scores(queries, keys, head):
    low = low_lanes(queries.shape[0])
    wide = queries.astype(f32)
    mine = jnp.where(low, wide, 0.0) if head == 0 else jnp.where(low, 0.0, wide)
    return lax.dot_general(
        keys, mine.astype(bf16), (((1,), (1,)), ((), ())), preferred_element_type=f32
    )


def with_ones(values):
    return jnp.concatenate([values, jnp.ones((16, values.shape[1]), bf16)], axis=0)


def own_kernel(q_ref, k_ref, v_ref, mixed_ref, stat_ref):
    @pl.loop(0, GROUPS)
    def _(group):
        at = group_lanes(group, GROUP)
        queries, keys = q_ref[:, at], k_ref[:, at]
        values = v_ref[:, at].T
        scores = []
        for head in range(4):
            lanes = slice(head // 2 * LANES, (head // 2 + 1) * LANES)
            scores.append(flipped_scores(queries[:, lanes], keys[:, lanes], head % 2))
        tops = [jnp.max(s, axis=0, keepdims=True) for s in scores]
        weights = [jnp.exp2(s - top).astype(bf16) for s, top in zip(scores, tops)]
        for head in range(4):
            rows = slice(head * HEAD, (head + 1) * HEAD)
            out = jnp.dot(with_ones(values[rows]), weights[head], preferred_element_type=f32)
            mixed_ref[group, rows, :] = out[:HEAD]
            stat_ref[group, head : head + 1, :] = tops[head]
            stat_ref[group, 4 + head : 5 + head, :] = out[HEAD : HEAD + 1]


def own_attend(queries, keys, values):
    return pl.pallas_call(
        own_kernel,
        out_shape=(pltpu.HBM((GROUPS, GROUP, TOK), f32), pltpu.HBM((GROUPS, 8, TOK), f32)),
        in_specs=[WHOLE, WHOLE, WHOLE],
        out_specs=(WHOLE, WHOLE),
        compiler_params=params(VMEM),
        cost_estimate=cost(8 * TOK * TOK * WIDTH, 10 * TOK * WIDTH, HEADS * TOK * TOK),
        name="own_attend",
    )(in_hbm(queries), in_hbm(keys), in_hbm(values))


def choose_kernel(key_list_ref, slab_ref, after_ref, out_hbm, out_ref, sems):
    del after_ref
    copies = []
    halves = [
        jnp.concatenate([slab_ref[key_list_ref[s], at : at + 16, :] for s in range(KEYS)], axis=0)
        for at in (0, 16)
    ]
    keys = jnp.concatenate(halves, axis=1)
    row = lax.broadcasted_iota(jnp.int32, (16, LANES), 0)
    col = lax.broadcasted_iota(jnp.int32, (16, LANES), 1)
    slot = jnp.where(col % 16 == row, col // 16, -1).astype(f32)
    for f in range(0, FRAMES, 8):
        picks = []
        for more in range(8):
            spare = slab_ref[f + more, 16:32, :].astype(f32)
            for which in range(2):
                wanted = spare[14 + which : 15 + which, :]
                picks.append(jnp.where(slot == wanted, 1.0, 0.0).astype(bf16))
        chosen = jnp.dot(jnp.concatenate(picks, axis=0), keys, preferred_element_type=f32)
        chosen = chosen.astype(bf16).reshape(8, 2, 16, 2 * LANES)
        out_ref[f : f + 8, :, 0:16, :] = chosen[..., :LANES]
        out_ref[f : f + 8, :, 16:32, :] = chosen[..., LANES:]
        if (f + 8) % 32 == 0:
            some = pl.ds(f - 24, 32)
            copies.append(
                pltpu.make_async_copy(out_ref.at[some], out_hbm.at[some], sems.at[len(copies)])
            )
            copies[-1].start()
    for copy in copies:
        copy.wait()


def choose(key_list, slab, after):
    return pl.pallas_call(
        choose_kernel,
        out_shape=pltpu.HBM((FRAMES, 2, SLAB, LANES), bf16),
        in_specs=[SMALL, WHOLE, THERE],
        out_specs=THERE,
        scratch_shapes=[
            pltpu.VMEM((FRAMES, 2, SLAB, LANES), bf16),
            pltpu.SemaphoreType.DMA((4,)),
        ],
        compiler_params=params(VMEM),
        cost_estimate=cost(4 * FRAMES * SLAB * LANES * 256, 6 * FRAMES * SLAB * LANES),
        name="choose",
    )(key_list, in_vmem(slab), in_hbm(after))


LARGE = 1e30


def attend_kernel(
    slab_ref, q_hbm, mixed_hbm, stat_hbm, weight_hbm, wo_hbm, video_hbm,
    spatial_hbm, out_slab_hbm,
    spatial_ref, out_slab_ref, rows_ref, heads_ref, most_ref, q_ref, mixed_ref, stat_ref,
    wk_ref, wv_ref, wo_ref, video_ref, sems, last_sems, out_sems,
):
    def copies(group):
        pairs = (
            (weight_hbm.at[:, group_lanes(group, GROUP, WIDTH)], wk_ref),
            (weight_hbm.at[:, group_lanes(group, GROUP, 2 * WIDTH)], wv_ref),
            (q_hbm.at[:, group_lanes(group, GROUP)], q_ref),
            (mixed_hbm.at[group], mixed_ref),
            (stat_hbm.at[group], stat_ref),
        )
        return [
            pltpu.make_async_copy(source, target.at[group], sems.at[i, group])
            for i, (source, target) in enumerate(pairs)
        ]

    last = (
        pltpu.make_async_copy(wo_hbm, wo_ref, last_sems.at[0]),
        pltpu.make_async_copy(video_hbm, video_ref, last_sems.at[1]),
    )
    for group in range(GROUPS):
        for copy in copies(group):
            copy.start()
    for copy in last:
        copy.start()

    swap = swap_matrix()
    for which in range(2):
        slab_to_rows(
            lambda block, half: slab_ref[
                16 * block : 16 * block + 16, which, 16 * half : 16 * half + 16, :
            ],
            rows_ref, swap, which * TOK,
        )
    most_ref[...] = jnp.zeros_like(most_ref)

    def project_group(group):
        rows = rows_ref[...]
        keys = jnp.dot(rows, wk_ref[group], preferred_element_type=f32).astype(bf16)
        values = jnp.dot(rows, wv_ref[group], preferred_element_type=f32).astype(bf16)
        return keys, values.T

    def score_group(group, keys):
        scores = []
        for head in range(4):
            lanes = slice(head // 2 * LANES, (head // 2 + 1) * LANES)
            scores.append(flipped_scores(q_ref[group, :, lanes], keys[:, lanes], head % 2))
        return scores

    def mix_group(group, weights, values, less):
        made, totals = [], []
        for head in range(4):
            rows = slice(head * HEAD, (head + 1) * HEAD)
            out = jnp.dot(with_ones(values[rows]), weights[head], preferred_element_type=f32)
            mixed, total = mixed_ref[group, rows, :], stat_ref[group, 4 + head : 5 + head, :]
            if less is not None:
                mixed, total = mixed * less[head], total * less[head]
            mixed, total = mixed + out[:HEAD], total + out[HEAD : HEAD + 1]
            made.append((mixed / total).astype(bf16))
            totals.append(total)
        heads_ref[group] = jnp.concatenate(made, axis=0).T
        return totals

    @pl.loop(0, GROUPS)
    def _(group):
        arriving = copies(group)
        for copy in arriving[:2]:
            copy.wait()
        keys, values = project_group(group)
        for copy in arriving[2:]:
            copy.wait()
        scores = score_group(group, keys)
        weights = [
            jnp.exp2(scores[head] - stat_ref[group, head : head + 1, :]).astype(bf16)
            for head in range(4)
        ]
        for total in mix_group(group, weights, values, None):
            most_ref[...] = jnp.maximum(most_ref[...], total)

    @pl.when(jnp.logical_not(jnp.max(most_ref[...]) < LARGE))
    def _():
        @pl.loop(0, GROUPS)
        def _(group):
            keys, values = project_group(group)
            scores = score_group(group, keys)
            own = [stat_ref[group, head : head + 1, :] for head in range(4)]
            tops = [
                jnp.maximum(top, jnp.max(s, axis=0, keepdims=True)) for s, top in zip(scores, own)
            ]
            weights = [jnp.exp2(s - top).astype(bf16) for s, top in zip(scores, tops)]
            mix_group(group, weights, values, [jnp.exp2(o - top) for o, top in zip(own, tops)])

    given = []

    def give(source, target):
        given.append(pltpu.make_async_copy(source, target, out_sems.at[len(given)]))
        given[-1].start()

    for copy in last:
        copy.wait()
    for k in range(PARTS):
        rows = pl.ds(k * FRAMES, FRAMES)
        heads = jnp.concatenate([heads_ref[g, rows, :] for g in range(GROUPS)], axis=1)
        added = jnp.dot(heads, wo_ref[...], preferred_element_type=f32)
        spatial_ref[rows, :] = (video_ref[rows, :].astype(f32) + added).astype(bf16)
        give(spatial_ref.at[rows], spatial_hbm.at[rows])
        if k == 1:
            rows_to_slab(tiles_of(spatial_ref), out_slab_ref, swap, halves=(0,))
            give(out_slab_ref.at[:, pl.ds(0, 16)], out_slab_hbm.at[:, pl.ds(0, 16)])
    rows_to_slab(tiles_of(spatial_ref), out_slab_ref, swap, halves=(1,))
    give(out_slab_ref.at[:, pl.ds(16, 16)], out_slab_hbm.at[:, pl.ds(16, 16)])
    for copy in given:
        copy.wait()


def attend(slab, queries, mixed, stat, weight, out_weight, video):
    return pl.pallas_call(
        attend_kernel,
        out_shape=(
            jax.ShapeDtypeStruct((TOK, WIDTH), bf16),
            pltpu.HBM((FRAMES, SLAB, LANES), bf16),
        ),
        in_specs=[WHOLE] + [THERE] * 6,
        out_specs=(THERE, THERE),
        scratch_shapes=[
            pltpu.VMEM((TOK, WIDTH), bf16),
            pltpu.VMEM((FRAMES, SLAB, LANES), bf16),
            pltpu.VMEM((2 * TOK, WIDTH), bf16),
            pltpu.VMEM((GROUPS, TOK, GROUP), bf16),
            pltpu.VMEM((1, TOK), f32),
            pltpu.VMEM((GROUPS, TOK, GROUP), bf16),
            pltpu.VMEM((GROUPS, GROUP, TOK), f32),
            pltpu.VMEM((GROUPS, 8, TOK), f32),
            pltpu.VMEM((GROUPS, WIDTH, GROUP), bf16),
            pltpu.VMEM((GROUPS, WIDTH, GROUP), bf16),
            pltpu.VMEM((WIDTH, WIDTH), bf16),
            pltpu.VMEM((TOK, WIDTH), bf16),
            pltpu.SemaphoreType.DMA((5, GROUPS)),
            pltpu.SemaphoreType.DMA((2,)),
            pltpu.SemaphoreType.DMA((PARTS + 2,)),
        ],
        compiler_params=params(VMEM),
        cost_estimate=cost(
            8 * TOK * WIDTH * WIDTH + 16 * TOK * TOK * WIDTH,
            6 * WIDTH * WIDTH + 20 * TOK * WIDTH,
            2 * HEADS * TOK * TOK,
        ),
        name="attend",
    )(
        in_vmem(slab), in_hbm(queries), in_hbm(mixed), in_hbm(stat),
        in_hbm(weight), in_hbm(out_weight), in_hbm(video),
    )


def time_kernel(
    slab_ref, gain_ref, weight_hbm, out_slab_ref, rows_ref, heads_ref, weight_ref, sems
):
    def copies(group):
        return [
            pltpu.make_async_copy(
                weight_hbm.at[:, group_lanes(group, GROUP, which * WIDTH)],
                weight_ref.at[which, group],
                sems.at[which, group],
            )
            for which in range(3)
        ]

    for group in range(GROUPS):
        for copy in copies(group):
            copy.start()
    swap = swap_matrix()
    slab_to_rows(
        lambda block, half: slab_ref[16 * block : 16 * block + 16, 16 * half : 16 * half + 16, :],
        rows_ref, swap,
    )
    for k in range(PARTS):
        rows = pl.ds(k * FRAMES, FRAMES)
        rows_ref[rows, :] = norm_rows(rows_ref[rows, :].astype(f32), gain_ref[...].reshape(1, WIDTH))

    @pl.loop(0, GROUPS)
    def _(group):
        for copy in copies(group):
            copy.wait()
        rows = rows_ref[...]
        made = [
            jnp.dot(rows, weight_ref[which, group], preferred_element_type=f32)
            for which in range(3)
        ]
        queries, keys, values = (made[0] * SCALE).astype(bf16), made[1].astype(bf16), made[2]
        units, places = [], []
        for pair in range(2):
            lanes = slice(pair * LANES, (pair + 1) * LANES)
            for k in range(PARTS):
                at = slice(k * FRAMES, (k + 1) * FRAMES)
                units.append((queries[at, lanes], keys[at, lanes], values[at, lanes], None))
                places.append((pair, at))
        for (pair, at), (mixed, total, _) in zip(places, attend_pairs(units)):
            heads_ref[2 * group + pair, at, :] = (mixed / total).astype(bf16)

    rows_to_slab(lambda at, g: heads_ref[g, at : at + 16, :], out_slab_ref, swap)


def time_attend(slab, gain, weight):
    return pl.pallas_call(
        time_kernel,
        out_shape=jax.ShapeDtypeStruct((FRAMES, SLAB, LANES), bf16),
        in_specs=[WHOLE, WHOLE, THERE],
        out_specs=WHOLE,
        scratch_shapes=[
            pltpu.VMEM((TOK, WIDTH), bf16),
            pltpu.VMEM((COLS, TOK, LANES), bf16),
            pltpu.VMEM((3, GROUPS, WIDTH, GROUP), bf16),
            pltpu.SemaphoreType.DMA((3, GROUPS)),
        ],
        compiler_params=params(VMEM),
        cost_estimate=cost(
            6 * TOK * WIDTH * WIDTH + 8 * TOK * FRAMES * WIDTH,
            6 * WIDTH * WIDTH + 4 * TOK * WIDTH,
            HEADS * TOK * FRAMES,
        ),
        name="time_attend",
    )(in_vmem(slab), gain, in_hbm(weight))


def unpack_kernel(slab_ref, out_hbm, out_ref, sems):
    swap = swap_matrix()
    copies = []
    for part in range(4):
        slab_to_rows(
            lambda block, half: slab_ref[
                16 * block : 16 * block + 16, 16 * half : 16 * half + 16, :
            ],
            out_ref, swap, blocks=(2 * part, 2 * part + 1),
        )
        for k in range(PARTS):
            some = pl.ds(k * FRAMES + 32 * part, 32)
            copies.append(
                pltpu.make_async_copy(out_ref.at[some], out_hbm.at[some], sems.at[len(copies)])
            )
            copies[-1].start()
    for copy in copies:
        copy.wait()


def unpack(slab):
    return pl.pallas_call(
        unpack_kernel,
        out_shape=jax.ShapeDtypeStruct((TOK, WIDTH), bf16),
        in_specs=[WHOLE],
        out_specs=THERE,
        scratch_shapes=[pltpu.VMEM((TOK, WIDTH), bf16), pltpu.SemaphoreType.DMA((4 * PARTS,))],
        compiler_params=params(VMEM),
        cost_estimate=cost(2 * TOK * WIDTH * 256, 4 * TOK * WIDTH),
        name="unpack",
    )(in_vmem(slab))


def exchange(slab):
    return lax.all_to_all(slab, "frame", split_axis=0, concat_axis=0, tiled=True)


def body(video, key_list, pairs, norm_gain, qkv_weight, out_weight, time_gain, time_weight):
    spread = exchange(prep(pairs, video, norm_gain))
    queries, keys, values = project(video, norm_gain, qkv_weight)
    wanted = exchange(choose(key_list, spread, queries))
    mixed, stat = own_attend(queries, keys, values)
    spatial, slab = attend(wanted, queries, mixed, stat, qkv_weight, out_weight, video)
    slab = time_attend(exchange(slab), time_gain, time_weight)
    return spatial, unpack(exchange(slab))


def solution(mesh):
    return jax.shard_map(
        body,
        mesh=mesh,
        in_specs=(P("frame", None), P(), P("frame", None), P(), P(), P(), P(), P()),
        out_specs=(P("frame", None), P("frame", None)),
        check_vma=False,
    )
```

```python
import jax
import jax.numpy as jnp
from jax import lax
from jax.experimental import pallas as pl
from jax.experimental.pallas import tpu as pltpu
from jax.sharding import PartitionSpec as P

WIDTH = 1280
HEADS = 20
HEAD = 64
TOK = 384
FRAMES = 128
KEYS = 8
PARTS = TOK // FRAMES
LANES = 128
COLS = WIDTH // LANES
SLAB = 32
GROUP = 256
GROUPS = WIDTH // GROUP
VMEM = 52
SCALE = 0.125 * 1.4426950408889634

bf16 = jnp.bfloat16
f32 = jnp.float32


def params(mib, **more):
    return pltpu.CompilerParams(vmem_limit_bytes=mib << 20, **more)


def cost(flops, moved, exps=0):
    return pl.CostEstimate(flops=int(flops), bytes_accessed=int(moved), transcendentals=int(exps))


def in_vmem(x):
    return pltpu.with_memory_space_constraint(x, pltpu.VMEM)


def in_hbm(x):
    return pltpu.with_memory_space_constraint(x, pltpu.HBM)


WHOLE = pl.BlockSpec(memory_space=pltpu.VMEM)
THERE = pl.BlockSpec(memory_space=pl.ANY)
SMALL = pl.BlockSpec(memory_space=pltpu.SMEM)


def norm_rows(values, gain):
    centred = values - jnp.mean(values, axis=-1, keepdims=True)
    spread = jnp.mean(centred * centred, axis=-1, keepdims=True)
    return (centred * lax.rsqrt(spread + 1e-05) * gain).astype(bf16)


def swap_matrix():
    row = lax.broadcasted_iota(jnp.int32, (256, 256), 0)
    col = lax.broadcasted_iota(jnp.int32, (256, 256), 1)
    return jnp.where(col == (row % 16) * 16 + row // 16, 1.0, 0.0).astype(bf16)


def rows_to_slab(tile, slab_ref, swap, spare=None, halves=(0, 1)):
    for half in halves:
        for pair in range(4):
            sides = []
            for block in (2 * pair, 2 * pair + 1):
                tiles = []
                for unit in range(16 * half, 16 * half + 16):
                    k, g = divmod(unit, COLS)
                    if k < PARTS:
                        tiles.append(tile(k * FRAMES + 16 * block, g))
                    elif spare is None:
                        tiles.append(jnp.zeros((16, LANES), bf16))
                    else:
                        tiles.append(spare[unit - PARTS * COLS])
                sides.append(jnp.concatenate(tiles, axis=0))
            both = jnp.concatenate(sides, axis=1)
            moved = jnp.dot(swap, both, preferred_element_type=f32).astype(bf16)
            for side in range(2):
                block = 2 * pair + side
                slab_ref[16 * block : 16 * block + 16, 16 * half : 16 * half + 16, :] = moved[
                    :, side * LANES : (side + 1) * LANES
                ].reshape(16, 16, LANES)


def tiles_of(rows_ref):
    return lambda at, g: rows_ref[at : at + 16, g * LANES : (g + 1) * LANES]


def slab_to_rows(load, rows_ref, swap, first=0, blocks=range(8)):
    for block in blocks:
        both = jnp.concatenate(
            [load(block, half).reshape(256, LANES) for half in range(2)], axis=1
        )
        moved = jnp.dot(swap, both, preferred_element_type=f32).astype(bf16)
        for unit in range(PARTS * COLS):
            half, row = divmod(unit, 16)
            k, g = divmod(unit, COLS)
            at = first + k * FRAMES + 16 * block
            rows_ref[at : at + 16, g * LANES : (g + 1) * LANES] = moved[
                16 * row : 16 * row + 16, half * LANES : (half + 1) * LANES
            ]


def prep_kernel(pairs_ref, video_ref, gain_ref, slab_hbm, normed_ref, slab_ref, sems):
    swap = swap_matrix()
    gain = gain_ref[...].reshape(1, WIDTH)
    spare = [
        jnp.full((16, LANES), pairs_ref[0, which], jnp.int32).astype(f32).astype(bf16)
        for which in range(2)
    ]
    leaving = []

    def give(half):
        rows_to_slab(tiles_of(normed_ref), slab_ref, swap, spare, halves=(half,))
        some = pl.ds(16 * half, 16)
        leaving.append(
            pltpu.make_async_copy(slab_ref.at[:, some], slab_hbm.at[:, some], sems.at[half])
        )
        leaving[-1].start()

    for k in range(PARTS):
        rows = pl.ds(k * FRAMES, FRAMES)
        normed_ref[rows, :] = norm_rows(video_ref[rows, :].astype(f32), gain)
        if k == 1:
            give(0)
    give(1)
    for copy in leaving:
        copy.wait()


def prep(pairs, video, gain):
    return pl.pallas_call(
        prep_kernel,
        out_shape=pltpu.HBM((FRAMES, SLAB, LANES), bf16),
        in_specs=[SMALL, WHOLE, WHOLE],
        out_specs=THERE,
        scratch_shapes=[
            pltpu.VMEM((TOK, WIDTH), bf16),
            pltpu.VMEM((FRAMES, SLAB, LANES), bf16),
            pltpu.SemaphoreType.DMA((2,)),
        ],
        compiler_params=params(VMEM),
        cost_estimate=cost(6 * TOK * WIDTH, 4 * TOK * WIDTH),
        name="prep",
    )(in_hbm(pairs), in_hbm(video), in_hbm(gain))


def project_kernel(video_ref, gain_ref, wq_ref, wk_ref, wv_ref, q_ref, k_ref, v_ref, normed_ref):
    @pl.when(pl.program_id(0) == 0)
    def _():
        gain = gain_ref[...].reshape(1, WIDTH)
        normed_ref[...] = norm_rows(video_ref[...].astype(f32), gain)

    rows = normed_ref[...]
    queries = jnp.dot(rows, wq_ref[...], preferred_element_type=f32) * SCALE
    q_ref[...] = queries.astype(bf16)
    k_ref[...] = jnp.dot(rows, wk_ref[...], preferred_element_type=f32).astype(bf16)
    v_ref[...] = jnp.dot(rows, wv_ref[...], preferred_element_type=f32).astype(bf16)


def project(video, gain, weight):
    out = pltpu.HBM((TOK, WIDTH), bf16)
    out_spec = pl.BlockSpec((TOK, GROUP), lambda i: (0, i))
    return pl.pallas_call(
        project_kernel,
        grid=(GROUPS,),
        out_shape=(out, out, out),
        in_specs=[
            WHOLE,
            WHOLE,
            pl.BlockSpec((WIDTH, GROUP), lambda i: (0, i)),
            pl.BlockSpec((WIDTH, GROUP), lambda i: (0, GROUPS + i)),
            pl.BlockSpec((WIDTH, GROUP), lambda i: (0, 2 * GROUPS + i)),
        ],
        out_specs=(out_spec, out_spec, out_spec),
        scratch_shapes=[pltpu.VMEM((TOK, WIDTH), bf16)],
        compiler_params=params(VMEM),
        cost_estimate=cost(6 * TOK * WIDTH * WIDTH, 6 * WIDTH * WIDTH + 8 * TOK * WIDTH),
        name="project",
    )(in_hbm(video), in_hbm(gain), in_hbm(weight), in_hbm(weight), in_hbm(weight))


def low_lanes(rows):
    return lax.broadcasted_iota(jnp.int32, (rows, LANES), 1) < HEAD


def attend_pairs(units):
    scores, padded = [], []
    for queries, keys, values, _ in units:
        low_q, low_v = low_lanes(queries.shape[0]), low_lanes(values.shape[0])
        wide = queries.astype(f32)
        for head in range(2):
            mine = jnp.where(low_q, wide, 0.0) if head == 0 else jnp.where(low_q, 0.0, wide)
            rest = jnp.where(low_v, values, 1.0) if head == 0 else jnp.where(low_v, 1.0, values)
            padded.append(rest.astype(bf16))
            scores.append(
                lax.dot_general(
                    mine.astype(bf16), keys, (((1,), (1,)), ((), ())), preferred_element_type=f32
                )
            )
    tops = [jnp.max(s, axis=-1, keepdims=True) for s in scores]
    for i, (_, _, _, top) in enumerate(units):
        if top is not None:
            for head in range(2):
                other = top[:, head * HEAD : head * HEAD + 1]
                tops[2 * i + head] = jnp.maximum(tops[2 * i + head], other)
    weights = [jnp.exp2(s - top).astype(bf16) for s, top in zip(scores, tops)]
    outs = [jnp.dot(w, v, preferred_element_type=f32) for w, v in zip(weights, padded)]
    given = []
    for i, (queries, _, _, _) in enumerate(units):
        low = low_lanes(queries.shape[0])
        one, two = outs[2 * i], outs[2 * i + 1]
        total = pltpu.roll(jnp.where(low, two, one), HEAD, 1)
        given.append((jnp.where(low, one, two), total, tops[2 * i : 2 * i + 2]))
    return given


def group_lanes(group, size, offset=0):
    return pl.ds(pl.multiple_of(offset + group * GROUP, LANES), size)


def flipped_scores(queries, keys, head):
    low = low_lanes(queries.shape[0])
    wide = queries.astype(f32)
    mine = jnp.where(low, wide, 0.0) if head == 0 else jnp.where(low, 0.0, wide)
    return lax.dot_general(
        keys, mine.astype(bf16), (((1,), (1,)), ((), ())), preferred_element_type=f32
    )


def with_ones(values):
    return jnp.concatenate([values, jnp.ones((16, values.shape[1]), bf16)], axis=0)


def own_kernel(q_ref, k_ref, v_ref, mixed_ref, stat_ref):
    @pl.loop(0, GROUPS)
    def _(group):
        at = group_lanes(group, GROUP)
        queries, keys = q_ref[:, at], k_ref[:, at]
        values = v_ref[:, at].T
        scores = []
        for head in range(4):
            lanes = slice(head // 2 * LANES, (head // 2 + 1) * LANES)
            scores.append(flipped_scores(queries[:, lanes], keys[:, lanes], head % 2))
        tops = [jnp.max(s, axis=0, keepdims=True) for s in scores]
        weights = [jnp.exp2(s - top).astype(bf16) for s, top in zip(scores, tops)]
        for head in range(4):
            rows = slice(head * HEAD, (head + 1) * HEAD)
            out = jnp.dot(with_ones(values[rows]), weights[head], preferred_element_type=f32)
            mixed_ref[group, rows, :] = out[:HEAD]
            stat_ref[group, head : head + 1, :] = tops[head]
            stat_ref[group, 4 + head : 5 + head, :] = out[HEAD : HEAD + 1]


def own_attend(queries, keys, values):
    return pl.pallas_call(
        own_kernel,
        out_shape=(pltpu.HBM((GROUPS, GROUP, TOK), f32), pltpu.HBM((GROUPS, 8, TOK), f32)),
        in_specs=[WHOLE, WHOLE, WHOLE],
        out_specs=(WHOLE, WHOLE),
        compiler_params=params(VMEM),
        cost_estimate=cost(8 * TOK * TOK * WIDTH, 10 * TOK * WIDTH, HEADS * TOK * TOK),
        name="own_attend",
    )(in_hbm(queries), in_hbm(keys), in_hbm(values))


def choose_kernel(key_list_ref, slab_ref, after_ref, out_hbm, out_ref, sems):
    del after_ref
    copies = []
    halves = [
        jnp.concatenate([slab_ref[key_list_ref[s], at : at + 16, :] for s in range(KEYS)], axis=0)
        for at in (0, 16)
    ]
    keys = jnp.concatenate(halves, axis=1)
    row = lax.broadcasted_iota(jnp.int32, (16, LANES), 0)
    col = lax.broadcasted_iota(jnp.int32, (16, LANES), 1)
    slot = jnp.where(col % 16 == row, col // 16, -1).astype(f32)
    for f in range(0, FRAMES, 8):
        picks = []
        for more in range(8):
            spare = slab_ref[f + more, 16:32, :].astype(f32)
            for which in range(2):
                wanted = spare[14 + which : 15 + which, :]
                picks.append(jnp.where(slot == wanted, 1.0, 0.0).astype(bf16))
        chosen = jnp.dot(jnp.concatenate(picks, axis=0), keys, preferred_element_type=f32)
        chosen = chosen.astype(bf16).reshape(8, 2, 16, 2 * LANES)
        out_ref[f : f + 8, :, 0:16, :] = chosen[..., :LANES]
        out_ref[f : f + 8, :, 16:32, :] = chosen[..., LANES:]
        if (f + 8) % 32 == 0:
            some = pl.ds(f - 24, 32)
            copies.append(
                pltpu.make_async_copy(out_ref.at[some], out_hbm.at[some], sems.at[len(copies)])
            )
            copies[-1].start()
    for copy in copies:
        copy.wait()


def choose(key_list, slab, after):
    return pl.pallas_call(
        choose_kernel,
        out_shape=pltpu.HBM((FRAMES, 2, SLAB, LANES), bf16),
        in_specs=[SMALL, WHOLE, THERE],
        out_specs=THERE,
        scratch_shapes=[
            pltpu.VMEM((FRAMES, 2, SLAB, LANES), bf16),
            pltpu.SemaphoreType.DMA((4,)),
        ],
        compiler_params=params(VMEM),
        cost_estimate=cost(4 * FRAMES * SLAB * LANES * 256, 6 * FRAMES * SLAB * LANES),
        name="choose",
    )(key_list, in_vmem(slab), in_hbm(after))


LARGE = 1e30


def attend_kernel(
    slab_ref, q_hbm, mixed_hbm, stat_hbm, weight_hbm, wo_hbm, video_hbm,
    spatial_hbm, out_slab_ref,
    spatial_ref, rows_ref, heads_ref, most_ref, q_ref, mixed_ref, stat_ref,
    wk_ref, wv_ref, wo_ref, video_ref, sems, last_sems, out_sems,
):
    def copies(group):
        pairs = (
            (weight_hbm.at[:, group_lanes(group, GROUP, WIDTH)], wk_ref),
            (weight_hbm.at[:, group_lanes(group, GROUP, 2 * WIDTH)], wv_ref),
            (q_hbm.at[:, group_lanes(group, GROUP)], q_ref),
            (mixed_hbm.at[group], mixed_ref),
            (stat_hbm.at[group], stat_ref),
        )
        return [
            pltpu.make_async_copy(source, target.at[group], sems.at[i, group])
            for i, (source, target) in enumerate(pairs)
        ]

    last = (
        pltpu.make_async_copy(wo_hbm, wo_ref, last_sems.at[0]),
        pltpu.make_async_copy(video_hbm, video_ref, last_sems.at[1]),
    )
    for group in range(GROUPS):
        for copy in copies(group):
            copy.start()
    for copy in last:
        copy.start()

    swap = swap_matrix()
    for which in range(2):
        slab_to_rows(
            lambda block, half: slab_ref[
                16 * block : 16 * block + 16, which, 16 * half : 16 * half + 16, :
            ],
            rows_ref, swap, which * TOK,
        )
    most_ref[...] = jnp.zeros_like(most_ref)

    def project_group(group):
        rows = rows_ref[...]
        keys = jnp.dot(rows, wk_ref[group], preferred_element_type=f32).astype(bf16)
        values = jnp.dot(rows, wv_ref[group], preferred_element_type=f32).astype(bf16)
        return keys, values.T

    def score_group(group, keys):
        scores = []
        for head in range(4):
            lanes = slice(head // 2 * LANES, (head // 2 + 1) * LANES)
            scores.append(flipped_scores(q_ref[group, :, lanes], keys[:, lanes], head % 2))
        return scores

    def mix_group(group, weights, values, less):
        made, totals = [], []
        for head in range(4):
            rows = slice(head * HEAD, (head + 1) * HEAD)
            out = jnp.dot(with_ones(values[rows]), weights[head], preferred_element_type=f32)
            mixed, total = mixed_ref[group, rows, :], stat_ref[group, 4 + head : 5 + head, :]
            if less is not None:
                mixed, total = mixed * less[head], total * less[head]
            mixed, total = mixed + out[:HEAD], total + out[HEAD : HEAD + 1]
            made.append((mixed / total).astype(bf16))
            totals.append(total)
        heads_ref[group] = jnp.concatenate(made, axis=0).T
        return totals

    @pl.loop(0, GROUPS)
    def _(group):
        arriving = copies(group)
        for copy in arriving[:2]:
            copy.wait()
        keys, values = project_group(group)
        for copy in arriving[2:]:
            copy.wait()
        scores = score_group(group, keys)
        weights = [
            jnp.exp2(scores[head] - stat_ref[group, head : head + 1, :]).astype(bf16)
            for head in range(4)
        ]
        for total in mix_group(group, weights, values, None):
            most_ref[...] = jnp.maximum(most_ref[...], total)

    @pl.when(jnp.logical_not(jnp.max(most_ref[...]) < LARGE))
    def _():
        @pl.loop(0, GROUPS)
        def _(group):
            keys, values = project_group(group)
            scores = score_group(group, keys)
            own = [stat_ref[group, head : head + 1, :] for head in range(4)]
            tops = [
                jnp.maximum(top, jnp.max(s, axis=0, keepdims=True)) for s, top in zip(scores, own)
            ]
            weights = [jnp.exp2(s - top).astype(bf16) for s, top in zip(scores, tops)]
            mix_group(group, weights, values, [jnp.exp2(o - top) for o, top in zip(own, tops)])

    given = []
    for copy in last:
        copy.wait()
    for k in range(PARTS):
        rows = pl.ds(k * FRAMES, FRAMES)
        heads = jnp.concatenate([heads_ref[g, rows, :] for g in range(GROUPS)], axis=1)
        added = jnp.dot(heads, wo_ref[...], preferred_element_type=f32)
        spatial_ref[rows, :] = (video_ref[rows, :].astype(f32) + added).astype(bf16)
        given.append(
            pltpu.make_async_copy(spatial_ref.at[rows], spatial_hbm.at[rows], out_sems.at[k])
        )
        given[-1].start()
    rows_to_slab(tiles_of(spatial_ref), out_slab_ref, swap)
    for copy in given:
        copy.wait()


def attend(slab, queries, mixed, stat, weight, out_weight, video):
    return pl.pallas_call(
        attend_kernel,
        out_shape=(
            jax.ShapeDtypeStruct((TOK, WIDTH), bf16),
            pltpu.VMEM((FRAMES, SLAB, LANES), bf16),
        ),
        in_specs=[WHOLE] + [THERE] * 6,
        out_specs=(THERE, WHOLE),
        scratch_shapes=[
            pltpu.VMEM((TOK, WIDTH), bf16),
            pltpu.VMEM((2 * TOK, WIDTH), bf16),
            pltpu.VMEM((GROUPS, TOK, GROUP), bf16),
            pltpu.VMEM((1, TOK), f32),
            pltpu.VMEM((GROUPS, TOK, GROUP), bf16),
            pltpu.VMEM((GROUPS, GROUP, TOK), f32),
            pltpu.VMEM((GROUPS, 8, TOK), f32),
            pltpu.VMEM((GROUPS, WIDTH, GROUP), bf16),
            pltpu.VMEM((GROUPS, WIDTH, GROUP), bf16),
            pltpu.VMEM((WIDTH, WIDTH), bf16),
            pltpu.VMEM((TOK, WIDTH), bf16),
            pltpu.SemaphoreType.DMA((5, GROUPS)),
            pltpu.SemaphoreType.DMA((2,)),
            pltpu.SemaphoreType.DMA((PARTS,)),
        ],
        compiler_params=params(VMEM),
        cost_estimate=cost(
            8 * TOK * WIDTH * WIDTH + 16 * TOK * TOK * WIDTH,
            6 * WIDTH * WIDTH + 20 * TOK * WIDTH,
            2 * HEADS * TOK * TOK,
        ),
        name="attend",
    )(
        in_vmem(slab), in_hbm(queries), in_hbm(mixed), in_hbm(stat),
        in_hbm(weight), in_hbm(out_weight), in_hbm(video),
    )


def time_kernel(
    slab_ref, gain_ref, weight_hbm, out_slab_ref, rows_ref, heads_ref, weight_ref, sems
):
    def copies(group):
        return [
            pltpu.make_async_copy(
                weight_hbm.at[:, group_lanes(group, GROUP, which * WIDTH)],
                weight_ref.at[which, group],
                sems.at[which, group],
            )
            for which in range(3)
        ]

    for group in range(GROUPS):
        for copy in copies(group):
            copy.start()
    swap = swap_matrix()
    slab_to_rows(
        lambda block, half: slab_ref[16 * block : 16 * block + 16, 16 * half : 16 * half + 16, :],
        rows_ref, swap,
    )
    for k in range(PARTS):
        rows = pl.ds(k * FRAMES, FRAMES)
        rows_ref[rows, :] = norm_rows(rows_ref[rows, :].astype(f32), gain_ref[...].reshape(1, WIDTH))

    @pl.loop(0, GROUPS)
    def _(group):
        for copy in copies(group):
            copy.wait()
        rows = rows_ref[...]
        made = [
            jnp.dot(rows, weight_ref[which, group], preferred_element_type=f32)
            for which in range(3)
        ]
        queries, keys, values = (made[0] * SCALE).astype(bf16), made[1].astype(bf16), made[2]
        units, places = [], []
        for pair in range(2):
            lanes = slice(pair * LANES, (pair + 1) * LANES)
            for k in range(PARTS):
                at = slice(k * FRAMES, (k + 1) * FRAMES)
                units.append((queries[at, lanes], keys[at, lanes], values[at, lanes], None))
                places.append((pair, at))
        for (pair, at), (mixed, total, _) in zip(places, attend_pairs(units)):
            heads_ref[2 * group + pair, at, :] = (mixed / total).astype(bf16)

    rows_to_slab(lambda at, g: heads_ref[g, at : at + 16, :], out_slab_ref, swap)


def time_attend(slab, gain, weight):
    return pl.pallas_call(
        time_kernel,
        out_shape=pltpu.VMEM((FRAMES, SLAB, LANES), bf16),
        in_specs=[WHOLE, WHOLE, THERE],
        out_specs=WHOLE,
        scratch_shapes=[
            pltpu.VMEM((TOK, WIDTH), bf16),
            pltpu.VMEM((COLS, TOK, LANES), bf16),
            pltpu.VMEM((3, GROUPS, WIDTH, GROUP), bf16),
            pltpu.SemaphoreType.DMA((3, GROUPS)),
        ],
        compiler_params=params(VMEM),
        cost_estimate=cost(
            6 * TOK * WIDTH * WIDTH + 8 * TOK * FRAMES * WIDTH,
            6 * WIDTH * WIDTH + 4 * TOK * WIDTH,
            HEADS * TOK * FRAMES,
        ),
        name="time_attend",
    )(in_vmem(slab), in_hbm(gain), in_hbm(weight))


def unpack_kernel(slab_ref, out_hbm, out_ref, sems):
    swap = swap_matrix()
    copies = []
    for part in range(4):
        slab_to_rows(
            lambda block, half: slab_ref[
                16 * block : 16 * block + 16, 16 * half : 16 * half + 16, :
            ],
            out_ref, swap, blocks=(2 * part, 2 * part + 1),
        )
        for k in range(PARTS):
            some = pl.ds(k * FRAMES + 32 * part, 32)
            copies.append(
                pltpu.make_async_copy(out_ref.at[some], out_hbm.at[some], sems.at[len(copies)])
            )
            copies[-1].start()
    for copy in copies:
        copy.wait()


def unpack(slab):
    return pl.pallas_call(
        unpack_kernel,
        out_shape=jax.ShapeDtypeStruct((TOK, WIDTH), bf16),
        in_specs=[WHOLE],
        out_specs=THERE,
        scratch_shapes=[pltpu.VMEM((TOK, WIDTH), bf16), pltpu.SemaphoreType.DMA((4 * PARTS,))],
        compiler_params=params(VMEM),
        cost_estimate=cost(2 * TOK * WIDTH * 256, 4 * TOK * WIDTH),
        name="unpack",
    )(in_vmem(slab))


def exchange(slab):
    return lax.all_to_all(slab, "frame", split_axis=0, concat_axis=0, tiled=True)


def body(video, key_list, pairs, norm_gain, qkv_weight, out_weight, time_gain, time_weight):
    spread = exchange(prep(pairs, video, norm_gain))
    queries, keys, values = project(video, norm_gain, qkv_weight)
    wanted = exchange(choose(key_list, spread, queries))
    mixed, stat = own_attend(queries, keys, values)
    spatial, slab = attend(wanted, queries, mixed, stat, qkv_weight, out_weight, video)
    slab = time_attend(exchange(slab), time_gain, time_weight)
    return spatial, unpack(exchange(slab))


def solution(mesh):
    return jax.shard_map(
        body,
        mesh=mesh,
        in_specs=(P("frame", None), P(), P("frame", None), P(), P(), P(), P(), P()),
        out_specs=(P("frame", None), P("frame", None)),
        check_vma=False,
    )
```

```python
import jax
import jax.numpy as jnp
from jax import lax
from jax.experimental import pallas as pl
from jax.experimental.pallas import tpu as pltpu
from jax.sharding import PartitionSpec as P

WIDTH = 1280
HEADS = 20
HEAD = 64
TOK = 384
FRAMES = 128
KEYS = 8
PARTS = TOK // FRAMES
LANES = 128
COLS = WIDTH // LANES
SLAB = 32
GROUP = 256
GROUPS = WIDTH // GROUP
VMEM = 52
SCALE = 0.125 * 1.4426950408889634

bf16 = jnp.bfloat16
f32 = jnp.float32


def params(mib, **more):
    return pltpu.CompilerParams(vmem_limit_bytes=mib << 20, **more)


def cost(flops, moved, exps=0):
    return pl.CostEstimate(flops=int(flops), bytes_accessed=int(moved), transcendentals=int(exps))


def in_vmem(x):
    return pltpu.with_memory_space_constraint(x, pltpu.VMEM)


def in_hbm(x):
    return pltpu.with_memory_space_constraint(x, pltpu.HBM)


WHOLE = pl.BlockSpec(memory_space=pltpu.VMEM)
THERE = pl.BlockSpec(memory_space=pl.ANY)
SMALL = pl.BlockSpec(memory_space=pltpu.SMEM)


def norm_rows(values, gain):
    centred = values - jnp.mean(values, axis=-1, keepdims=True)
    spread = jnp.mean(centred * centred, axis=-1, keepdims=True)
    return (centred * lax.rsqrt(spread + 1e-05) * gain).astype(bf16)


def swap_matrix():
    row = lax.broadcasted_iota(jnp.int32, (256, 256), 0)
    col = lax.broadcasted_iota(jnp.int32, (256, 256), 1)
    return jnp.where(col == (row % 16) * 16 + row // 16, 1.0, 0.0).astype(bf16)


def rows_to_slab(tile, slab_ref, swap, spare=None, halves=(0, 1)):
    for half in halves:
        for pair in range(4):
            sides = []
            for block in (2 * pair, 2 * pair + 1):
                tiles = []
                for unit in range(16 * half, 16 * half + 16):
                    k, g = divmod(unit, COLS)
                    if k < PARTS:
                        tiles.append(tile(k * FRAMES + 16 * block, g))
                    elif spare is None:
                        tiles.append(jnp.zeros((16, LANES), bf16))
                    else:
                        tiles.append(spare[unit - PARTS * COLS])
                sides.append(jnp.concatenate(tiles, axis=0))
            both = jnp.concatenate(sides, axis=1)
            moved = jnp.dot(swap, both, preferred_element_type=f32).astype(bf16)
            for side in range(2):
                block = 2 * pair + side
                slab_ref[16 * block : 16 * block + 16, 16 * half : 16 * half + 16, :] = moved[
                    :, side * LANES : (side + 1) * LANES
                ].reshape(16, 16, LANES)


def tiles_of(rows_ref):
    return lambda at, g: rows_ref[at : at + 16, g * LANES : (g + 1) * LANES]


def slab_to_rows(load, rows_ref, swap, first=0, blocks=range(8)):
    for block in blocks:
        both = jnp.concatenate(
            [load(block, half).reshape(256, LANES) for half in range(2)], axis=1
        )
        moved = jnp.dot(swap, both, preferred_element_type=f32).astype(bf16)
        for unit in range(PARTS * COLS):
            half, row = divmod(unit, 16)
            k, g = divmod(unit, COLS)
            at = first + k * FRAMES + 16 * block
            rows_ref[at : at + 16, g * LANES : (g + 1) * LANES] = moved[
                16 * row : 16 * row + 16, half * LANES : (half + 1) * LANES
            ]


def prep_kernel(pairs_ref, video_ref, gain_ref, slab_hbm, normed_ref, slab_ref, sems):
    swap = swap_matrix()
    gain = gain_ref[...].reshape(1, WIDTH)
    spare = [
        jnp.full((16, LANES), pairs_ref[0, which], jnp.int32).astype(f32).astype(bf16)
        for which in range(2)
    ]
    leaving = []

    def give(half):
        rows_to_slab(tiles_of(normed_ref), slab_ref, swap, spare, halves=(half,))
        some = pl.ds(16 * half, 16)
        leaving.append(
            pltpu.make_async_copy(slab_ref.at[:, some], slab_hbm.at[:, some], sems.at[half])
        )
        leaving[-1].start()

    for k in range(PARTS):
        rows = pl.ds(k * FRAMES, FRAMES)
        normed_ref[rows, :] = norm_rows(video_ref[rows, :].astype(f32), gain)
        if k == 1:
            give(0)
    give(1)
    for copy in leaving:
        copy.wait()


def prep(pairs, video, gain):
    return pl.pallas_call(
        prep_kernel,
        out_shape=pltpu.HBM((FRAMES, SLAB, LANES), bf16),
        in_specs=[SMALL, WHOLE, WHOLE],
        out_specs=THERE,
        scratch_shapes=[
            pltpu.VMEM((TOK, WIDTH), bf16),
            pltpu.VMEM((FRAMES, SLAB, LANES), bf16),
            pltpu.SemaphoreType.DMA((2,)),
        ],
        compiler_params=params(VMEM),
        cost_estimate=cost(6 * TOK * WIDTH, 4 * TOK * WIDTH),
        name="prep",
    )(in_hbm(pairs), in_hbm(video), in_hbm(gain))


def low_lanes(rows):
    return lax.broadcasted_iota(jnp.int32, (rows, LANES), 1) < HEAD


def attend_pairs(units):
    scores, padded = [], []
    for queries, keys, values, _ in units:
        low_q, low_v = low_lanes(queries.shape[0]), low_lanes(values.shape[0])
        wide = queries.astype(f32)
        for head in range(2):
            mine = jnp.where(low_q, wide, 0.0) if head == 0 else jnp.where(low_q, 0.0, wide)
            rest = jnp.where(low_v, values, 1.0) if head == 0 else jnp.where(low_v, 1.0, values)
            padded.append(rest.astype(bf16))
            scores.append(
                lax.dot_general(
                    mine.astype(bf16), keys, (((1,), (1,)), ((), ())), preferred_element_type=f32
                )
            )
    tops = [jnp.max(s, axis=-1, keepdims=True) for s in scores]
    for i, (_, _, _, top) in enumerate(units):
        if top is not None:
            for head in range(2):
                other = top[:, head * HEAD : head * HEAD + 1]
                tops[2 * i + head] = jnp.maximum(tops[2 * i + head], other)
    weights = [jnp.exp2(s - top).astype(bf16) for s, top in zip(scores, tops)]
    outs = [jnp.dot(w, v, preferred_element_type=f32) for w, v in zip(weights, padded)]
    given = []
    for i, (queries, _, _, _) in enumerate(units):
        low = low_lanes(queries.shape[0])
        one, two = outs[2 * i], outs[2 * i + 1]
        total = pltpu.roll(jnp.where(low, two, one), HEAD, 1)
        given.append((jnp.where(low, one, two), total, tops[2 * i : 2 * i + 2]))
    return given


def group_lanes(group, size, offset=0):
    return pl.ds(pl.multiple_of(offset + group * GROUP, LANES), size)


def flipped_scores(queries, keys, head):
    low = low_lanes(queries.shape[0])
    wide = queries.astype(f32)
    mine = jnp.where(low, wide, 0.0) if head == 0 else jnp.where(low, 0.0, wide)
    return lax.dot_general(
        keys, mine.astype(bf16), (((1,), (1,)), ((), ())), preferred_element_type=f32
    )


def with_ones(values):
    return jnp.concatenate([values, jnp.ones((16, values.shape[1]), bf16)], axis=0)


def group_copies(weight_hbm, weight_ref, sems, group):
    return [
        pltpu.make_async_copy(
            weight_hbm.at[:, group_lanes(group, GROUP, which * WIDTH)],
            weight_ref.at[which, group],
            sems.at[which, group],
        )
        for which in range(3)
    ]


def own_kernel(
    video_ref, gain_ref, weight_hbm, q_ref, mixed_ref, stat_ref, rows_ref, weight_ref, sems
):
    for group in range(GROUPS):
        for copy in group_copies(weight_hbm, weight_ref, sems, group):
            copy.start()
    gain = gain_ref[...].reshape(1, WIDTH)
    for k in range(PARTS):
        rows = pl.ds(k * FRAMES, FRAMES)
        rows_ref[rows, :] = norm_rows(video_ref[rows, :].astype(f32), gain)

    @pl.loop(0, GROUPS)
    def _(group):
        for copy in group_copies(weight_hbm, weight_ref, sems, group):
            copy.wait()
        rows = rows_ref[...]
        queries, keys, values = [
            jnp.dot(rows, weight_ref[which, group], preferred_element_type=f32)
            for which in range(3)
        ]
        queries, keys, values = (queries * SCALE).astype(bf16), keys.astype(bf16), values.astype(bf16).T
        q_ref[:, group_lanes(group, GROUP)] = queries
        scores = []
        for head in range(4):
            lanes = slice(head // 2 * LANES, (head // 2 + 1) * LANES)
            scores.append(flipped_scores(queries[:, lanes], keys[:, lanes], head % 2))
        tops = [jnp.max(s, axis=0, keepdims=True) for s in scores]
        weights = [jnp.exp2(s - top).astype(bf16) for s, top in zip(scores, tops)]
        for head in range(4):
            rows = slice(head * HEAD, (head + 1) * HEAD)
            out = jnp.dot(with_ones(values[rows]), weights[head], preferred_element_type=f32)
            mixed_ref[group, rows, :] = out[:HEAD]
            stat_ref[group, head : head + 1, :] = tops[head]
            stat_ref[group, 4 + head : 5 + head, :] = out[HEAD : HEAD + 1]


def own_attend(video, gain, weight):
    return pl.pallas_call(
        own_kernel,
        out_shape=(
            pltpu.HBM((TOK, WIDTH), bf16),
            pltpu.HBM((GROUPS, GROUP, TOK), f32),
            pltpu.HBM((GROUPS, 8, TOK), f32),
        ),
        in_specs=[WHOLE, WHOLE, THERE],
        out_specs=(WHOLE, WHOLE, WHOLE),
        scratch_shapes=[
            pltpu.VMEM((TOK, WIDTH), bf16),
            pltpu.VMEM((3, GROUPS, WIDTH, GROUP), bf16),
            pltpu.SemaphoreType.DMA((3, GROUPS)),
        ],
        compiler_params=params(VMEM),
        cost_estimate=cost(
            6 * TOK * WIDTH * WIDTH + 8 * TOK * TOK * WIDTH,
            6 * WIDTH * WIDTH + 10 * TOK * WIDTH,
            HEADS * TOK * TOK,
        ),
        name="own_attend",
    )(in_hbm(video), in_hbm(gain), in_hbm(weight))


def choose_kernel(key_list_ref, slab_ref, after_ref, out_ref):
    del after_ref
    halves = [
        jnp.concatenate([slab_ref[key_list_ref[s], at : at + 16, :] for s in range(KEYS)], axis=0)
        for at in (0, 16)
    ]
    keys = jnp.concatenate(halves, axis=1)
    row = lax.broadcasted_iota(jnp.int32, (16, LANES), 0)
    col = lax.broadcasted_iota(jnp.int32, (16, LANES), 1)
    slot = jnp.where(col % 16 == row, col // 16, -1).astype(f32)
    for f in range(0, FRAMES, 8):
        picks = []
        for more in range(8):
            spare = slab_ref[f + more, 16:32, :].astype(f32)
            for which in range(2):
                wanted = spare[14 + which : 15 + which, :]
                picks.append(jnp.where(slot == wanted, 1.0, 0.0).astype(bf16))
        chosen = jnp.dot(jnp.concatenate(picks, axis=0), keys, preferred_element_type=f32)
        chosen = chosen.astype(bf16).reshape(8, 2, 16, 2 * LANES)
        out_ref[f : f + 8, :, 0:16, :] = chosen[..., :LANES]
        out_ref[f : f + 8, :, 16:32, :] = chosen[..., LANES:]


def choose(key_list, slab, after):
    return pl.pallas_call(
        choose_kernel,
        out_shape=pltpu.VMEM((FRAMES, 2, SLAB, LANES), bf16),
        in_specs=[SMALL, WHOLE, THERE],
        out_specs=WHOLE,
        compiler_params=params(VMEM),
        cost_estimate=cost(4 * FRAMES * SLAB * LANES * 256, 6 * FRAMES * SLAB * LANES),
        name="choose",
    )(key_list, in_vmem(slab), in_hbm(after))


LARGE = 1e30


def attend_kernel(
    slab_ref, q_hbm, mixed_hbm, stat_hbm, weight_hbm, wo_hbm, video_hbm,
    spatial_hbm, out_slab_ref,
    spatial_ref, rows_ref, heads_ref, most_ref, q_ref, mixed_ref, stat_ref,
    wk_ref, wv_ref, wo_ref, video_ref, sems, last_sems, out_sems,
):
    def copies(group):
        pairs = (
            (weight_hbm.at[:, group_lanes(group, GROUP, WIDTH)], wk_ref),
            (weight_hbm.at[:, group_lanes(group, GROUP, 2 * WIDTH)], wv_ref),
            (q_hbm.at[:, group_lanes(group, GROUP)], q_ref),
            (mixed_hbm.at[group], mixed_ref),
            (stat_hbm.at[group], stat_ref),
        )
        return [
            pltpu.make_async_copy(source, target.at[group], sems.at[i, group])
            for i, (source, target) in enumerate(pairs)
        ]

    last = (
        pltpu.make_async_copy(wo_hbm, wo_ref, last_sems.at[0]),
        pltpu.make_async_copy(video_hbm, video_ref, last_sems.at[1]),
    )
    for group in range(GROUPS):
        for copy in copies(group):
            copy.start()
    for copy in last:
        copy.start()

    swap = swap_matrix()
    for which in range(2):
        slab_to_rows(
            lambda block, half: slab_ref[
                16 * block : 16 * block + 16, which, 16 * half : 16 * half + 16, :
            ],
            rows_ref, swap, which * TOK,
        )
    most_ref[...] = jnp.zeros_like(most_ref)

    def project_group(group):
        rows = rows_ref[...]
        keys = jnp.dot(rows, wk_ref[group], preferred_element_type=f32).astype(bf16)
        values = jnp.dot(rows, wv_ref[group], preferred_element_type=f32).astype(bf16)
        return keys, values.T

    def score_group(group, keys):
        scores = []
        for head in range(4):
            lanes = slice(head // 2 * LANES, (head // 2 + 1) * LANES)
            scores.append(flipped_scores(q_ref[group, :, lanes], keys[:, lanes], head % 2))
        return scores

    def mix_group(group, weights, values, less):
        made, totals = [], []
        for head in range(4):
            rows = slice(head * HEAD, (head + 1) * HEAD)
            out = jnp.dot(with_ones(values[rows]), weights[head], preferred_element_type=f32)
            mixed, total = mixed_ref[group, rows, :], stat_ref[group, 4 + head : 5 + head, :]
            if less is not None:
                mixed, total = mixed * less[head], total * less[head]
            mixed, total = mixed + out[:HEAD], total + out[HEAD : HEAD + 1]
            made.append((mixed / total).astype(bf16))
            totals.append(total)
        heads_ref[group] = jnp.concatenate(made, axis=0).T
        return totals

    @pl.loop(0, GROUPS)
    def _(group):
        arriving = copies(group)
        for copy in arriving[:2]:
            copy.wait()
        keys, values = project_group(group)
        for copy in arriving[2:]:
            copy.wait()
        scores = score_group(group, keys)
        weights = [
            jnp.exp2(scores[head] - stat_ref[group, head : head + 1, :]).astype(bf16)
            for head in range(4)
        ]
        for total in mix_group(group, weights, values, None):
            most_ref[...] = jnp.maximum(most_ref[...], total)

    @pl.when(jnp.logical_not(jnp.max(most_ref[...]) < LARGE))
    def _():
        @pl.loop(0, GROUPS)
        def _(group):
            keys, values = project_group(group)
            scores = score_group(group, keys)
            own = [stat_ref[group, head : head + 1, :] for head in range(4)]
            tops = [
                jnp.maximum(top, jnp.max(s, axis=0, keepdims=True)) for s, top in zip(scores, own)
            ]
            weights = [jnp.exp2(s - top).astype(bf16) for s, top in zip(scores, tops)]
            mix_group(group, weights, values, [jnp.exp2(o - top) for o, top in zip(own, tops)])

    given = []
    for copy in last:
        copy.wait()
    for k in range(PARTS):
        rows = pl.ds(k * FRAMES, FRAMES)
        heads = jnp.concatenate([heads_ref[g, rows, :] for g in range(GROUPS)], axis=1)
        added = jnp.dot(heads, wo_ref[...], preferred_element_type=f32)
        spatial_ref[rows, :] = (video_ref[rows, :].astype(f32) + added).astype(bf16)
        given.append(
            pltpu.make_async_copy(spatial_ref.at[rows], spatial_hbm.at[rows], out_sems.at[k])
        )
        given[-1].start()
    rows_to_slab(tiles_of(spatial_ref), out_slab_ref, swap)
    for copy in given:
        copy.wait()


def attend(slab, queries, mixed, stat, weight, out_weight, video):
    return pl.pallas_call(
        attend_kernel,
        out_shape=(
            jax.ShapeDtypeStruct((TOK, WIDTH), bf16),
            pltpu.VMEM((FRAMES, SLAB, LANES), bf16),
        ),
        in_specs=[WHOLE] + [THERE] * 6,
        out_specs=(THERE, WHOLE),
        scratch_shapes=[
            pltpu.VMEM((TOK, WIDTH), bf16),
            pltpu.VMEM((2 * TOK, WIDTH), bf16),
            pltpu.VMEM((GROUPS, TOK, GROUP), bf16),
            pltpu.VMEM((1, TOK), f32),
            pltpu.VMEM((GROUPS, TOK, GROUP), bf16),
            pltpu.VMEM((GROUPS, GROUP, TOK), f32),
            pltpu.VMEM((GROUPS, 8, TOK), f32),
            pltpu.VMEM((GROUPS, WIDTH, GROUP), bf16),
            pltpu.VMEM((GROUPS, WIDTH, GROUP), bf16),
            pltpu.VMEM((WIDTH, WIDTH), bf16),
            pltpu.VMEM((TOK, WIDTH), bf16),
            pltpu.SemaphoreType.DMA((5, GROUPS)),
            pltpu.SemaphoreType.DMA((2,)),
            pltpu.SemaphoreType.DMA((PARTS,)),
        ],
        compiler_params=params(VMEM),
        cost_estimate=cost(
            8 * TOK * WIDTH * WIDTH + 16 * TOK * TOK * WIDTH,
            6 * WIDTH * WIDTH + 20 * TOK * WIDTH,
            2 * HEADS * TOK * TOK,
        ),
        name="attend",
    )(
        in_vmem(slab), in_hbm(queries), in_hbm(mixed), in_hbm(stat),
        in_hbm(weight), in_hbm(out_weight), in_hbm(video),
    )


def time_kernel(
    slab_ref, gain_ref, weight_hbm, out_slab_ref, rows_ref, heads_ref, weight_ref, sems
):
    for group in range(GROUPS):
        for copy in group_copies(weight_hbm, weight_ref, sems, group):
            copy.start()
    swap = swap_matrix()
    slab_to_rows(
        lambda block, half: slab_ref[16 * block : 16 * block + 16, 16 * half : 16 * half + 16, :],
        rows_ref, swap,
    )
    for k in range(PARTS):
        rows = pl.ds(k * FRAMES, FRAMES)
        rows_ref[rows, :] = norm_rows(rows_ref[rows, :].astype(f32), gain_ref[...].reshape(1, WIDTH))

    @pl.loop(0, GROUPS)
    def _(group):
        for copy in group_copies(weight_hbm, weight_ref, sems, group):
            copy.wait()
        rows = rows_ref[...]
        made = [
            jnp.dot(rows, weight_ref[which, group], preferred_element_type=f32)
            for which in range(3)
        ]
        queries, keys, values = (made[0] * SCALE).astype(bf16), made[1].astype(bf16), made[2]
        units, places = [], []
        for pair in range(2):
            lanes = slice(pair * LANES, (pair + 1) * LANES)
            for k in range(PARTS):
                at = slice(k * FRAMES, (k + 1) * FRAMES)
                units.append((queries[at, lanes], keys[at, lanes], values[at, lanes], None))
                places.append((pair, at))
        for (pair, at), (mixed, total, _) in zip(places, attend_pairs(units)):
            heads_ref[2 * group + pair, at, :] = (mixed / total).astype(bf16)

    rows_to_slab(lambda at, g: heads_ref[g, at : at + 16, :], out_slab_ref, swap)


def time_attend(slab, gain, weight):
    return pl.pallas_call(
        time_kernel,
        out_shape=pltpu.VMEM((FRAMES, SLAB, LANES), bf16),
        in_specs=[WHOLE, WHOLE, THERE],
        out_specs=WHOLE,
        scratch_shapes=[
            pltpu.VMEM((TOK, WIDTH), bf16),
            pltpu.VMEM((COLS, TOK, LANES), bf16),
            pltpu.VMEM((3, GROUPS, WIDTH, GROUP), bf16),
            pltpu.SemaphoreType.DMA((3, GROUPS)),
        ],
        compiler_params=params(VMEM),
        cost_estimate=cost(
            6 * TOK * WIDTH * WIDTH + 8 * TOK * FRAMES * WIDTH,
            6 * WIDTH * WIDTH + 4 * TOK * WIDTH,
            HEADS * TOK * FRAMES,
        ),
        name="time_attend",
    )(in_vmem(slab), in_hbm(gain), in_hbm(weight))


def unpack_kernel(slab_ref, out_hbm, out_ref, sems):
    swap = swap_matrix()
    copies = []
    for part in range(4):
        slab_to_rows(
            lambda block, half: slab_ref[
                16 * block : 16 * block + 16, 16 * half : 16 * half + 16, :
            ],
            out_ref, swap, blocks=(2 * part, 2 * part + 1),
        )
        for k in range(PARTS):
            some = pl.ds(k * FRAMES + 32 * part, 32)
            copies.append(
                pltpu.make_async_copy(out_ref.at[some], out_hbm.at[some], sems.at[len(copies)])
            )
            copies[-1].start()
    for copy in copies:
        copy.wait()


def unpack(slab):
    return pl.pallas_call(
        unpack_kernel,
        out_shape=jax.ShapeDtypeStruct((TOK, WIDTH), bf16),
        in_specs=[WHOLE],
        out_specs=THERE,
        scratch_shapes=[pltpu.VMEM((TOK, WIDTH), bf16), pltpu.SemaphoreType.DMA((4 * PARTS,))],
        compiler_params=params(VMEM),
        cost_estimate=cost(2 * TOK * WIDTH * 256, 4 * TOK * WIDTH),
        name="unpack",
    )(in_vmem(slab))


def exchange(slab):
    return lax.all_to_all(slab, "frame", split_axis=0, concat_axis=0, tiled=True)


def body(video, key_list, pairs, norm_gain, qkv_weight, out_weight, time_gain, time_weight):
    spread = exchange(prep(pairs, video, norm_gain))
    queries, mixed, stat = own_attend(video, norm_gain, qkv_weight)
    wanted = exchange(choose(key_list, spread, queries))
    spatial, slab = attend(wanted, queries, mixed, stat, qkv_weight, out_weight, video)
    slab = time_attend(exchange(slab), time_gain, time_weight)
    return spatial, unpack(exchange(slab))


def solution(mesh):
    return jax.shard_map(
        body,
        mesh=mesh,
        in_specs=(P("frame", None), P(), P("frame", None), P(), P(), P(), P(), P()),
        out_specs=(P("frame", None), P("frame", None)),
        check_vma=False,
    )
```

```python
import jax
import jax.numpy as jnp
from jax import lax
from jax.experimental import pallas as pl
from jax.experimental.pallas import tpu as pltpu
from jax.sharding import PartitionSpec as P

WIDTH = 1280
HEADS = 20
HEAD = 64
TOK = 384
FRAMES = 128
KEYS = 8
PARTS = TOK // FRAMES
LANES = 128
COLS = WIDTH // LANES
SLAB = 32
GROUP = 256
GROUPS = WIDTH // GROUP
VMEM = 52
SCALE = 0.125 * 1.4426950408889634

bf16 = jnp.bfloat16
f32 = jnp.float32


def params(mib, **more):
    return pltpu.CompilerParams(vmem_limit_bytes=mib << 20, **more)


def cost(flops, moved, exps=0):
    return pl.CostEstimate(flops=int(flops), bytes_accessed=int(moved), transcendentals=int(exps))


def in_vmem(x):
    return pltpu.with_memory_space_constraint(x, pltpu.VMEM)


def in_hbm(x):
    return pltpu.with_memory_space_constraint(x, pltpu.HBM)


WHOLE = pl.BlockSpec(memory_space=pltpu.VMEM)
THERE = pl.BlockSpec(memory_space=pl.ANY)
SMALL = pl.BlockSpec(memory_space=pltpu.SMEM)


def norm_rows(values, gain):
    centred = values - jnp.mean(values, axis=-1, keepdims=True)
    spread = jnp.mean(centred * centred, axis=-1, keepdims=True)
    return (centred * lax.rsqrt(spread + 1e-05) * gain).astype(bf16)


def swap_matrix():
    row = lax.broadcasted_iota(jnp.int32, (256, 256), 0)
    col = lax.broadcasted_iota(jnp.int32, (256, 256), 1)
    return jnp.where(col == (row % 16) * 16 + row // 16, 1.0, 0.0).astype(bf16)


def rows_to_slab(tile, slab_ref, swap, spare=None, halves=(0, 1)):
    for half in halves:
        for pair in range(4):
            sides = []
            for block in (2 * pair, 2 * pair + 1):
                tiles = []
                for unit in range(16 * half, 16 * half + 16):
                    k, g = divmod(unit, COLS)
                    if k < PARTS:
                        tiles.append(tile(k * FRAMES + 16 * block, g))
                    elif spare is None:
                        tiles.append(jnp.zeros((16, LANES), bf16))
                    else:
                        tiles.append(spare[unit - PARTS * COLS])
                sides.append(jnp.concatenate(tiles, axis=0))
            both = jnp.concatenate(sides, axis=1)
            moved = jnp.dot(swap, both, preferred_element_type=f32).astype(bf16)
            for side in range(2):
                block = 2 * pair + side
                slab_ref[16 * block : 16 * block + 16, 16 * half : 16 * half + 16, :] = moved[
                    :, side * LANES : (side + 1) * LANES
                ].reshape(16, 16, LANES)


def tiles_of(rows_ref):
    return lambda at, g: rows_ref[at : at + 16, g * LANES : (g + 1) * LANES]


def slab_to_rows(load, rows_ref, swap, first=0, blocks=range(8)):
    for block in blocks:
        both = jnp.concatenate(
            [load(block, half).reshape(256, LANES) for half in range(2)], axis=1
        )
        moved = jnp.dot(swap, both, preferred_element_type=f32).astype(bf16)
        for unit in range(PARTS * COLS):
            half, row = divmod(unit, 16)
            k, g = divmod(unit, COLS)
            at = first + k * FRAMES + 16 * block
            rows_ref[at : at + 16, g * LANES : (g + 1) * LANES] = moved[
                16 * row : 16 * row + 16, half * LANES : (half + 1) * LANES
            ]


def prep_kernel(pairs_ref, video_ref, gain_ref, slab_ref, normed_ref):
    gain = gain_ref[...].reshape(1, WIDTH)
    for k in range(PARTS):
        rows = pl.ds(k * FRAMES, FRAMES)
        normed_ref[rows, :] = norm_rows(video_ref[rows, :].astype(f32), gain)
    spare = [
        jnp.full((16, LANES), pairs_ref[0, which], jnp.int32).astype(f32).astype(bf16)
        for which in range(2)
    ]
    rows_to_slab(tiles_of(normed_ref), slab_ref, swap_matrix(), spare)


def prep(pairs, video, gain):
    return pl.pallas_call(
        prep_kernel,
        out_shape=pltpu.VMEM((FRAMES, SLAB, LANES), bf16),
        in_specs=[SMALL, WHOLE, WHOLE],
        out_specs=WHOLE,
        scratch_shapes=[pltpu.VMEM((TOK, WIDTH), bf16)],
        compiler_params=params(VMEM),
        cost_estimate=cost(6 * TOK * WIDTH, 4 * TOK * WIDTH),
        name="prep",
    )(in_hbm(pairs), in_hbm(video), in_hbm(gain))


def low_lanes(rows):
    return lax.broadcasted_iota(jnp.int32, (rows, LANES), 1) < HEAD


def attend_pairs(units):
    scores, padded = [], []
    for queries, keys, values, _ in units:
        low_q, low_v = low_lanes(queries.shape[0]), low_lanes(values.shape[0])
        wide = queries.astype(f32)
        for head in range(2):
            mine = jnp.where(low_q, wide, 0.0) if head == 0 else jnp.where(low_q, 0.0, wide)
            rest = jnp.where(low_v, values, 1.0) if head == 0 else jnp.where(low_v, 1.0, values)
            padded.append(rest.astype(bf16))
            scores.append(
                lax.dot_general(
                    mine.astype(bf16), keys, (((1,), (1,)), ((), ())), preferred_element_type=f32
                )
            )
    tops = [jnp.max(s, axis=-1, keepdims=True) for s in scores]
    for i, (_, _, _, top) in enumerate(units):
        if top is not None:
            for head in range(2):
                other = top[:, head * HEAD : head * HEAD + 1]
                tops[2 * i + head] = jnp.maximum(tops[2 * i + head], other)
    weights = [jnp.exp2(s - top).astype(bf16) for s, top in zip(scores, tops)]
    outs = [jnp.dot(w, v, preferred_element_type=f32) for w, v in zip(weights, padded)]
    given = []
    for i, (queries, _, _, _) in enumerate(units):
        low = low_lanes(queries.shape[0])
        one, two = outs[2 * i], outs[2 * i + 1]
        total = pltpu.roll(jnp.where(low, two, one), HEAD, 1)
        given.append((jnp.where(low, one, two), total, tops[2 * i : 2 * i + 2]))
    return given


def group_lanes(group, size, offset=0):
    return pl.ds(pl.multiple_of(offset + group * GROUP, LANES), size)


def flipped_scores(queries, keys, head):
    low = low_lanes(queries.shape[0])
    wide = queries.astype(f32)
    mine = jnp.where(low, wide, 0.0) if head == 0 else jnp.where(low, 0.0, wide)
    return lax.dot_general(
        keys, mine.astype(bf16), (((1,), (1,)), ((), ())), preferred_element_type=f32
    )


def with_ones(values):
    return jnp.concatenate([values, jnp.ones((16, values.shape[1]), bf16)], axis=0)


def group_copies(weight_hbm, weight_ref, sems, group):
    return [
        pltpu.make_async_copy(
            weight_hbm.at[:, group_lanes(group, GROUP, which * WIDTH)],
            weight_ref.at[which, group],
            sems.at[which, group],
        )
        for which in range(3)
    ]


def own_kernel(
    video_ref, gain_ref, weight_hbm, after_ref, q_ref, mixed_ref, stat_ref, rows_ref, weight_ref, sems
):
    del after_ref
    for group in range(GROUPS):
        for copy in group_copies(weight_hbm, weight_ref, sems, group):
            copy.start()
    gain = gain_ref[...].reshape(1, WIDTH)
    for k in range(PARTS):
        rows = pl.ds(k * FRAMES, FRAMES)
        rows_ref[rows, :] = norm_rows(video_ref[rows, :].astype(f32), gain)

    @pl.loop(0, GROUPS)
    def _(group):
        for copy in group_copies(weight_hbm, weight_ref, sems, group):
            copy.wait()
        rows = rows_ref[...]
        queries, keys, values = [
            jnp.dot(rows, weight_ref[which, group], preferred_element_type=f32)
            for which in range(3)
        ]
        queries, keys, values = (queries * SCALE).astype(bf16), keys.astype(bf16), values.astype(bf16).T
        q_ref[:, group_lanes(group, GROUP)] = queries
        scores = []
        for head in range(4):
            lanes = slice(head // 2 * LANES, (head // 2 + 1) * LANES)
            scores.append(flipped_scores(queries[:, lanes], keys[:, lanes], head % 2))
        tops = [jnp.max(s, axis=0, keepdims=True) for s in scores]
        weights = [jnp.exp2(s - top).astype(bf16) for s, top in zip(scores, tops)]
        for head in range(4):
            rows = slice(head * HEAD, (head + 1) * HEAD)
            out = jnp.dot(with_ones(values[rows]), weights[head], preferred_element_type=f32)
            mixed_ref[group, rows, :] = out[:HEAD]
            stat_ref[group, head : head + 1, :] = tops[head]
            stat_ref[group, 4 + head : 5 + head, :] = out[HEAD : HEAD + 1]


def own_attend(video, gain, weight, after):
    return pl.pallas_call(
        own_kernel,
        out_shape=(
            pltpu.HBM((TOK, WIDTH), bf16),
            pltpu.HBM((GROUPS, GROUP, TOK), f32),
            pltpu.HBM((GROUPS, 8, TOK), f32),
        ),
        in_specs=[WHOLE, WHOLE, THERE, THERE],
        out_specs=(WHOLE, WHOLE, WHOLE),
        scratch_shapes=[
            pltpu.VMEM((TOK, WIDTH), bf16),
            pltpu.VMEM((3, GROUPS, WIDTH, GROUP), bf16),
            pltpu.SemaphoreType.DMA((3, GROUPS)),
        ],
        compiler_params=params(VMEM),
        cost_estimate=cost(
            6 * TOK * WIDTH * WIDTH + 8 * TOK * TOK * WIDTH,
            6 * WIDTH * WIDTH + 10 * TOK * WIDTH,
            HEADS * TOK * TOK,
        ),
        name="own_attend",
    )(in_hbm(video), in_hbm(gain), in_hbm(weight), in_hbm(after))


def choose_kernel(key_list_ref, slab_ref, out_hbm, out_ref, sems):
    copies = []
    halves = [
        jnp.concatenate([slab_ref[key_list_ref[s], at : at + 16, :] for s in range(KEYS)], axis=0)
        for at in (0, 16)
    ]
    keys = jnp.concatenate(halves, axis=1)
    row = lax.broadcasted_iota(jnp.int32, (16, LANES), 0)
    col = lax.broadcasted_iota(jnp.int32, (16, LANES), 1)
    slot = jnp.where(col % 16 == row, col // 16, -1).astype(f32)
    for f in range(0, FRAMES, 8):
        picks = []
        for more in range(8):
            spare = slab_ref[f + more, 16:32, :].astype(f32)
            for which in range(2):
                wanted = spare[14 + which : 15 + which, :]
                picks.append(jnp.where(slot == wanted, 1.0, 0.0).astype(bf16))
        chosen = jnp.dot(jnp.concatenate(picks, axis=0), keys, preferred_element_type=f32)
        chosen = chosen.astype(bf16).reshape(8, 2, 16, 2 * LANES)
        out_ref[f : f + 8, :, 0:16, :] = chosen[..., :LANES]
        out_ref[f : f + 8, :, 16:32, :] = chosen[..., LANES:]
        if (f + 8) % 32 == 0:
            some = pl.ds(f - 24, 32)
            copies.append(
                pltpu.make_async_copy(out_ref.at[some], out_hbm.at[some], sems.at[len(copies)])
            )
            copies[-1].start()
    for copy in copies:
        copy.wait()


def choose(key_list, slab):
    return pl.pallas_call(
        choose_kernel,
        out_shape=pltpu.HBM((FRAMES, 2, SLAB, LANES), bf16),
        in_specs=[SMALL, WHOLE],
        out_specs=THERE,
        scratch_shapes=[
            pltpu.VMEM((FRAMES, 2, SLAB, LANES), bf16),
            pltpu.SemaphoreType.DMA((4,)),
        ],
        compiler_params=params(VMEM),
        cost_estimate=cost(4 * FRAMES * SLAB * LANES * 256, 6 * FRAMES * SLAB * LANES),
        name="choose",
    )(key_list, in_vmem(slab))


LARGE = 1e30


def attend_kernel(
    slab_ref, q_hbm, mixed_hbm, stat_hbm, weight_hbm, wo_hbm, video_hbm,
    spatial_hbm, out_slab_ref,
    spatial_ref, rows_ref, heads_ref, most_ref, q_ref, mixed_ref, stat_ref,
    wk_ref, wv_ref, wo_ref, video_ref, sems, last_sems, out_sems,
):
    def copies(group):
        pairs = (
            (weight_hbm.at[:, group_lanes(group, GROUP, WIDTH)], wk_ref),
            (weight_hbm.at[:, group_lanes(group, GROUP, 2 * WIDTH)], wv_ref),
            (q_hbm.at[:, group_lanes(group, GROUP)], q_ref),
            (mixed_hbm.at[group], mixed_ref),
            (stat_hbm.at[group], stat_ref),
        )
        return [
            pltpu.make_async_copy(source, target.at[group], sems.at[i, group])
            for i, (source, target) in enumerate(pairs)
        ]

    last = (
        pltpu.make_async_copy(wo_hbm, wo_ref, last_sems.at[0]),
        pltpu.make_async_copy(video_hbm, video_ref, last_sems.at[1]),
    )
    for group in range(GROUPS):
        for copy in copies(group):
            copy.start()
    for copy in last:
        copy.start()

    swap = swap_matrix()
    for which in range(2):
        slab_to_rows(
            lambda block, half: slab_ref[
                16 * block : 16 * block + 16, which, 16 * half : 16 * half + 16, :
            ],
            rows_ref, swap, which * TOK,
        )
    most_ref[...] = jnp.zeros_like(most_ref)

    def project_group(group):
        rows = rows_ref[...]
        keys = jnp.dot(rows, wk_ref[group], preferred_element_type=f32).astype(bf16)
        values = jnp.dot(rows, wv_ref[group], preferred_element_type=f32).astype(bf16)
        return keys, values.T

    def score_group(group, keys):
        scores = []
        for head in range(4):
            lanes = slice(head // 2 * LANES, (head // 2 + 1) * LANES)
            scores.append(flipped_scores(q_ref[group, :, lanes], keys[:, lanes], head % 2))
        return scores

    def mix_group(group, weights, values, less):
        made, totals = [], []
        for head in range(4):
            rows = slice(head * HEAD, (head + 1) * HEAD)
            out = jnp.dot(with_ones(values[rows]), weights[head], preferred_element_type=f32)
            mixed, total = mixed_ref[group, rows, :], stat_ref[group, 4 + head : 5 + head, :]
            if less is not None:
                mixed, total = mixed * less[head], total * less[head]
            mixed, total = mixed + out[:HEAD], total + out[HEAD : HEAD + 1]
            made.append((mixed / total).astype(bf16))
            totals.append(total)
        heads_ref[group] = jnp.concatenate(made, axis=0).T
        return totals

    @pl.loop(0, GROUPS)
    def _(group):
        arriving = copies(group)
        for copy in arriving[:2]:
            copy.wait()
        keys, values = project_group(group)
        for copy in arriving[2:]:
            copy.wait()
        scores = score_group(group, keys)
        weights = [
            jnp.exp2(scores[head] - stat_ref[group, head : head + 1, :]).astype(bf16)
            for head in range(4)
        ]
        for total in mix_group(group, weights, values, None):
            most_ref[...] = jnp.maximum(most_ref[...], total)

    @pl.when(jnp.logical_not(jnp.max(most_ref[...]) < LARGE))
    def _():
        @pl.loop(0, GROUPS)
        def _(group):
            keys, values = project_group(group)
            scores = score_group(group, keys)
            own = [stat_ref[group, head : head + 1, :] for head in range(4)]
            tops = [
                jnp.maximum(top, jnp.max(s, axis=0, keepdims=True)) for s, top in zip(scores, own)
            ]
            weights = [jnp.exp2(s - top).astype(bf16) for s, top in zip(scores, tops)]
            mix_group(group, weights, values, [jnp.exp2(o - top) for o, top in zip(own, tops)])

    given = []
    for copy in last:
        copy.wait()
    for k in range(PARTS):
        rows = pl.ds(k * FRAMES, FRAMES)
        heads = jnp.concatenate([heads_ref[g, rows, :] for g in range(GROUPS)], axis=1)
        added = jnp.dot(heads, wo_ref[...], preferred_element_type=f32)
        spatial_ref[rows, :] = (video_ref[rows, :].astype(f32) + added).astype(bf16)
        given.append(
            pltpu.make_async_copy(spatial_ref.at[rows], spatial_hbm.at[rows], out_sems.at[k])
        )
        given[-1].start()
    rows_to_slab(tiles_of(spatial_ref), out_slab_ref, swap)
    for copy in given:
        copy.wait()


def attend(slab, queries, mixed, stat, weight, out_weight, video):
    return pl.pallas_call(
        attend_kernel,
        out_shape=(
            jax.ShapeDtypeStruct((TOK, WIDTH), bf16),
            pltpu.VMEM((FRAMES, SLAB, LANES), bf16),
        ),
        in_specs=[WHOLE] + [THERE] * 6,
        out_specs=(THERE, WHOLE),
        scratch_shapes=[
            pltpu.VMEM((TOK, WIDTH), bf16),
            pltpu.VMEM((2 * TOK, WIDTH), bf16),
            pltpu.VMEM((GROUPS, TOK, GROUP), bf16),
            pltpu.VMEM((1, TOK), f32),
            pltpu.VMEM((GROUPS, TOK, GROUP), bf16),
            pltpu.VMEM((GROUPS, GROUP, TOK), f32),
            pltpu.VMEM((GROUPS, 8, TOK), f32),
            pltpu.VMEM((GROUPS, WIDTH, GROUP), bf16),
            pltpu.VMEM((GROUPS, WIDTH, GROUP), bf16),
            pltpu.VMEM((WIDTH, WIDTH), bf16),
            pltpu.VMEM((TOK, WIDTH), bf16),
            pltpu.SemaphoreType.DMA((5, GROUPS)),
            pltpu.SemaphoreType.DMA((2,)),
            pltpu.SemaphoreType.DMA((PARTS,)),
        ],
        compiler_params=params(VMEM),
        cost_estimate=cost(
            8 * TOK * WIDTH * WIDTH + 16 * TOK * TOK * WIDTH,
            6 * WIDTH * WIDTH + 20 * TOK * WIDTH,
            2 * HEADS * TOK * TOK,
        ),
        name="attend",
    )(
        in_vmem(slab), in_hbm(queries), in_hbm(mixed), in_hbm(stat),
        in_hbm(weight), in_hbm(out_weight), in_hbm(video),
    )


def time_kernel(
    slab_ref, gain_ref, weight_hbm, out_slab_ref, rows_ref, heads_ref, weight_ref, sems
):
    for group in range(GROUPS):
        for copy in group_copies(weight_hbm, weight_ref, sems, group):
            copy.start()
    swap = swap_matrix()
    slab_to_rows(
        lambda block, half: slab_ref[16 * block : 16 * block + 16, 16 * half : 16 * half + 16, :],
        rows_ref, swap,
    )
    for k in range(PARTS):
        rows = pl.ds(k * FRAMES, FRAMES)
        rows_ref[rows, :] = norm_rows(rows_ref[rows, :].astype(f32), gain_ref[...].reshape(1, WIDTH))

    @pl.loop(0, GROUPS)
    def _(group):
        for copy in group_copies(weight_hbm, weight_ref, sems, group):
            copy.wait()
        rows = rows_ref[...]
        made = [
            jnp.dot(rows, weight_ref[which, group], preferred_element_type=f32)
            for which in range(3)
        ]
        queries, keys, values = (made[0] * SCALE).astype(bf16), made[1].astype(bf16), made[2]
        units, places = [], []
        for pair in range(2):
            lanes = slice(pair * LANES, (pair + 1) * LANES)
            for k in range(PARTS):
                at = slice(k * FRAMES, (k + 1) * FRAMES)
                units.append((queries[at, lanes], keys[at, lanes], values[at, lanes], None))
                places.append((pair, at))
        for (pair, at), (mixed, total, _) in zip(places, attend_pairs(units)):
            heads_ref[2 * group + pair, at, :] = (mixed / total).astype(bf16)

    rows_to_slab(lambda at, g: heads_ref[g, at : at + 16, :], out_slab_ref, swap)


def time_attend(slab, gain, weight):
    return pl.pallas_call(
        time_kernel,
        out_shape=pltpu.VMEM((FRAMES, SLAB, LANES), bf16),
        in_specs=[WHOLE, WHOLE, THERE],
        out_specs=WHOLE,
        scratch_shapes=[
            pltpu.VMEM((TOK, WIDTH), bf16),
            pltpu.VMEM((COLS, TOK, LANES), bf16),
            pltpu.VMEM((3, GROUPS, WIDTH, GROUP), bf16),
            pltpu.SemaphoreType.DMA((3, GROUPS)),
        ],
        compiler_params=params(VMEM),
        cost_estimate=cost(
            6 * TOK * WIDTH * WIDTH + 8 * TOK * FRAMES * WIDTH,
            6 * WIDTH * WIDTH + 4 * TOK * WIDTH,
            HEADS * TOK * FRAMES,
        ),
        name="time_attend",
    )(in_vmem(slab), in_hbm(gain), in_hbm(weight))


def unpack_kernel(slab_ref, out_hbm, out_ref, sems):
    swap = swap_matrix()
    copies = []
    for part in range(4):
        slab_to_rows(
            lambda block, half: slab_ref[
                16 * block : 16 * block + 16, 16 * half : 16 * half + 16, :
            ],
            out_ref, swap, blocks=(2 * part, 2 * part + 1),
        )
        for k in range(PARTS):
            some = pl.ds(k * FRAMES + 32 * part, 32)
            copies.append(
                pltpu.make_async_copy(out_ref.at[some], out_hbm.at[some], sems.at[len(copies)])
            )
            copies[-1].start()
    for copy in copies:
        copy.wait()


def unpack(slab):
    return pl.pallas_call(
        unpack_kernel,
        out_shape=jax.ShapeDtypeStruct((TOK, WIDTH), bf16),
        in_specs=[WHOLE],
        out_specs=THERE,
        scratch_shapes=[pltpu.VMEM((TOK, WIDTH), bf16), pltpu.SemaphoreType.DMA((4 * PARTS,))],
        compiler_params=params(VMEM),
        cost_estimate=cost(2 * TOK * WIDTH * 256, 4 * TOK * WIDTH),
        name="unpack",
    )(in_vmem(slab))


def exchange(slab):
    return lax.all_to_all(slab, "frame", split_axis=0, concat_axis=0, tiled=True)


def body(video, key_list, pairs, norm_gain, qkv_weight, out_weight, time_gain, time_weight):
    chosen = choose(key_list, exchange(prep(pairs, video, norm_gain)))
    wanted = exchange(chosen)
    queries, mixed, stat = own_attend(video, norm_gain, qkv_weight, chosen)
    spatial, slab = attend(wanted, queries, mixed, stat, qkv_weight, out_weight, video)
    slab = time_attend(exchange(slab), time_gain, time_weight)
    return spatial, unpack(exchange(slab))


def solution(mesh):
    return jax.shard_map(
        body,
        mesh=mesh,
        in_specs=(P("frame", None), P(), P("frame", None), P(), P(), P(), P(), P()),
        out_specs=(P("frame", None), P("frame", None)),
        check_vma=False,
    )
```

```python
import jax
import jax.numpy as jnp
from jax import lax
from jax.experimental import pallas as pl
from jax.experimental.pallas import tpu as pltpu
from jax.sharding import PartitionSpec as P

WIDTH = 1280
HEADS = 20
HEAD = 64
TOK = 384
FRAMES = 128
KEYS = 8
PARTS = TOK // FRAMES
LANES = 128
COLS = WIDTH // LANES
SLAB = 32
GROUP = 256
GROUPS = WIDTH // GROUP
VMEM = 52
SCALE = 0.125 * 1.4426950408889634

bf16 = jnp.bfloat16
f32 = jnp.float32


def params(mib, **more):
    return pltpu.CompilerParams(vmem_limit_bytes=mib << 20, **more)


def cost(flops, moved, exps=0):
    return pl.CostEstimate(flops=int(flops), bytes_accessed=int(moved), transcendentals=int(exps))


def in_vmem(x):
    return pltpu.with_memory_space_constraint(x, pltpu.VMEM)


def in_hbm(x):
    return pltpu.with_memory_space_constraint(x, pltpu.HBM)


WHOLE = pl.BlockSpec(memory_space=pltpu.VMEM)
THERE = pl.BlockSpec(memory_space=pl.ANY)
SMALL = pl.BlockSpec(memory_space=pltpu.SMEM)


def norm_rows(values, gain):
    centred = values - jnp.mean(values, axis=-1, keepdims=True)
    spread = jnp.mean(centred * centred, axis=-1, keepdims=True)
    return (centred * lax.rsqrt(spread + 1e-05) * gain).astype(bf16)


def swap_matrix():
    row = lax.broadcasted_iota(jnp.int32, (256, 256), 0)
    col = lax.broadcasted_iota(jnp.int32, (256, 256), 1)
    return jnp.where(col == (row % 16) * 16 + row // 16, 1.0, 0.0).astype(bf16)


def rows_to_slab(tile, slab_ref, swap, spare=None, halves=(0, 1)):
    for half in halves:
        for pair in range(4):
            sides = []
            for block in (2 * pair, 2 * pair + 1):
                tiles = []
                for unit in range(16 * half, 16 * half + 16):
                    k, g = divmod(unit, COLS)
                    if k < PARTS:
                        tiles.append(tile(k * FRAMES + 16 * block, g))
                    elif spare is None:
                        tiles.append(jnp.zeros((16, LANES), bf16))
                    else:
                        tiles.append(spare[unit - PARTS * COLS])
                sides.append(jnp.concatenate(tiles, axis=0))
            both = jnp.concatenate(sides, axis=1)
            moved = jnp.dot(swap, both, preferred_element_type=f32).astype(bf16)
            for side in range(2):
                block = 2 * pair + side
                slab_ref[16 * block : 16 * block + 16, 16 * half : 16 * half + 16, :] = moved[
                    :, side * LANES : (side + 1) * LANES
                ].reshape(16, 16, LANES)


def tiles_of(rows_ref):
    return lambda at, g: rows_ref[at : at + 16, g * LANES : (g + 1) * LANES]


def slab_to_rows(load, rows_ref, swap, first=0, blocks=range(8)):
    for block in blocks:
        both = jnp.concatenate(
            [load(block, half).reshape(256, LANES) for half in range(2)], axis=1
        )
        moved = jnp.dot(swap, both, preferred_element_type=f32).astype(bf16)
        for unit in range(PARTS * COLS):
            half, row = divmod(unit, 16)
            k, g = divmod(unit, COLS)
            at = first + k * FRAMES + 16 * block
            rows_ref[at : at + 16, g * LANES : (g + 1) * LANES] = moved[
                16 * row : 16 * row + 16, half * LANES : (half + 1) * LANES
            ]


def prep_kernel(pairs_ref, video_ref, gain_ref, slab_hbm, normed_ref, slab_ref, sems):
    swap = swap_matrix()
    gain = gain_ref[...].reshape(1, WIDTH)
    spare = [
        jnp.full((16, LANES), pairs_ref[0, which], jnp.int32).astype(f32).astype(bf16)
        for which in range(2)
    ]
    leaving = []

    def give(half):
        rows_to_slab(tiles_of(normed_ref), slab_ref, swap, spare, halves=(half,))
        some = pl.ds(16 * half, 16)
        leaving.append(
            pltpu.make_async_copy(slab_ref.at[:, some], slab_hbm.at[:, some], sems.at[half])
        )
        leaving[-1].start()

    for k in range(PARTS):
        rows = pl.ds(k * FRAMES, FRAMES)
        normed_ref[rows, :] = norm_rows(video_ref[rows, :].astype(f32), gain)
        if k == 1:
            give(0)
    give(1)
    for copy in leaving:
        copy.wait()


def prep(pairs, video, gain):
    return pl.pallas_call(
        prep_kernel,
        out_shape=pltpu.HBM((FRAMES, SLAB, LANES), bf16),
        in_specs=[SMALL, WHOLE, WHOLE],
        out_specs=THERE,
        scratch_shapes=[
            pltpu.VMEM((TOK, WIDTH), bf16),
            pltpu.VMEM((FRAMES, SLAB, LANES), bf16),
            pltpu.SemaphoreType.DMA((2,)),
        ],
        compiler_params=params(VMEM),
        cost_estimate=cost(6 * TOK * WIDTH, 4 * TOK * WIDTH),
        name="prep",
    )(in_hbm(pairs), in_hbm(video), in_hbm(gain))


def low_lanes(rows):
    return lax.broadcasted_iota(jnp.int32, (rows, LANES), 1) < HEAD


def attend_pairs(units):
    scores, padded = [], []
    for queries, keys, values, _ in units:
        low_q, low_v = low_lanes(queries.shape[0]), low_lanes(values.shape[0])
        wide = queries.astype(f32)
        for head in range(2):
            mine = jnp.where(low_q, wide, 0.0) if head == 0 else jnp.where(low_q, 0.0, wide)
            rest = jnp.where(low_v, values, 1.0) if head == 0 else jnp.where(low_v, 1.0, values)
            padded.append(rest.astype(bf16))
            scores.append(
                lax.dot_general(
                    mine.astype(bf16), keys, (((1,), (1,)), ((), ())), preferred_element_type=f32
                )
            )
    tops = [jnp.max(s, axis=-1, keepdims=True) for s in scores]
    for i, (_, _, _, top) in enumerate(units):
        if top is not None:
            for head in range(2):
                other = top[:, head * HEAD : head * HEAD + 1]
                tops[2 * i + head] = jnp.maximum(tops[2 * i + head], other)
    weights = [jnp.exp2(s - top).astype(bf16) for s, top in zip(scores, tops)]
    outs = [jnp.dot(w, v, preferred_element_type=f32) for w, v in zip(weights, padded)]
    given = []
    for i, (queries, _, _, _) in enumerate(units):
        low = low_lanes(queries.shape[0])
        one, two = outs[2 * i], outs[2 * i + 1]
        total = pltpu.roll(jnp.where(low, two, one), HEAD, 1)
        given.append((jnp.where(low, one, two), total, tops[2 * i : 2 * i + 2]))
    return given


def group_lanes(group, size, offset=0):
    return pl.ds(pl.multiple_of(offset + group * GROUP, LANES), size)


def flipped_scores(queries, keys, head):
    low = low_lanes(queries.shape[0])
    wide = queries.astype(f32)
    mine = jnp.where(low, wide, 0.0) if head == 0 else jnp.where(low, 0.0, wide)
    return lax.dot_general(
        keys, mine.astype(bf16), (((1,), (1,)), ((), ())), preferred_element_type=f32
    )


def with_ones(values):
    return jnp.concatenate([values, jnp.ones((16, values.shape[1]), bf16)], axis=0)


def group_copies(weight_hbm, weight_ref, sems, group):
    return [
        pltpu.make_async_copy(
            weight_hbm.at[:, group_lanes(group, GROUP, which * WIDTH)],
            weight_ref.at[group, :, pl.ds(which * GROUP, GROUP)],
            sems.at[which, group],
        )
        for which in range(3)
    ]


def own_kernel(
    video_ref, gain_ref, weight_hbm, q_ref, mixed_ref, stat_ref, rows_ref, weight_ref, sems
):
    for group in range(GROUPS):
        for copy in group_copies(weight_hbm, weight_ref, sems, group):
            copy.start()
    gain = gain_ref[...].reshape(1, WIDTH)
    for k in range(PARTS):
        rows = pl.ds(k * FRAMES, FRAMES)
        rows_ref[rows, :] = norm_rows(video_ref[rows, :].astype(f32), gain)

    @pl.loop(0, GROUPS)
    def _(group):
        for copy in group_copies(weight_hbm, weight_ref, sems, group):
            copy.wait()
        rows = rows_ref[...]
        made = jnp.dot(rows, weight_ref[group], preferred_element_type=f32)
        queries, keys, values = [made[:, w * GROUP : (w + 1) * GROUP] for w in range(3)]
        queries, keys, values = (queries * SCALE).astype(bf16), keys.astype(bf16), values.astype(bf16).T
        q_ref[:, group_lanes(group, GROUP)] = queries
        scores = []
        for head in range(4):
            lanes = slice(head // 2 * LANES, (head // 2 + 1) * LANES)
            scores.append(flipped_scores(queries[:, lanes], keys[:, lanes], head % 2))
        tops = [jnp.max(s, axis=0, keepdims=True) for s in scores]
        weights = [jnp.exp2(s - top).astype(bf16) for s, top in zip(scores, tops)]
        for head in range(4):
            rows = slice(head * HEAD, (head + 1) * HEAD)
            out = jnp.dot(with_ones(values[rows]), weights[head], preferred_element_type=f32)
            mixed_ref[group, rows, :] = out[:HEAD]
            stat_ref[group, head : head + 1, :] = tops[head]
            stat_ref[group, 4 + head : 5 + head, :] = out[HEAD : HEAD + 1]


def own_attend(video, gain, weight):
    return pl.pallas_call(
        own_kernel,
        out_shape=(
            pltpu.HBM((TOK, WIDTH), bf16),
            pltpu.HBM((GROUPS, GROUP, TOK), f32),
            pltpu.HBM((GROUPS, 8, TOK), f32),
        ),
        in_specs=[WHOLE, WHOLE, THERE],
        out_specs=(WHOLE, WHOLE, WHOLE),
        scratch_shapes=[
            pltpu.VMEM((TOK, WIDTH), bf16),
            pltpu.VMEM((GROUPS, WIDTH, 3 * GROUP), bf16),
            pltpu.SemaphoreType.DMA((3, GROUPS)),
        ],
        compiler_params=params(VMEM),
        cost_estimate=cost(
            6 * TOK * WIDTH * WIDTH + 8 * TOK * TOK * WIDTH,
            6 * WIDTH * WIDTH + 10 * TOK * WIDTH,
            HEADS * TOK * TOK,
        ),
        name="own_attend",
    )(in_hbm(video), in_hbm(gain), in_hbm(weight))


def choose_kernel(key_list_ref, slab_ref, after_ref, out_ref):
    del after_ref
    halves = [
        jnp.concatenate([slab_ref[key_list_ref[s], at : at + 16, :] for s in range(KEYS)], axis=0)
        for at in (0, 16)
    ]
    keys = jnp.concatenate(halves, axis=1)
    row = lax.broadcasted_iota(jnp.int32, (16, LANES), 0)
    col = lax.broadcasted_iota(jnp.int32, (16, LANES), 1)
    slot = jnp.where(col % 16 == row, col // 16, -1).astype(f32)
    for f in range(0, FRAMES, 8):
        picks = []
        for more in range(8):
            spare = slab_ref[f + more, 16:32, :].astype(f32)
            for which in range(2):
                wanted = spare[14 + which : 15 + which, :]
                picks.append(jnp.where(slot == wanted, 1.0, 0.0).astype(bf16))
        chosen = jnp.dot(jnp.concatenate(picks, axis=0), keys, preferred_element_type=f32)
        chosen = chosen.astype(bf16).reshape(8, 2, 16, 2 * LANES)
        out_ref[f : f + 8, :, 0:16, :] = chosen[..., :LANES]
        out_ref[f : f + 8, :, 16:32, :] = chosen[..., LANES:]


def choose(key_list, slab, after):
    return pl.pallas_call(
        choose_kernel,
        out_shape=pltpu.VMEM((FRAMES, 2, SLAB, LANES), bf16),
        in_specs=[SMALL, WHOLE, THERE],
        out_specs=WHOLE,
        compiler_params=params(VMEM),
        cost_estimate=cost(4 * FRAMES * SLAB * LANES * 256, 6 * FRAMES * SLAB * LANES),
        name="choose",
    )(key_list, in_vmem(slab), in_hbm(after))


LARGE = 1e30


def attend_kernel(
    slab_ref, q_hbm, mixed_hbm, stat_hbm, weight_hbm, wo_hbm, video_hbm,
    spatial_hbm, out_slab_ref,
    spatial_ref, rows_ref, heads_ref, most_ref, q_ref, mixed_ref, stat_ref,
    wkv_ref, wo_ref, video_ref, sems, last_sems, out_sems,
):
    def copies(group):
        pairs = (
            (weight_hbm.at[:, group_lanes(group, GROUP, WIDTH)], wkv_ref.at[:, :, pl.ds(0, GROUP)]),
            (weight_hbm.at[:, group_lanes(group, GROUP, 2 * WIDTH)], wkv_ref.at[:, :, pl.ds(GROUP, GROUP)]),
            (q_hbm.at[:, group_lanes(group, GROUP)], q_ref),
            (mixed_hbm.at[group], mixed_ref),
            (stat_hbm.at[group], stat_ref),
        )
        return [
            pltpu.make_async_copy(source, target.at[group], sems.at[i, group])
            for i, (source, target) in enumerate(pairs)
        ]

    last = (
        pltpu.make_async_copy(wo_hbm, wo_ref, last_sems.at[0]),
        pltpu.make_async_copy(video_hbm, video_ref, last_sems.at[1]),
    )
    for group in range(GROUPS):
        for copy in copies(group):
            copy.start()
    for copy in last:
        copy.start()

    swap = swap_matrix()
    for which in range(2):
        slab_to_rows(
            lambda block, half: slab_ref[
                16 * block : 16 * block + 16, which, 16 * half : 16 * half + 16, :
            ],
            rows_ref, swap, which * TOK,
        )
    most_ref[...] = jnp.zeros_like(most_ref)

    def project_group(group):
        rows = rows_ref[...]
        both = jnp.dot(rows, wkv_ref[group], preferred_element_type=f32).astype(bf16)
        return both[:, :GROUP], both[:, GROUP:].T

    def score_group(group, keys):
        scores = []
        for head in range(4):
            lanes = slice(head // 2 * LANES, (head // 2 + 1) * LANES)
            scores.append(flipped_scores(q_ref[group, :, lanes], keys[:, lanes], head % 2))
        return scores

    def mix_group(group, weights, values, less):
        made, totals = [], []
        for head in range(4):
            rows = slice(head * HEAD, (head + 1) * HEAD)
            out = jnp.dot(with_ones(values[rows]), weights[head], preferred_element_type=f32)
            mixed, total = mixed_ref[group, rows, :], stat_ref[group, 4 + head : 5 + head, :]
            if less is not None:
                mixed, total = mixed * less[head], total * less[head]
            mixed, total = mixed + out[:HEAD], total + out[HEAD : HEAD + 1]
            made.append((mixed / total).astype(bf16))
            totals.append(total)
        heads_ref[group] = jnp.concatenate(made, axis=0).T
        return totals

    @pl.loop(0, GROUPS)
    def _(group):
        arriving = copies(group)
        for copy in arriving[:2]:
            copy.wait()
        keys, values = project_group(group)
        for copy in arriving[2:]:
            copy.wait()
        scores = score_group(group, keys)
        weights = [
            jnp.exp2(scores[head] - stat_ref[group, head : head + 1, :]).astype(bf16)
            for head in range(4)
        ]
        for total in mix_group(group, weights, values, None):
            most_ref[...] = jnp.maximum(most_ref[...], total)

    @pl.when(jnp.logical_not(jnp.max(most_ref[...]) < LARGE))
    def _():
        @pl.loop(0, GROUPS)
        def _(group):
            keys, values = project_group(group)
            scores = score_group(group, keys)
            own = [stat_ref[group, head : head + 1, :] for head in range(4)]
            tops = [
                jnp.maximum(top, jnp.max(s, axis=0, keepdims=True)) for s, top in zip(scores, own)
            ]
            weights = [jnp.exp2(s - top).astype(bf16) for s, top in zip(scores, tops)]
            mix_group(group, weights, values, [jnp.exp2(o - top) for o, top in zip(own, tops)])

    given = []
    for copy in last:
        copy.wait()
    for k in range(PARTS):
        rows = pl.ds(k * FRAMES, FRAMES)
        heads = jnp.concatenate([heads_ref[g, rows, :] for g in range(GROUPS)], axis=1)
        added = jnp.dot(heads, wo_ref[...], preferred_element_type=f32)
        spatial_ref[rows, :] = (video_ref[rows, :].astype(f32) + added).astype(bf16)
        given.append(
            pltpu.make_async_copy(spatial_ref.at[rows], spatial_hbm.at[rows], out_sems.at[k])
        )
        given[-1].start()
    rows_to_slab(tiles_of(spatial_ref), out_slab_ref, swap)
    for copy in given:
        copy.wait()


def attend(slab, queries, mixed, stat, weight, out_weight, video):
    return pl.pallas_call(
        attend_kernel,
        out_shape=(
            jax.ShapeDtypeStruct((TOK, WIDTH), bf16),
            pltpu.VMEM((FRAMES, SLAB, LANES), bf16),
        ),
        in_specs=[WHOLE] + [THERE] * 6,
        out_specs=(THERE, WHOLE),
        scratch_shapes=[
            pltpu.VMEM((TOK, WIDTH), bf16),
            pltpu.VMEM((2 * TOK, WIDTH), bf16),
            pltpu.VMEM((GROUPS, TOK, GROUP), bf16),
            pltpu.VMEM((1, TOK), f32),
            pltpu.VMEM((GROUPS, TOK, GROUP), bf16),
            pltpu.VMEM((GROUPS, GROUP, TOK), f32),
            pltpu.VMEM((GROUPS, 8, TOK), f32),
            pltpu.VMEM((GROUPS, WIDTH, 2 * GROUP), bf16),
            pltpu.VMEM((WIDTH, WIDTH), bf16),
            pltpu.VMEM((TOK, WIDTH), bf16),
            pltpu.SemaphoreType.DMA((5, GROUPS)),
            pltpu.SemaphoreType.DMA((2,)),
            pltpu.SemaphoreType.DMA((PARTS,)),
        ],
        compiler_params=params(VMEM),
        cost_estimate=cost(
            8 * TOK * WIDTH * WIDTH + 16 * TOK * TOK * WIDTH,
            6 * WIDTH * WIDTH + 20 * TOK * WIDTH,
            2 * HEADS * TOK * TOK,
        ),
        name="attend",
    )(
        in_vmem(slab), in_hbm(queries), in_hbm(mixed), in_hbm(stat),
        in_hbm(weight), in_hbm(out_weight), in_hbm(video),
    )


def time_kernel(
    slab_ref, gain_ref, weight_hbm, out_slab_ref, rows_ref, heads_ref, weight_ref, sems
):
    for group in range(GROUPS):
        for copy in group_copies(weight_hbm, weight_ref, sems, group):
            copy.start()
    swap = swap_matrix()
    slab_to_rows(
        lambda block, half: slab_ref[16 * block : 16 * block + 16, 16 * half : 16 * half + 16, :],
        rows_ref, swap,
    )
    for k in range(PARTS):
        rows = pl.ds(k * FRAMES, FRAMES)
        rows_ref[rows, :] = norm_rows(rows_ref[rows, :].astype(f32), gain_ref[...].reshape(1, WIDTH))

    @pl.loop(0, GROUPS)
    def _(group):
        for copy in group_copies(weight_hbm, weight_ref, sems, group):
            copy.wait()
        rows = rows_ref[...]
        made = jnp.dot(rows, weight_ref[group], preferred_element_type=f32)
        made = [made[:, w * GROUP : (w + 1) * GROUP] for w in range(3)]
        queries, keys, values = (made[0] * SCALE).astype(bf16), made[1].astype(bf16), made[2]
        units, places = [], []
        for pair in range(2):
            lanes = slice(pair * LANES, (pair + 1) * LANES)
            for k in range(PARTS):
                at = slice(k * FRAMES, (k + 1) * FRAMES)
                units.append((queries[at, lanes], keys[at, lanes], values[at, lanes], None))
                places.append((pair, at))
        for (pair, at), (mixed, total, _) in zip(places, attend_pairs(units)):
            heads_ref[2 * group + pair, at, :] = (mixed / total).astype(bf16)

    rows_to_slab(lambda at, g: heads_ref[g, at : at + 16, :], out_slab_ref, swap)


def time_attend(slab, gain, weight):
    return pl.pallas_call(
        time_kernel,
        out_shape=pltpu.VMEM((FRAMES, SLAB, LANES), bf16),
        in_specs=[WHOLE, WHOLE, THERE],
        out_specs=WHOLE,
        scratch_shapes=[
            pltpu.VMEM((TOK, WIDTH), bf16),
            pltpu.VMEM((COLS, TOK, LANES), bf16),
            pltpu.VMEM((GROUPS, WIDTH, 3 * GROUP), bf16),
            pltpu.SemaphoreType.DMA((3, GROUPS)),
        ],
        compiler_params=params(VMEM),
        cost_estimate=cost(
            6 * TOK * WIDTH * WIDTH + 8 * TOK * FRAMES * WIDTH,
            6 * WIDTH * WIDTH + 4 * TOK * WIDTH,
            HEADS * TOK * FRAMES,
        ),
        name="time_attend",
    )(in_vmem(slab), in_hbm(gain), in_hbm(weight))


def unpack_kernel(slab_ref, out_hbm, out_ref, sems):
    swap = swap_matrix()
    copies = []
    for part in range(4):
        slab_to_rows(
            lambda block, half: slab_ref[
                16 * block : 16 * block + 16, 16 * half : 16 * half + 16, :
            ],
            out_ref, swap, blocks=(2 * part, 2 * part + 1),
        )
        for k in range(PARTS):
            some = pl.ds(k * FRAMES + 32 * part, 32)
            copies.append(
                pltpu.make_async_copy(out_ref.at[some], out_hbm.at[some], sems.at[len(copies)])
            )
            copies[-1].start()
    for copy in copies:
        copy.wait()


def unpack(slab):
    return pl.pallas_call(
        unpack_kernel,
        out_shape=jax.ShapeDtypeStruct((TOK, WIDTH), bf16),
        in_specs=[WHOLE],
        out_specs=THERE,
        scratch_shapes=[pltpu.VMEM((TOK, WIDTH), bf16), pltpu.SemaphoreType.DMA((4 * PARTS,))],
        compiler_params=params(VMEM),
        cost_estimate=cost(2 * TOK * WIDTH * 256, 4 * TOK * WIDTH),
        name="unpack",
    )(in_vmem(slab))


def exchange(slab):
    return lax.all_to_all(slab, "frame", split_axis=0, concat_axis=0, tiled=True)


def body(video, key_list, pairs, norm_gain, qkv_weight, out_weight, time_gain, time_weight):
    spread = exchange(prep(pairs, video, norm_gain))
    queries, mixed, stat = own_attend(video, norm_gain, qkv_weight)
    wanted = exchange(choose(key_list, spread, queries))
    spatial, slab = attend(wanted, queries, mixed, stat, qkv_weight, out_weight, video)
    slab = time_attend(exchange(slab), time_gain, time_weight)
    return spatial, unpack(exchange(slab))


def solution(mesh):
    return jax.shard_map(
        body,
        mesh=mesh,
        in_specs=(P("frame", None), P(), P("frame", None), P(), P(), P(), P(), P()),
        out_specs=(P("frame", None), P("frame", None)),
        check_vma=False,
    )
```

```python
import jax
import jax.numpy as jnp
from jax import lax
from jax.experimental import pallas as pl
from jax.experimental.pallas import tpu as pltpu
from jax.sharding import PartitionSpec as P

WIDTH = 1280
HEADS = 20
HEAD = 64
TOK = 384
FRAMES = 128
KEYS = 8
PARTS = TOK // FRAMES
LANES = 128
COLS = WIDTH // LANES
SLAB = 32
GROUP = 256
GROUPS = WIDTH // GROUP
VMEM = 52
SCALE = 0.125 * 1.4426950408889634

bf16 = jnp.bfloat16
f32 = jnp.float32


def params(mib, **more):
    return pltpu.CompilerParams(vmem_limit_bytes=mib << 20, **more)


def cost(flops, moved, exps=0):
    return pl.CostEstimate(flops=int(flops), bytes_accessed=int(moved), transcendentals=int(exps))


def in_vmem(x):
    return pltpu.with_memory_space_constraint(x, pltpu.VMEM)


def in_hbm(x):
    return pltpu.with_memory_space_constraint(x, pltpu.HBM)


WHOLE = pl.BlockSpec(memory_space=pltpu.VMEM)
THERE = pl.BlockSpec(memory_space=pl.ANY)
SMALL = pl.BlockSpec(memory_space=pltpu.SMEM)


def norm_rows(values, gain):
    centred = values - jnp.mean(values, axis=-1, keepdims=True)
    spread = jnp.mean(centred * centred, axis=-1, keepdims=True)
    return (centred * lax.rsqrt(spread + 1e-05) * gain).astype(bf16)


def swap_matrix():
    row = lax.broadcasted_iota(jnp.int32, (256, 256), 0)
    col = lax.broadcasted_iota(jnp.int32, (256, 256), 1)
    return jnp.where(col == (row % 16) * 16 + row // 16, 1.0, 0.0).astype(bf16)


def rows_to_slab(tile, slab_ref, swap, spare=None, halves=(0, 1)):
    for half in halves:
        for pair in range(4):
            sides = []
            for block in (2 * pair, 2 * pair + 1):
                tiles = []
                for unit in range(16 * half, 16 * half + 16):
                    k, g = divmod(unit, COLS)
                    if k < PARTS:
                        tiles.append(tile(k * FRAMES + 16 * block, g))
                    elif spare is None:
                        tiles.append(jnp.zeros((16, LANES), bf16))
                    else:
                        tiles.append(spare[unit - PARTS * COLS])
                sides.append(jnp.concatenate(tiles, axis=0))
            both = jnp.concatenate(sides, axis=1)
            moved = jnp.dot(swap, both, preferred_element_type=f32).astype(bf16)
            for side in range(2):
                block = 2 * pair + side
                slab_ref[16 * block : 16 * block + 16, 16 * half : 16 * half + 16, :] = moved[
                    :, side * LANES : (side + 1) * LANES
                ].reshape(16, 16, LANES)


def tiles_of(rows_ref):
    return lambda at, g: rows_ref[at : at + 16, g * LANES : (g + 1) * LANES]


def slab_to_rows(load, rows_ref, swap, first=0, blocks=range(8)):
    for block in blocks:
        both = jnp.concatenate(
            [load(block, half).reshape(256, LANES) for half in range(2)], axis=1
        )
        moved = jnp.dot(swap, both, preferred_element_type=f32).astype(bf16)
        for unit in range(PARTS * COLS):
            half, row = divmod(unit, 16)
            k, g = divmod(unit, COLS)
            at = first + k * FRAMES + 16 * block
            rows_ref[at : at + 16, g * LANES : (g + 1) * LANES] = moved[
                16 * row : 16 * row + 16, half * LANES : (half + 1) * LANES
            ]


def prep_kernel(pairs_ref, video_ref, gain_ref, slab_hbm, normed_ref, slab_ref, sems):
    swap = swap_matrix()
    gain = gain_ref[...].reshape(1, WIDTH)
    spare = [
        jnp.full((16, LANES), pairs_ref[0, which], jnp.int32).astype(f32).astype(bf16)
        for which in range(2)
    ]
    leaving = []

    def give(half):
        rows_to_slab(tiles_of(normed_ref), slab_ref, swap, spare, halves=(half,))
        some = pl.ds(16 * half, 16)
        leaving.append(
            pltpu.make_async_copy(slab_ref.at[:, some], slab_hbm.at[:, some], sems.at[half])
        )
        leaving[-1].start()

    for k in range(PARTS):
        rows = pl.ds(k * FRAMES, FRAMES)
        normed_ref[rows, :] = norm_rows(video_ref[rows, :].astype(f32), gain)
        if k == 1:
            give(0)
    give(1)
    for copy in leaving:
        copy.wait()


def prep(pairs, video, gain):
    return pl.pallas_call(
        prep_kernel,
        out_shape=pltpu.HBM((FRAMES, SLAB, LANES), bf16),
        in_specs=[SMALL, WHOLE, WHOLE],
        out_specs=THERE,
        scratch_shapes=[
            pltpu.VMEM((TOK, WIDTH), bf16),
            pltpu.VMEM((FRAMES, SLAB, LANES), bf16),
            pltpu.SemaphoreType.DMA((2,)),
        ],
        compiler_params=params(VMEM),
        cost_estimate=cost(6 * TOK * WIDTH, 4 * TOK * WIDTH),
        name="prep",
    )(in_hbm(pairs), in_hbm(video), in_hbm(gain))


def low_lanes(rows):
    return lax.broadcasted_iota(jnp.int32, (rows, LANES), 1) < HEAD


def attend_pairs(units):
    scores, padded = [], []
    for queries, keys, values, _ in units:
        low_q, low_v = low_lanes(queries.shape[0]), low_lanes(values.shape[0])
        wide = queries.astype(f32)
        for head in range(2):
            mine = jnp.where(low_q, wide, 0.0) if head == 0 else jnp.where(low_q, 0.0, wide)
            rest = jnp.where(low_v, values, 1.0) if head == 0 else jnp.where(low_v, 1.0, values)
            padded.append(rest.astype(bf16))
            scores.append(
                lax.dot_general(
                    mine.astype(bf16), keys, (((1,), (1,)), ((), ())), preferred_element_type=f32
                )
            )
    tops = [jnp.max(s, axis=-1, keepdims=True) for s in scores]
    for i, (_, _, _, top) in enumerate(units):
        if top is not None:
            for head in range(2):
                other = top[:, head * HEAD : head * HEAD + 1]
                tops[2 * i + head] = jnp.maximum(tops[2 * i + head], other)
    weights = [jnp.exp2(s - top).astype(bf16) for s, top in zip(scores, tops)]
    outs = [jnp.dot(w, v, preferred_element_type=f32) for w, v in zip(weights, padded)]
    given = []
    for i, (queries, _, _, _) in enumerate(units):
        low = low_lanes(queries.shape[0])
        one, two = outs[2 * i], outs[2 * i + 1]
        total = pltpu.roll(jnp.where(low, two, one), HEAD, 1)
        given.append((jnp.where(low, one, two), total, tops[2 * i : 2 * i + 2]))
    return given


def group_lanes(group, size, offset=0):
    return pl.ds(pl.multiple_of(offset + group * GROUP, LANES), size)


def flipped_scores(queries, keys, head):
    low = low_lanes(queries.shape[0])
    wide = queries.astype(f32)
    mine = jnp.where(low, wide, 0.0) if head == 0 else jnp.where(low, 0.0, wide)
    return lax.dot_general(
        keys, mine.astype(bf16), (((1,), (1,)), ((), ())), preferred_element_type=f32
    )


def with_ones(values):
    return jnp.concatenate([values, jnp.ones((16, values.shape[1]), bf16)], axis=0)


def group_copies(weight_hbm, weight_ref, sems, group):
    return [
        pltpu.make_async_copy(
            weight_hbm.at[:, group_lanes(group, GROUP, which * WIDTH)],
            weight_ref.at[which, group],
            sems.at[which, group],
        )
        for which in range(3)
    ]


def own_kernel(
    video_ref, gain_ref, weight_hbm, q_ref, mixed_ref, stat_ref, rows_ref, weight_ref, sems
):
    for group in range(GROUPS):
        for copy in group_copies(weight_hbm, weight_ref, sems, group):
            copy.start(priority=0 if group == 0 else 1)
    gain = gain_ref[...].reshape(1, WIDTH)
    for k in range(PARTS):
        rows = pl.ds(k * FRAMES, FRAMES)
        rows_ref[rows, :] = norm_rows(video_ref[rows, :].astype(f32), gain)

    @pl.loop(0, GROUPS)
    def _(group):
        for copy in group_copies(weight_hbm, weight_ref, sems, group):
            copy.wait()
        rows = rows_ref[...]
        queries, keys, values = [
            jnp.dot(rows, weight_ref[which, group], preferred_element_type=f32)
            for which in range(3)
        ]
        queries, keys, values = (queries * SCALE).astype(bf16), keys.astype(bf16), values.astype(bf16).T
        q_ref[:, group_lanes(group, GROUP)] = queries
        scores = []
        for head in range(4):
            lanes = slice(head // 2 * LANES, (head // 2 + 1) * LANES)
            scores.append(flipped_scores(queries[:, lanes], keys[:, lanes], head % 2))
        tops = [jnp.max(s, axis=0, keepdims=True) for s in scores]
        weights = [jnp.exp2(s - top).astype(bf16) for s, top in zip(scores, tops)]
        for head in range(4):
            rows = slice(head * HEAD, (head + 1) * HEAD)
            out = jnp.dot(with_ones(values[rows]), weights[head], preferred_element_type=f32)
            mixed_ref[group, rows, :] = out[:HEAD]
            stat_ref[group, head : head + 1, :] = tops[head]
            stat_ref[group, 4 + head : 5 + head, :] = out[HEAD : HEAD + 1]


def own_attend(video, gain, weight):
    return pl.pallas_call(
        own_kernel,
        out_shape=(
            pltpu.HBM((TOK, WIDTH), bf16),
            pltpu.HBM((GROUPS, GROUP, TOK), f32),
            pltpu.HBM((GROUPS, 8, TOK), f32),
        ),
        in_specs=[WHOLE, WHOLE, THERE],
        out_specs=(WHOLE, WHOLE, WHOLE),
        scratch_shapes=[
            pltpu.VMEM((TOK, WIDTH), bf16),
            pltpu.VMEM((3, GROUPS, WIDTH, GROUP), bf16),
            pltpu.SemaphoreType.DMA((3, GROUPS)),
        ],
        compiler_params=params(VMEM),
        cost_estimate=cost(
            6 * TOK * WIDTH * WIDTH + 8 * TOK * TOK * WIDTH,
            6 * WIDTH * WIDTH + 10 * TOK * WIDTH,
            HEADS * TOK * TOK,
        ),
        name="own_attend",
    )(in_hbm(video), in_hbm(gain), in_hbm(weight))


def choose_kernel(key_list_ref, slab_ref, after_ref, out_ref):
    del after_ref
    halves = [
        jnp.concatenate([slab_ref[key_list_ref[s], at : at + 16, :] for s in range(KEYS)], axis=0)
        for at in (0, 16)
    ]
    keys = jnp.concatenate(halves, axis=1)
    row = lax.broadcasted_iota(jnp.int32, (16, LANES), 0)
    col = lax.broadcasted_iota(jnp.int32, (16, LANES), 1)
    slot = jnp.where(col % 16 == row, col // 16, -1).astype(f32)
    for f in range(0, FRAMES, 8):
        picks = []
        for more in range(8):
            spare = slab_ref[f + more, 16:32, :].astype(f32)
            for which in range(2):
                wanted = spare[14 + which : 15 + which, :]
                picks.append(jnp.where(slot == wanted, 1.0, 0.0).astype(bf16))
        chosen = jnp.dot(jnp.concatenate(picks, axis=0), keys, preferred_element_type=f32)
        chosen = chosen.astype(bf16).reshape(8, 2, 16, 2 * LANES)
        out_ref[f : f + 8, :, 0:16, :] = chosen[..., :LANES]
        out_ref[f : f + 8, :, 16:32, :] = chosen[..., LANES:]


def choose(key_list, slab, after):
    return pl.pallas_call(
        choose_kernel,
        out_shape=pltpu.VMEM((FRAMES, 2, SLAB, LANES), bf16),
        in_specs=[SMALL, WHOLE, THERE],
        out_specs=WHOLE,
        compiler_params=params(VMEM),
        cost_estimate=cost(4 * FRAMES * SLAB * LANES * 256, 6 * FRAMES * SLAB * LANES),
        name="choose",
    )(key_list, in_vmem(slab), in_hbm(after))


LARGE = 1e30


def attend_kernel(
    slab_ref, q_hbm, mixed_hbm, stat_hbm, weight_hbm, wo_hbm, video_hbm,
    spatial_hbm, out_slab_ref,
    spatial_ref, rows_ref, heads_ref, most_ref, q_ref, mixed_ref, stat_ref,
    wk_ref, wv_ref, wo_ref, video_ref, sems, last_sems, out_sems,
):
    def copies(group):
        pairs = (
            (weight_hbm.at[:, group_lanes(group, GROUP, WIDTH)], wk_ref),
            (weight_hbm.at[:, group_lanes(group, GROUP, 2 * WIDTH)], wv_ref),
            (q_hbm.at[:, group_lanes(group, GROUP)], q_ref),
            (mixed_hbm.at[group], mixed_ref),
            (stat_hbm.at[group], stat_ref),
        )
        return [
            pltpu.make_async_copy(source, target.at[group], sems.at[i, group])
            for i, (source, target) in enumerate(pairs)
        ]

    last = (
        pltpu.make_async_copy(wo_hbm, wo_ref, last_sems.at[0]),
        pltpu.make_async_copy(video_hbm, video_ref, last_sems.at[1]),
    )
    for group in range(GROUPS):
        for copy in copies(group):
            copy.start(priority=0 if group == 0 else 1)
    for copy in last:
        copy.start(priority=1)

    swap = swap_matrix()
    for which in range(2):
        slab_to_rows(
            lambda block, half: slab_ref[
                16 * block : 16 * block + 16, which, 16 * half : 16 * half + 16, :
            ],
            rows_ref, swap, which * TOK,
        )
    most_ref[...] = jnp.zeros_like(most_ref)

    def project_group(group):
        rows = rows_ref[...]
        keys = jnp.dot(rows, wk_ref[group], preferred_element_type=f32).astype(bf16)
        values = jnp.dot(rows, wv_ref[group], preferred_element_type=f32).astype(bf16)
        return keys, values.T

    def score_group(group, keys):
        scores = []
        for head in range(4):
            lanes = slice(head // 2 * LANES, (head // 2 + 1) * LANES)
            scores.append(flipped_scores(q_ref[group, :, lanes], keys[:, lanes], head % 2))
        return scores

    def mix_group(group, weights, values, less):
        made, totals = [], []
        for head in range(4):
            rows = slice(head * HEAD, (head + 1) * HEAD)
            out = jnp.dot(with_ones(values[rows]), weights[head], preferred_element_type=f32)
            mixed, total = mixed_ref[group, rows, :], stat_ref[group, 4 + head : 5 + head, :]
            if less is not None:
                mixed, total = mixed * less[head], total * less[head]
            mixed, total = mixed + out[:HEAD], total + out[HEAD : HEAD + 1]
            made.append((mixed / total).astype(bf16))
            totals.append(total)
        heads_ref[group] = jnp.concatenate(made, axis=0).T
        return totals

    @pl.loop(0, GROUPS)
    def _(group):
        arriving = copies(group)
        for copy in arriving[:2]:
            copy.wait()
        keys, values = project_group(group)
        for copy in arriving[2:]:
            copy.wait()
        scores = score_group(group, keys)
        weights = [
            jnp.exp2(scores[head] - stat_ref[group, head : head + 1, :]).astype(bf16)
            for head in range(4)
        ]
        for total in mix_group(group, weights, values, None):
            most_ref[...] = jnp.maximum(most_ref[...], total)

    @pl.when(jnp.logical_not(jnp.max(most_ref[...]) < LARGE))
    def _():
        @pl.loop(0, GROUPS)
        def _(group):
            keys, values = project_group(group)
            scores = score_group(group, keys)
            own = [stat_ref[group, head : head + 1, :] for head in range(4)]
            tops = [
                jnp.maximum(top, jnp.max(s, axis=0, keepdims=True)) for s, top in zip(scores, own)
            ]
            weights = [jnp.exp2(s - top).astype(bf16) for s, top in zip(scores, tops)]
            mix_group(group, weights, values, [jnp.exp2(o - top) for o, top in zip(own, tops)])

    given = []
    for copy in last:
        copy.wait()
    for k in range(PARTS):
        rows = pl.ds(k * FRAMES, FRAMES)
        heads = jnp.concatenate([heads_ref[g, rows, :] for g in range(GROUPS)], axis=1)
        added = jnp.dot(heads, wo_ref[...], preferred_element_type=f32)
        spatial_ref[rows, :] = (video_ref[rows, :].astype(f32) + added).astype(bf16)
        given.append(
            pltpu.make_async_copy(spatial_ref.at[rows], spatial_hbm.at[rows], out_sems.at[k])
        )
        given[-1].start()
    rows_to_slab(tiles_of(spatial_ref), out_slab_ref, swap)
    for copy in given:
        copy.wait()


def attend(slab, queries, mixed, stat, weight, out_weight, video):
    return pl.pallas_call(
        attend_kernel,
        out_shape=(
            jax.ShapeDtypeStruct((TOK, WIDTH), bf16),
            pltpu.VMEM((FRAMES, SLAB, LANES), bf16),
        ),
        in_specs=[WHOLE] + [THERE] * 6,
        out_specs=(THERE, WHOLE),
        scratch_shapes=[
            pltpu.VMEM((TOK, WIDTH), bf16),
            pltpu.VMEM((2 * TOK, WIDTH), bf16),
            pltpu.VMEM((GROUPS, TOK, GROUP), bf16),
            pltpu.VMEM((1, TOK), f32),
            pltpu.VMEM((GROUPS, TOK, GROUP), bf16),
            pltpu.VMEM((GROUPS, GROUP, TOK), f32),
            pltpu.VMEM((GROUPS, 8, TOK), f32),
            pltpu.VMEM((GROUPS, WIDTH, GROUP), bf16),
            pltpu.VMEM((GROUPS, WIDTH, GROUP), bf16),
            pltpu.VMEM((WIDTH, WIDTH), bf16),
            pltpu.VMEM((TOK, WIDTH), bf16),
            pltpu.SemaphoreType.DMA((5, GROUPS)),
            pltpu.SemaphoreType.DMA((2,)),
            pltpu.SemaphoreType.DMA((PARTS,)),
        ],
        compiler_params=params(VMEM),
        cost_estimate=cost(
            8 * TOK * WIDTH * WIDTH + 16 * TOK * TOK * WIDTH,
            6 * WIDTH * WIDTH + 20 * TOK * WIDTH,
            2 * HEADS * TOK * TOK,
        ),
        name="attend",
    )(
        in_vmem(slab), in_hbm(queries), in_hbm(mixed), in_hbm(stat),
        in_hbm(weight), in_hbm(out_weight), in_hbm(video),
    )


def time_kernel(
    slab_ref, gain_ref, weight_hbm, out_slab_ref, rows_ref, heads_ref, weight_ref, sems
):
    for group in range(GROUPS):
        for copy in group_copies(weight_hbm, weight_ref, sems, group):
            copy.start(priority=0 if group == 0 else 1)
    swap = swap_matrix()
    slab_to_rows(
        lambda block, half: slab_ref[16 * block : 16 * block + 16, 16 * half : 16 * half + 16, :],
        rows_ref, swap,
    )
    for k in range(PARTS):
        rows = pl.ds(k * FRAMES, FRAMES)
        rows_ref[rows, :] = norm_rows(rows_ref[rows, :].astype(f32), gain_ref[...].reshape(1, WIDTH))

    @pl.loop(0, GROUPS)
    def _(group):
        for copy in group_copies(weight_hbm, weight_ref, sems, group):
            copy.wait()
        rows = rows_ref[...]
        made = [
            jnp.dot(rows, weight_ref[which, group], preferred_element_type=f32)
            for which in range(3)
        ]
        queries, keys, values = (made[0] * SCALE).astype(bf16), made[1].astype(bf16), made[2]
        units, places = [], []
        for pair in range(2):
            lanes = slice(pair * LANES, (pair + 1) * LANES)
            for k in range(PARTS):
                at = slice(k * FRAMES, (k + 1) * FRAMES)
                units.append((queries[at, lanes], keys[at, lanes], values[at, lanes], None))
                places.append((pair, at))
        for (pair, at), (mixed, total, _) in zip(places, attend_pairs(units)):
            heads_ref[2 * group + pair, at, :] = (mixed / total).astype(bf16)

    rows_to_slab(lambda at, g: heads_ref[g, at : at + 16, :], out_slab_ref, swap)


def time_attend(slab, gain, weight):
    return pl.pallas_call(
        time_kernel,
        out_shape=pltpu.VMEM((FRAMES, SLAB, LANES), bf16),
        in_specs=[WHOLE, WHOLE, THERE],
        out_specs=WHOLE,
        scratch_shapes=[
            pltpu.VMEM((TOK, WIDTH), bf16),
            pltpu.VMEM((COLS, TOK, LANES), bf16),
            pltpu.VMEM((3, GROUPS, WIDTH, GROUP), bf16),
            pltpu.SemaphoreType.DMA((3, GROUPS)),
        ],
        compiler_params=params(VMEM),
        cost_estimate=cost(
            6 * TOK * WIDTH * WIDTH + 8 * TOK * FRAMES * WIDTH,
            6 * WIDTH * WIDTH + 4 * TOK * WIDTH,
            HEADS * TOK * FRAMES,
        ),
        name="time_attend",
    )(in_vmem(slab), in_hbm(gain), in_hbm(weight))


def unpack_kernel(slab_ref, out_hbm, out_ref, sems):
    swap = swap_matrix()
    copies = []
    for part in range(4):
        slab_to_rows(
            lambda block, half: slab_ref[
                16 * block : 16 * block + 16, 16 * half : 16 * half + 16, :
            ],
            out_ref, swap, blocks=(2 * part, 2 * part + 1),
        )
        for k in range(PARTS):
            some = pl.ds(k * FRAMES + 32 * part, 32)
            copies.append(
                pltpu.make_async_copy(out_ref.at[some], out_hbm.at[some], sems.at[len(copies)])
            )
            copies[-1].start()
    for copy in copies:
        copy.wait()


def unpack(slab):
    return pl.pallas_call(
        unpack_kernel,
        out_shape=jax.ShapeDtypeStruct((TOK, WIDTH), bf16),
        in_specs=[WHOLE],
        out_specs=THERE,
        scratch_shapes=[pltpu.VMEM((TOK, WIDTH), bf16), pltpu.SemaphoreType.DMA((4 * PARTS,))],
        compiler_params=params(VMEM),
        cost_estimate=cost(2 * TOK * WIDTH * 256, 4 * TOK * WIDTH),
        name="unpack",
    )(in_vmem(slab))


def exchange(slab):
    return lax.all_to_all(slab, "frame", split_axis=0, concat_axis=0, tiled=True)


def body(video, key_list, pairs, norm_gain, qkv_weight, out_weight, time_gain, time_weight):
    spread = exchange(prep(pairs, video, norm_gain))
    queries, mixed, stat = own_attend(video, norm_gain, qkv_weight)
    wanted = exchange(choose(key_list, spread, queries))
    spatial, slab = attend(wanted, queries, mixed, stat, qkv_weight, out_weight, video)
    slab = time_attend(exchange(slab), time_gain, time_weight)
    return spatial, unpack(exchange(slab))


def solution(mesh):
    return jax.shard_map(
        body,
        mesh=mesh,
        in_specs=(P("frame", None), P(), P("frame", None), P(), P(), P(), P(), P()),
        out_specs=(P("frame", None), P("frame", None)),
        check_vma=False,
    )
```
